256 devices in a mesh: pipe: 2 (over x_hi), seg: 32 (over x_lo, z, core), dp: 4 (over y).
Axes of the slice: x: 4 (x_hi: 2, x_lo: 2; x = x_hi * 2 + x_lo), y: 4, z: 8, core: 2. Of those that a mesh axis runs over, the one named last changes fastest.
Arguments:
- inputs: bfloat16 [2, 4, 4096, 4096], P('pipe', 'dp', 'seg'), may hold values from -8 to 8
- mixed: bfloat16 [2, 4, 4096, 4096], P('pipe', 'dp', 'seg'), may hold values from -6 to 6
- gate_in: bfloat16 [2, 4, 4096, 4096], P('pipe', 'dp', 'seg'), may hold values from -6 to 6
- entry_states: float32 [2, 4, 32, 64, 64, 128], P('pipe', 'dp', 'seg'), may hold values from -6 to 6
- out_grad: bfloat16 [4, 4096, 4096], P('dp', 'seg'), may hold values from -6 to 6
- doc_lengths: int32 [4, 6], P('dp'), may hold values from 1 to 2048, 4096 in all within a row
- proj_weight: bfloat16 [2, 4096, 320], P('pipe', ('seg', 'dp')), may hold values from -0.05078125 to 0.05078125
- decay_rate: float32 [2, 64], P('pipe'), may hold values from 7.324219e-05 to 0.1
- dt_bias: float32 [2, 64], P('pipe'), may hold values from -1 to 1
- skip_gain: float32 [2, 64], P('pipe'), may hold values from 0.5 to 1.5
Outputs:
- input_grad: bfloat16 [2, 4, 4096, 4096], P('pipe', 'dp', 'seg')
- mixed_grad: bfloat16 [2, 4, 4096, 4096], P('pipe', 'dp', 'seg')
- gate_grad: bfloat16 [2, 4, 4096, 4096], P('pipe', 'dp', 'seg')
- weight_grad: float32 [2, 4096, 320], P('pipe', ('seg', 'dp'))
The draws below stay inside these ranges and needn't reach their ends.
All inputs are finite; a program needn't handle non-finite values.
Results may differ from the reference program's by a relative error of at most 0.009.
Values may be sent and summed in bfloat16 or wider, within the bound.
A program may use at most 320 MiB of HBM per device.

```python
import math
import jax
import jax.numpy as jnp
import numpy as np
from jax import lax

D = 4096
HEADS = 64
HEAD_DIM = 64
STATE = 128
SEG = 128
MB = 1
DOCS = 6
L = 4096
SEGMENTS = 32
BATCH = 4
PROJ = 320
N_SEG = 32


def draw_inputs(key, part):
    key = jax.random.fold_in(key, 11)
    groups = BATCH // MB
    blocks = SEGMENTS * groups
    block_width = D // blocks
    noise_key, level_key, order_key = jax.random.split(key, 3)
    shape = (2, BATCH, SEGMENTS, SEG, blocks, block_width)
    noise = jax.random.normal(noise_key, shape, jnp.float32)
    levels = jnp.exp(jax.random.uniform(level_key, (2, BATCH, SEGMENTS), jnp.float32, -1.2, 0.7))
    orders = jnp.stack([jax.random.permutation(jax.random.fold_in(order_key, 0), blocks), jax.random.permutation(jax.random.fold_in(order_key, 1), blocks)]).astype(jnp.int32)
    owner_index = (jnp.arange(BATCH, dtype=jnp.int32) // MB)[:, None] * SEGMENTS + jnp.arange(SEGMENTS, dtype=jnp.int32)[None, :]
    owners = orders[:, owner_index]
    marked = (owners[..., None] == jnp.arange(blocks, dtype=jnp.int32)).astype(jnp.float32)
    factor = 1.0 + 1.5 * marked
    values = noise * levels[:, :, :, None, None, None] * factor[:, :, :, None, :, None]
    return jnp.clip(values, -8.0, 8.0).reshape(2, BATCH, SEGMENTS * SEG, D).astype(jnp.bfloat16)


def draw_proj_weight(key, part):
    key = jax.random.fold_in(key, 12)
    raw = jnp.clip(jax.random.normal(key, (2, D, PROJ), jnp.float32), -2.5, 2.5)
    column = jnp.arange(PROJ, dtype=jnp.int32)
    scale = jnp.where(column < 2 * STATE, (D * STATE / 2.0) ** (-0.5), 1.3 * D ** (-0.5))
    return (raw * scale[None, None, :]).astype(jnp.bfloat16)


def steps_of(key, dims, cuts, least, high):
    def one(axis_at, parts):
        draws = jax.random.uniform(jax.random.fold_in(jax.random.fold_in(key, 6), axis_at), (parts,), jnp.float32, least / len(cuts), high / len(cuts))
        return jnp.repeat(jnp.exp(draws), dims[axis_at] // parts).reshape((-1,) + (1,) * (len(dims) - axis_at - 1))

    level = one(*cuts[0])
    for cut in cuts[1:]:
        level = level * one(*cut)
    return level


def length_profile(number_of, total, reach, slope):
    loads = [(1 << 20) // math.isqrt(grade ** slope) + 1 for grade in range(2, number_of + 1)]
    rest, holding = total - reach - (number_of - 1), [1] * (number_of - 1)
    while rest > 0:
        candidates = [i for i in range(number_of - 1) if holding[i] < reach]
        pool, left = sum([loads[i] for i in candidates]), rest
        for i in candidates:
            addition = min(reach - holding[i], max(1, left * loads[i] // pool), rest)
            holding[i] = holding[i] + addition
            rest = rest - addition
    return np.array([reach] + holding)


def uneven(rng, number_of, total, limit, slope):
    if number_of == 2:
        one = jax.random.randint(rng, (), max(1, total - limit), min(limit, total - 1) + 1)
        return jnp.stack([one, total - one])
    tallies = jnp.asarray(length_profile(number_of, total, limit, slope), jnp.int32)
    pairs = (number_of - 1) // 2
    giver, sink = tallies[1:1 + 2 * pairs:2], tallies[2:2 + 2 * pairs:2]
    margin = jnp.minimum(giver - 1, limit - sink)
    shifted = jax.random.randint(jax.random.fold_in(rng, 1), (pairs,), 0, 1 << 20) % (margin + 1)
    tallies = tallies.at[1:1 + 2 * pairs:2].set(giver - shifted).at[2:2 + 2 * pairs:2].set(sink + shifted)
    return tallies[jax.random.permutation(jax.random.fold_in(rng, 2), number_of)]


def scatter_about(rng, shape, deviation, limit, pieces=(), kind=jnp.bfloat16):
    factor_of = steps_of(rng, shape, pieces, -0.22, 0.18) if pieces else 1.0
    result = jax.random.normal(rng, shape, jnp.float32) * deviation * factor_of
    return jnp.minimum(jnp.maximum(result, -limit), limit).astype(kind)


def setup_inputs(seed: int = 0) -> dict:
    arg_keys = jax.random.split(jax.random.key(seed), 11)
    inputs = draw_inputs(jax.random.fold_in(arg_keys[10], 71), 0)
    mixed = scatter_about(arg_keys[1], (2, BATCH, L, D), 1.0, 6.0, ((0, 2), (1, 4), (2, 32)))
    gate_in = scatter_about(arg_keys[2], (2, BATCH, L, D), 1.0, 6.0, ((0, 2), (1, 4), (2, 32)))
    entry_states = scatter_about(arg_keys[3], (2, BATCH, SEGMENTS, HEADS, HEAD_DIM, STATE), 1.0, 6.0, ((0, 2), (1, 4), (2, 32)), jnp.float32)
    out_grad = scatter_about(arg_keys[4], (BATCH, L, D), 1.0, 6.0, ((0, 4), (1, 32)))
    doc_lengths = jax.vmap(lambda own: uneven(own, DOCS, SEG * N_SEG, SEG * N_SEG // 2, 2))(jax.random.split(arg_keys[5], BATCH)).reshape((BATCH, DOCS)).astype(jnp.int32)
    proj_weight = draw_proj_weight(jax.random.fold_in(arg_keys[10], 71), 0)
    decay_rate = jnp.clip(jnp.exp(math.log(0.1) - 7.219154 * jax.random.uniform(arg_keys[7], (2, HEADS), jnp.float32) ** steps_of(arg_keys[7], (2, HEADS), ((0, 2),), -0.2, 0.2)), 7.324219041038305e-05, 0.1)
    dt_bias = jnp.clip(jax.random.uniform(arg_keys[8], (2, HEADS), jnp.float32, -1.0, 1.0) * steps_of(arg_keys[8], (2, HEADS), ((0, 2),), -0.4, 0.0), -1.0, 1.0)
    skip_gain = jnp.clip(0.5 + 1.0 * jax.random.uniform(arg_keys[9], (2, HEADS), jnp.float32) ** steps_of(arg_keys[9], (2, HEADS), ((0, 2),), -0.2, 0.2), 0.5, 1.5)
    return {"inputs": inputs, "mixed": mixed, "gate_in": gate_in, "entry_states": entry_states, "out_grad": out_grad, "doc_lengths": doc_lengths, "proj_weight": proj_weight, "decay_rate": decay_rate, "dt_bias": dt_bias, "skip_gain": skip_gain}


highest = lax.Precision.HIGHEST

def block_states(xs_f, b_mat, dt_step, log_decay, counts):
    last_log = log_decay[-1]
    kept_mask = (counts == counts[-1]).astype(jnp.float32)
    weighting = jnp.exp(last_log[None, :] - log_decay) * kept_mask[:, None] * dt_step
    states = jnp.einsum('sh,shp,sn->hpn', weighting, xs_f, b_mat, precision=highest)
    passing = jnp.exp(last_log) * (counts[-1] == 0).astype(jnp.float32)
    return (states, passing)

def block_passing(dt_step, rates, counts):
    log_decay = jnp.cumsum(-dt_step * rates[None, :], axis=0)
    return jnp.exp(log_decay[-1]) * (counts[-1] == 0).astype(jnp.float32)

def block_scan(start_state, xs_f, b_mat, c_mat, dt_step, rates, counts):
    log_decay = jnp.cumsum(-dt_step * rates[None, :], axis=0)
    positions = jnp.arange(xs_f.shape[0], dtype=jnp.int32)
    causal = (positions[:, None] >= positions[None, :]) & (counts[:, None] == counts[None, :])
    gap_log = jnp.where(causal[:, :, None], log_decay[:, None, :] - log_decay[None, :, :], 0.0)
    decay_mat = jnp.exp(gap_log) * causal[:, :, None].astype(jnp.float32)
    scores = jnp.dot(c_mat, b_mat.T, precision=highest)
    mixing = decay_mat * scores[:, :, None] * dt_step[None, :, :]
    inner_out = jnp.einsum('tsh,shp->thp', mixing, xs_f, precision=highest)
    entry_weight = jnp.exp(log_decay) * (counts == 0).astype(jnp.float32)[:, None]
    carried = jnp.einsum('tn,hpn->thp', c_mat, start_state, precision=highest)
    states, passing = block_states(xs_f, b_mat, dt_step, log_decay, counts)
    return (inner_out + entry_weight[:, :, None] * carried, states + passing[:, None, None] * start_state)

def entry_adjoint(c_mat, dt_step, rates, counts, grad_y):
    log_decay = jnp.cumsum(-dt_step * rates[None, :], axis=0)
    entry_weight = jnp.exp(log_decay) * (counts == 0).astype(jnp.float32)[:, None]
    return jnp.einsum('th,tn,thp->hpn', entry_weight, c_mat, grad_y, precision=highest)

def block_grads(start_state, exit_adj, xs_f, b_mat, c_mat, dt_step, rates, counts, grad_y):

    def local_fn(state_in, xs_in, b_in, c_in, dt_in):
        return block_scan(state_in, xs_in, b_in, c_in, dt_in, rates, counts)
    results, pullback = jax.vjp(local_fn, start_state, xs_f, b_mat, c_mat, dt_step)
    gradients = pullback((grad_y, exit_adj))
    return (results[0], gradients[1], gradients[2], gradients[3], gradients[4])

def layer_tail(inputs, xs_f, gate_in, grad_in, weights, dt_raw, skip_gain, y_ssd, grad_y, grad_xs, grad_b, grad_c, grad_dt):
    rows_all = inputs.shape[0]
    gate_f = gate_in.astype(jnp.float32)
    gate_sig = jax.nn.sigmoid(gate_f)
    y_full = (y_ssd + skip_gain[None, :, None] * xs_f).reshape(rows_all, -1)
    grad_gate = (grad_in * y_full * gate_sig * (1.0 + gate_f * (1.0 - gate_sig))).astype(jnp.bfloat16)
    grad_mixed = (grad_xs + skip_gain[None, :, None] * grad_y).reshape(rows_all, -1).astype(jnp.bfloat16)
    grad_proj = jnp.concatenate([grad_b, grad_c, grad_dt * jax.nn.sigmoid(dt_raw)], axis=1).astype(jnp.bfloat16)
    back_term = jnp.einsum('te,de->td', grad_proj, weights, preferred_element_type=jnp.float32)
    grad_x = (grad_in + back_term).astype(jnp.bfloat16)
    weight_term = jnp.einsum('td,te->de', inputs, grad_proj, preferred_element_type=jnp.float32)
    return (grad_x, grad_mixed, grad_gate, weight_term)

def combine_pairs(earlier, later):
    return (earlier[0] * later[0], later[0][..., None, None] * earlier[1] + later[1])

def per_sequence(inputs, mixed, gate_in, grad_out, lengths, entry_state, weights, rates, dt_shift, skip_gain):
    length_all = inputs.shape[0]
    projected = jnp.dot(inputs, weights, preferred_element_type=jnp.float32)
    b_mat = projected[:, :STATE]
    c_mat = projected[:, STATE:2 * STATE]
    dt_raw = projected[:, 2 * STATE:] + dt_shift[None, :]
    dt_step = jax.nn.softplus(dt_raw)
    xs_f = mixed.astype(jnp.float32).reshape(length_all, HEADS, HEAD_DIM)
    doc_ends = jnp.cumsum(lengths).astype(jnp.int32)
    starts = doc_ends[:-1].astype(jnp.int32)
    positions = jnp.arange(length_all, dtype=jnp.int32)
    resets = jnp.any(positions[:, None] == starts[None, :], axis=1).astype(jnp.int32)

    def to_blocks(array):
        return array.reshape((N_SEG, SEG) + array.shape[1:])
    counts = jnp.cumsum(to_blocks(resets), axis=1).astype(jnp.int32)
    xs_b, b_blk, c_blk, dt_blk = (to_blocks(xs_f), to_blocks(b_mat), to_blocks(c_mat), to_blocks(dt_step))
    passings = jax.vmap(lambda da, ca: block_passing(da, rates, ca))(dt_blk, counts)
    grad_in = grad_out.astype(jnp.float32)
    gate_act = jax.nn.silu(gate_in.astype(jnp.float32))
    grad_y = (grad_in * gate_act).reshape(length_all, HEADS, HEAD_DIM)
    grad_y_blk = to_blocks(grad_y)
    own_adj = jax.vmap(lambda ca, da, cn, ga: entry_adjoint(ca, da, rates, cn, ga))(c_blk, dt_blk, counts, grad_y_blk)

    def backward_step(carried, element):
        return (combine_pairs((jnp.float32(1.0), carried), element)[1], carried)
    zeros_state = jnp.zeros((HEADS, HEAD_DIM, STATE), jnp.float32)
    _, exit_adj = lax.scan(backward_step, zeros_state, (passings, own_adj), reverse=True)
    y_ssd, grad_xs, grad_b, grad_c, grad_dt = jax.vmap(lambda sa, ea, xa, ba, ca, da, cn, ga: block_grads(sa, ea, xa, ba, ca, da, rates, cn, ga))(entry_state, exit_adj, xs_b, b_blk, c_blk, dt_blk, counts, grad_y_blk)

    def flat(array):
        return array.reshape((length_all,) + array.shape[2:])
    return layer_tail(inputs, xs_f, gate_in, grad_in, weights, dt_raw, skip_gain, flat(y_ssd), grad_y, flat(grad_xs), flat(grad_b), flat(grad_c), flat(grad_dt))

def reference(inputs, mixed, gate_in, entry_states, out_grad, doc_lengths, proj_weight, decay_rate, dt_bias, skip_gain):
    incoming = out_grad
    collected = [None, None]
    for layer_idx in (1, 0):

        def per_item(element, layer_idx=layer_idx):
            return per_sequence(element[0], element[1], element[2], element[3], element[4], element[5], proj_weight[layer_idx], decay_rate[layer_idx], dt_bias[layer_idx], skip_gain[layer_idx])
        grad_x, grad_mixed, grad_gate, weight_terms = lax.map(per_item, (inputs[layer_idx], mixed[layer_idx], gate_in[layer_idx], incoming, doc_lengths, entry_states[layer_idx]))
        collected[layer_idx] = (grad_x, grad_mixed, grad_gate, lax.optimization_barrier(jnp.sum(weight_terms, axis=0)))
        incoming = grad_x
    input_grad = jnp.stack([collected[0][0], collected[1][0]])
    mixed_grad = jnp.stack([collected[0][1], collected[1][1]])
    gate_grad = jnp.stack([collected[0][2], collected[1][2]])
    weight_grad = jnp.stack([collected[0][3], collected[1][3]])
    return (input_grad, mixed_grad, gate_grad, weight_grad)
```

```python
import functools

import jax
import jax.numpy as jnp
from jax import lax
from jax.experimental import pallas as pl
from jax.experimental.pallas import tpu as pltpu
from jax.sharding import PartitionSpec as P

MESH = pl.DeviceIdType.MESH
F32 = jnp.float32
BF16 = jnp.bfloat16
HIGH = lax.Precision.HIGHEST
LANES = 128
NEG = -1e30
VMEM_BYTES = 56 * 1024 * 1024
VMEM = pl.BlockSpec(memory_space=pltpu.VMEM)
SMEM = pl.BlockSpec(memory_space=pltpu.SMEM)
NN = (((1,), (0,)), ((), ()))
NT = (((1,), (1,)), ((), ()))
TN = (((0,), (0,)), ((), ()))


def dot(a, b, dims=NN, precision=None):
    return lax.dot_general(a, b, dims, precision=precision, preferred_element_type=F32)


def iota(axis, shape=(LANES, LANES)):
    return lax.broadcasted_iota(jnp.int32, shape, axis)


def tile_at(j):
    return pl.ds(pl.multiple_of(j * LANES, LANES), LANES)


def split_two(value):
    high = value.astype(BF16)
    low = (value - high.astype(F32)).astype(BF16)
    return high, low


def split_three(value):
    high = value.astype(BF16)
    rest = value - high.astype(F32)
    mid = rest.astype(BF16)
    low = (rest - mid.astype(F32)).astype(BF16)
    return high, mid, low


def pass_rows(value):
    high, mid, low = split_three(value)
    row = iota(0, (16, LANES))
    zero = jnp.zeros((16, LANES), F32)
    out = jnp.where(row == 0, high.astype(F32), zero)
    out = jnp.where(row == 1, mid.astype(F32), out)
    out = jnp.where(row == 2, low.astype(F32), out)
    return out.astype(BF16)


def pass_value(rows):
    return jnp.sum(rows.astype(F32), axis=0, keepdims=True)


def place():
    seg = lax.axis_index("seg")
    chip = seg // 2
    core = seg - 2 * chip
    return lax.axis_index("pipe"), seg, chip, core, lax.axis_index("dp")


def greet(devices):
    barrier = pltpu.get_barrier_semaphore()
    for count, device_of in devices:
        def one(k, carry, device_of=device_of):
            pl.semaphore_signal(barrier, inc=1, device_id=device_of(k), device_id_type=MESH)
            return carry

        lax.fori_loop(0, count, one, 0)
    pl.semaphore_wait(barrier, sum(count for count, _ in devices))


def remote(src, dst, send_sem, recv_sem, device):
    return pltpu.make_async_remote_copy(
        src_ref=src, dst_ref=dst, send_sem=send_sem, recv_sem=recv_sem,
        device_id=device, device_id_type=MESH,
    )


def each(count, body):
    def step(k, carry):
        body(k)
        return carry

    lax.fori_loop(0, count, step, 0)


def gather_kernel(n_chip, n_dp, w_ref, own_ref, one_ref, shard, pipe_sems, sems_a, sems_b):
    pipe, seg, chip, core, dp = place()

    def chip_device(k):
        return {"seg": lax.rem(chip + 1 + k, n_chip) * 2 + core}

    def dp_device(k):
        return {"dp": lax.rem(dp + 1 + k, n_dp)}

    def sibling(k):
        return {"seg": seg + 1 - 2 * core}

    def partner(k):
        return {"pipe": 1 - pipe}

    greet([(n_chip - 1, chip_device), (n_dp - 1, dp_device), (1, sibling), (1, partner)])

    def gather(src, dst, sems):
        chip_send, chip_recv, dp_send, dp_recv, core_sems = sems
        dst[chip, core, dp] = src[...]

        def chip_copy(k):
            block = dst.at[chip, core, dp]
            return remote(block, block, chip_send.at[k], chip_recv.at[k], chip_device(k))

        def dp_copy(k):
            block = dst.at[:, core, dp]
            return remote(block, block, dp_send.at[k], dp_recv.at[k], dp_device(k))

        each(n_chip - 1, lambda k: chip_copy(k).start())
        each(n_chip - 1, lambda k: chip_copy(k).wait_recv())
        each(n_dp - 1, lambda k: dp_copy(k).start())
        each(n_dp - 1, lambda k: dp_copy(k).wait_recv())
        block = dst.at[:, core]
        last = remote(block, block, core_sems.at[0], core_sems.at[1], sibling(0))
        last.start()
        last.wait()
        each(n_chip - 1, lambda k: chip_copy(k).wait_send())
        each(n_dp - 1, lambda k: dp_copy(k).wait_send())

    shard_copy = remote(w_ref, shard, pipe_sems.at[0], pipe_sems.at[1], partner(0))

    @pl.when(pipe == 1)
    def _():
        shard_copy.start()

    gather(w_ref, own_ref, sems_a)

    @pl.when(pipe == 1)
    def _():
        shard_copy.wait_send()

    @pl.when(pipe == 0)
    def _():
        shard_copy.wait_recv()
        gather(shard, one_ref, sems_b)


def gather_sems(n_chip, n_dp):
    dma = pltpu.SemaphoreType.DMA
    return (dma((n_chip - 1,)), dma((n_chip - 1,)), dma((n_dp - 1,)), dma((n_dp - 1,)), dma((2,)))


def gather_weights(w, n_chip, n_dp):
    rows, cols = w.shape
    full = jax.ShapeDtypeStruct((n_chip, 2, n_dp, rows, cols), BF16)
    own, one = pl.pallas_call(
        functools.partial(gather_kernel, n_chip, n_dp),
        out_shape=(full, full),
        in_specs=[VMEM],
        out_specs=(VMEM, VMEM),
        scratch_shapes=[
            pltpu.VMEM((rows, cols), BF16),
            pltpu.SemaphoreType.DMA((2,)),
            gather_sems(n_chip, n_dp),
            gather_sems(n_chip, n_dp),
        ],
        compiler_params=pltpu.CompilerParams(
            collective_id=1, has_side_effects=True, vmem_limit_bytes=VMEM_BYTES
        ),
    )(w)
    return own.reshape(-1, cols), one.reshape(-1, cols)


def prep_kernel(
    x_ref, w_ref, bias_ref, rate_ref, doc_ref, s0_ref,
    bf_ref, cf_ref, log_ref, logt_ref, dt_ref, dtt_ref, sig_ref, rho_ref, mask_ref, first_ref, kept_ref,
    s0t_ref, pad,
):
    rows = x_ref.shape[0]
    heads = bias_ref.shape[1]
    state = bf_ref.shape[1]
    projected = dot(x_ref[...], w_ref[...])
    bf_ref[...] = projected[:, :state]
    cf_ref[...] = projected[:, state : 2 * state]
    pad[...] = jnp.zeros_like(pad)
    pad[0, :, :heads] = projected[:, 2 * state :] + bias_ref[...]
    pad[1, 0:1, :heads] = rate_ref[...]
    raw = pad[0]
    rate = pad[1, 0:1, :]
    soft = jnp.maximum(raw, 0.0) + jnp.log1p(jnp.exp(-jnp.abs(raw)))
    sig = 1.0 / (1.0 + jnp.exp(-jnp.abs(raw)))
    sig = jnp.where(raw >= 0, sig, 1.0 - sig)
    small = raw < -15.0
    exp_raw = jnp.exp(jnp.minimum(raw, 0.0))
    sig = jnp.where(small, exp_raw, sig)
    soft = jnp.where(small, exp_raw, soft)
    rho = jnp.where(small, 1.0, sig / jnp.where(small, 1.0, soft))
    lower = (iota(0) >= iota(1)).astype(F32)
    log = dot(lower, -soft * rate, precision=HIGH)
    log_ref[...] = log
    logt_ref[...] = log.T
    dt_ref[...] = soft
    dtt_ref[...] = soft.T
    sig_ref[...] = sig
    rho_ref[...] = rho
    begin = lax.axis_index("seg") * rows
    count_t = jnp.zeros((rows, rows), jnp.int32)
    count_s = jnp.zeros((rows, rows), jnp.int32)
    count_last = jnp.zeros((rows, rows), jnp.int32)
    start = jnp.int32(0)
    for k in range(doc_ref.shape[1] - 1):
        start = start + doc_ref[0, k]
        offset = start - begin
        inside = offset >= 0
        count_t += (inside & (iota(0) >= offset)).astype(jnp.int32)
        count_s += (inside & (iota(1) >= offset)).astype(jnp.int32)
        count_last += jnp.broadcast_to((inside & (offset <= rows - 1)).astype(jnp.int32), (rows, rows))
    allowed = (iota(0) >= iota(1)) & (count_t == count_s)
    mask_ref[...] = jnp.where(allowed, 0.0, NEG)
    first_ref[...] = jnp.where(count_t == 0, 0.0, NEG)
    kept_ref[...] = jnp.where(count_t == count_last, 0.0, NEG)

    def turn(j, carry):
        s0t_ref[j] = s0_ref[tile_at(j), :].T.astype(BF16)
        return carry

    lax.fori_loop(0, s0t_ref.shape[0], turn, 0)


def prepare(x, w, bias, rate, docs, s0):
    rows, width = x.shape
    state = s0.shape[1]
    pairs = width // LANES
    square = jax.ShapeDtypeStruct((rows, LANES), F32)
    return pl.pallas_call(
        prep_kernel,
        out_shape=(square,) * 11 + (jax.ShapeDtypeStruct((pairs, state, LANES), BF16),),
        in_specs=[VMEM, VMEM, VMEM, VMEM, SMEM, VMEM],
        out_specs=(VMEM,) * 12,
        scratch_shapes=[pltpu.VMEM((2, rows, LANES), F32)],
        compiler_params=pltpu.CompilerParams(vmem_limit_bytes=VMEM_BYTES),
    )(x, w, bias, rate, docs, s0)


def pair_columns(ref, j):
    turned = pltpu.roll(ref[...], lax.rem(LANES - 2 * j, LANES), 1)
    shape = (turned.shape[0], LANES)
    return jnp.broadcast_to(turned[:, 0:1], shape), jnp.broadcast_to(turned[:, 1:2], shape)


def by_half(first, second):
    return jnp.where(iota(1, (1, LANES)) < LANES // 2, first, second)


def own_kernel(final, *refs):
    if final:
        out_grad_ref, later_ref, w_ref, gate_ref, cf_ref, log_ref, first_ref, msg_ref, g_ref = refs
        pipe = lax.axis_index("pipe")
        chunk = 512

        def recompute(k, carry):
            cols = pl.ds(pl.multiple_of(k * chunk, chunk), chunk)
            back = dot(later_ref[...], w_ref[cols, :], NT)
            g = out_grad_ref[:, cols].astype(F32)
            g_ref[:, cols] = jnp.where(pipe == 0, g + back, g).astype(BF16)
            return carry

        lax.fori_loop(0, out_grad_ref.shape[1] // chunk, recompute, 0)
    else:
        g_ref, gate_ref, cf_ref, log_ref, first_ref, msg_ref = refs
    ct = cf_ref[...].T.astype(BF16)
    state = ct.shape[0]

    def body(j, carry):
        cols = tile_at(j)
        gate = gate_ref[:, cols].astype(F32)
        grad_y = g_ref[:, cols].astype(F32) * gate * jax.nn.sigmoid(gate)
        log0, log1 = pair_columns(log_ref, j)
        entry = jnp.exp(by_half(log0, log1) + first_ref[...])
        msg_ref[j, 0:state] = dot(ct, (entry * grad_y).astype(BF16)).astype(BF16)
        msg_ref[j, state : state + 16] = pass_rows(entry[-1:, :])
        return carry

    lax.fori_loop(0, msg_ref.shape[0], body, 0)


def own_adjoint(final, args, pairs, state):
    shapes = [jax.ShapeDtypeStruct((pairs, state + 16, LANES), BF16)]
    if final:
        shapes.append(jax.ShapeDtypeStruct(args[0].shape, BF16))
    return pl.pallas_call(
        functools.partial(own_kernel, final),
        out_shape=tuple(shapes),
        in_specs=[VMEM] * len(args),
        out_specs=(VMEM,) * len(shapes),
        compiler_params=pltpu.CompilerParams(vmem_limit_bytes=VMEM_BYTES),
    )(*args)


def scan_kernel(n_chip, n_dp, with_x, *refs):
    if with_x:
        msg_ref, xt_ref, out_ref, group_ref = refs[:4]
        both, total, got, back, exits, other, sems, x_sems = refs[4:]
    else:
        msg_ref, out_ref = refs[:2]
        both, total, got, back, exits, other, sems = refs[2:]
    core_sems, local_sems, send, recv, back_send, back_recv = sems
    pipe, seg, chip, core, dp = place()
    state = out_ref.shape[1]
    half = n_chip

    def chip_device(k):
        return {"seg": lax.rem(chip + 1 + k, n_chip) * 2 + core}

    def sibling(k):
        return {"seg": seg + 1 - 2 * core}

    def group_place(k):
        slot = lax.rem(dp * 2 + core + 1 + k, 2 * n_dp)
        to_dp = slot // 2
        return to_dp, slot - 2 * to_dp

    def group_device(k):
        to_dp, to_core = group_place(k)
        return {"seg": chip * 2 + to_core, "dp": to_dp}

    met = [(n_chip - 1, chip_device)]
    met.append((2 * n_dp - 1, group_device) if with_x else (1, sibling))
    greet(met)

    mine = pl.ds(core * half, half)
    theirs = pl.ds((1 - core) * half, half)
    swap = remote(msg_ref.at[theirs], both.at[core], core_sems.at[0], core_sems.at[1], sibling(0))
    swap.start()
    keep = pltpu.make_async_copy(msg_ref.at[mine], both.at[core], local_sems.at[0])
    keep.start()
    if with_x:
        x_send, x_recv, x_local = x_sems

        def x_copy(k):
            to_dp, to_core = group_place(k)
            return remote(
                xt_ref.at[:, to_core, to_dp], group_ref.at[dp * 2 + core],
                x_send.at[k], x_recv.at[k], group_device(k),
            )

        each(2 * n_dp - 1, lambda k: x_copy(k).start())
        x_keep = pltpu.make_async_copy(xt_ref.at[:, core, dp], group_ref.at[dp * 2 + core], x_local.at[0])
        x_keep.start()
    keep.wait()
    swap.wait()

    def combine(j):
        pass0 = pass_value(both[0, j, state : state + 16])
        pass1 = pass_value(both[1, j, state : state + 16])
        joined = both[0, j, :state].astype(F32) + pass0 * both[1, j, :state].astype(F32)
        total[j, :state] = joined.astype(BF16)
        total[j, state : state + 16] = pass_rows(pass0 * pass1)

    def send_copy(k):
        slot = lax.rem(chip + 1 + k, n_chip)
        return remote(total.at[slot], got.at[chip], send.at[k], recv.at[chip], chip_device(k))

    def combine_send(k):
        combine(lax.rem(chip + 1 + k, n_chip))
        send_copy(k).start()

    each(n_chip - 1, combine_send)
    combine(chip)
    own_copy = pltpu.make_async_copy(total.at[chip], got.at[chip], local_sems.at[1])
    own_copy.start()
    own_copy.wait()

    def back_copy(k):
        return remote(back.at[k], exits.at[chip], back_send.at[k], back_recv.at[chip], {"seg": k * 2 + core})

    def scan(step, carry):
        k = n_chip - 1 - step

        @pl.when(k != chip)
        def _():
            remote(got.at[k], got.at[k], send.at[0], recv.at[k], sibling(0)).wait_recv()

        back[k] = carry.astype(BF16)

        @pl.when(k != chip)
        def _():
            back_copy(k).start()

        return got[k, :state].astype(F32) + pass_value(got[k, state : state + 16]) * carry

    lax.fori_loop(0, n_chip, scan, jnp.zeros((state, LANES), F32))
    own_back = pltpu.make_async_copy(back.at[chip], exits.at[chip], local_sems.at[2])
    own_back.start()
    own_back.wait()

    def finish(j):
        @pl.when(j != chip)
        def _():
            remote(back.at[j], exits.at[j], back_send.at[0], back_recv.at[j], sibling(0)).wait_recv()

        later = exits[j].astype(F32)
        pass1 = pass_value(both[1, j, state : state + 16])
        earlier = both[1, j, :state].astype(F32) + pass1 * later
        is_later = core == 1
        out_ref[core * half + j] = jnp.where(is_later, later, earlier).astype(BF16)
        other[j] = jnp.where(is_later, earlier, later).astype(BF16)

    each(n_chip, finish)
    swap_back = remote(other, out_ref.at[mine], core_sems.at[2], core_sems.at[3], sibling(0))
    swap_back.start()
    each(n_chip - 1, lambda k: send_copy(k).wait_send())

    def sent_back(k):
        @pl.when(k != chip)
        def _():
            back_copy(k).wait_send()

    each(n_chip, sent_back)
    if with_x:
        each(2 * n_dp - 1, lambda k: x_copy(k).wait())
        x_keep.wait()
    swap_back.wait()


def scan_states(msg, xt, n_chip, n_dp, collective_id):
    pairs, rows, lanes = msg.shape
    state = rows - 16
    with_x = xt is not None
    dma = pltpu.SemaphoreType.DMA
    shapes = [jax.ShapeDtypeStruct((pairs, state, lanes), BF16)]
    scratch = [
        pltpu.VMEM((2, n_chip, rows, lanes), BF16),
        pltpu.VMEM((n_chip, rows, lanes), BF16),
        pltpu.VMEM((n_chip, rows, lanes), BF16),
        pltpu.VMEM((n_chip, state, lanes), BF16),
        pltpu.VMEM((n_chip, state, lanes), BF16),
        pltpu.VMEM((n_chip, state, lanes), BF16),
        (dma((4,)), dma((3,)), dma((n_chip,)), dma((n_chip,)), dma((n_chip,)), dma((n_chip,))),
    ]
    args = [msg]
    if with_x:
        shapes.append(jax.ShapeDtypeStruct((2 * n_dp, n_chip, xt.shape[3], xt.shape[4]), BF16))
        scratch.append((dma((2 * n_dp - 1,)), dma((2 * n_dp - 1,)), dma((1,))))
        args.append(xt)
    return pl.pallas_call(
        functools.partial(scan_kernel, n_chip, n_dp, with_x),
        out_shape=tuple(shapes),
        in_specs=[VMEM] * len(args),
        out_specs=(VMEM,) * len(shapes),
        scratch_shapes=scratch,
        compiler_params=pltpu.CompilerParams(
            collective_id=collective_id, has_side_effects=True, vmem_limit_bytes=VMEM_BYTES
        ),
    )(*args)


def grads_kernel(final, *refs):
    (
        x_ref, gate_ref, g_ref, adj_ref, s0t_ref, bf_ref, cf_ref, log_ref, logt_ref, dt_ref, dtt_ref,
        sig_ref, rho_ref, mask_ref, first_ref, kept_ref, rate_ref,
    ) = refs[:17]
    refs = refs[17:]
    if final:
        skip_ref, w_ref, dproj_ref, mixed_grad_ref, gate_grad_ref, input_grad_ref = refs[:6]
        refs = refs[6:]
    else:
        dproj_ref = refs[0]
        refs = refs[1:]
    acc_scores, acc_b, acc_c, acc_y, acc_x, acc_s, acc_a, pad = refs
    for ref in (acc_scores, acc_b, acc_c, acc_y, acc_x, acc_s, acc_a):
        ref[...] = jnp.zeros_like(ref)
    scores = dot(cf_ref[...], bf_ref[...], NT, precision=HIGH)
    b_low = bf_ref[...].astype(BF16)
    c_low = cf_ref[...].astype(BF16)
    first = iota(1, (1, LANES)) < LANES // 2
    heads = rate_ref.shape[1]

    def body(j, carry):
        cols = tile_at(j)
        x_pair = x_ref[:, cols]
        gate = gate_ref[:, cols].astype(F32)
        sig = jax.nn.sigmoid(gate)
        act = gate * sig
        g = g_ref[:, cols].astype(F32)
        grad_y = g * act
        grad_low = grad_y.astype(BF16)
        zero = jnp.zeros_like(x_pair)
        x0, x1 = jnp.where(first, x_pair, zero), jnp.where(first, zero, x_pair)
        y0, y1 = jnp.where(first, grad_low, zero), jnp.where(first, zero, grad_low)
        log0, log1 = pair_columns(log_ref, j)
        dt0, dt1 = pair_columns(dt_ref, j)
        mask = mask_ref[...]
        decay0 = jnp.exp(log0 - logt_ref[pl.ds(2 * j, 1), :] + mask) * dtt_ref[pl.ds(2 * j, 1), :]
        decay1 = jnp.exp(log1 - logt_ref[pl.ds(2 * j + 1, 1), :] + mask) * dtt_ref[pl.ds(2 * j + 1, 1), :]
        mix0 = (decay0 * scores).astype(BF16)
        mix1 = (decay1 * scores).astype(BF16)
        acc_scores[...] += dot(y0, x_pair, NT) * decay0 + dot(y1, x_pair, NT) * decay1
        log_pair = jnp.where(first, log0, log1)
        entry = jnp.exp(log_pair + first_ref[...])
        s0t = s0t_ref[j]
        y = dot(mix0, x0) + dot(mix1, x1) + entry * dot(c_low, s0t)
        acc_c[...] += dot((entry * grad_y).astype(BF16), s0t, NT)
        inner = dot(mix0, y0, TN) + dot(mix1, y1, TN)
        adj = adj_ref[j]
        weight = jnp.exp(log_pair[-1:, :] - log_pair + kept_ref[...]) * jnp.where(first, dt0, dt1)
        outer = weight * dot(b_low, adj)
        x_f = x_pair.astype(F32)
        acc_b[...] += dot((x_f * weight).astype(BF16), adj, NT)
        select = (iota(1) == 2 * j + (iota(0) >= LANES // 2).astype(jnp.int32)).astype(BF16)
        select = jnp.concatenate([select, select], axis=0)

        def heads_of(value):
            return dot(jnp.concatenate(split_two(value), axis=1), select)

        acc_y[...] += heads_of(grad_low.astype(F32) * y)
        acc_x[...] += heads_of(x_f * inner)
        acc_s[...] += heads_of(x_f * outer)
        passed = entry[-1:, :] * jnp.sum(adj.astype(F32) * s0t.astype(F32), axis=0, keepdims=True)
        acc_a[...] += heads_of(jnp.broadcast_to(passed, (8, LANES)))
        if final:
            skip = skip_ref[:, cols]
            slope = sig * (1.0 + gate * (1.0 - sig))
            gate_grad_ref[:, cols] = (g * (y + skip * x_f) * slope).astype(BF16)
            mixed_grad_ref[:, cols] = (inner + outer + skip * grad_y).astype(BF16)
        return carry

    lax.fori_loop(0, adj_ref.shape[0], body, 0)
    pad[...] = jnp.zeros_like(pad)
    pad[0:1, :heads] = rate_ref[...]
    u = acc_x[...] + acc_s[...]
    last = jnp.sum(acc_s[...], axis=0, keepdims=True) + acc_a[0:1, :]
    upper = (iota(0) <= iota(1)).astype(F32)
    log_grad = dot(upper, acc_y[...] - u, precision=HIGH) + last
    raw_grad = u * rho_ref[...] - pad[0:1, :] * log_grad * sig_ref[...]
    b_grad = acc_b[...] + dot(acc_scores[...].T, cf_ref[...], precision=HIGH)
    c_grad = acc_c[...] + dot(acc_scores[...], bf_ref[...], precision=HIGH)
    dproj_ref[:, 0:LANES] = b_grad.astype(BF16)
    dproj_ref[:, LANES : 2 * LANES] = c_grad.astype(BF16)
    dproj_ref[:, 2 * LANES : 2 * LANES + heads] = raw_grad[:, :heads].astype(BF16)
    if final:
        chunk = 512
        dproj = dproj_ref[...]

        def back(k, carry):
            cols = pl.ds(pl.multiple_of(k * chunk, chunk), chunk)
            g = g_ref[:, cols].astype(F32)
            input_grad_ref[:, cols] = (g + dot(dproj, w_ref[cols, :], NT)).astype(BF16)
            return carry

        lax.fori_loop(0, g_ref.shape[1] // chunk, back, 0)


def segment_grads(final, args, proj_cols):
    rows, width = args[0].shape
    square = pltpu.VMEM((rows, LANES), F32)
    shapes = [jax.ShapeDtypeStruct((rows, proj_cols), BF16)]
    if final:
        shapes += [jax.ShapeDtypeStruct((rows, width), BF16)] * 3
    return pl.pallas_call(
        functools.partial(grads_kernel, final),
        out_shape=tuple(shapes),
        in_specs=[VMEM] * len(args),
        out_specs=(VMEM,) * len(shapes),
        scratch_shapes=[square] * 6 + [pltpu.VMEM((8, LANES), F32)] * 2,
        compiler_params=pltpu.CompilerParams(vmem_limit_bytes=VMEM_BYTES),
    )(*args)


def hand_kernel(src_ref, out_ref, sems):
    pipe = lax.axis_index("pipe")

    def partner(k):
        return {"pipe": 1 - pipe}

    greet([(1, partner)])
    copy = remote(src_ref, out_ref, sems.at[0], sems.at[1], partner(0))
    copy.start()
    copy.wait()


def hand_over(value):
    return pl.pallas_call(
        hand_kernel,
        out_shape=jax.ShapeDtypeStruct(value.shape, value.dtype),
        in_specs=[VMEM],
        out_specs=VMEM,
        scratch_shapes=[pltpu.SemaphoreType.DMA((2,))],
        compiler_params=pltpu.CompilerParams(collective_id=4, has_side_effects=True),
    )(value)


def weight_kernel(n_chip, n_dp, xg_ref, dproj_ref, out_ref, grads, part, total, got, sems):
    pipe, seg, chip, core, dp = place()
    group_send, group_recv, send, recv = sems
    members = 2 * n_dp
    me = dp * 2 + core

    def group_device(k):
        slot = lax.rem(me + 1 + k, members)
        to_dp = slot // 2
        return {"seg": chip * 2 + slot - 2 * to_dp, "dp": to_dp}

    def chip_device(k):
        return {"seg": lax.rem(chip + 1 + k, n_chip) * 2 + core}

    greet([(members - 1, group_device), (n_chip - 1, chip_device)])

    def group_copy(k):
        return remote(dproj_ref, grads.at[me], group_send.at[k], group_recv.at[k], group_device(k))

    each(members - 1, lambda k: group_copy(k).start())
    grads[me] = dproj_ref[...]

    def block(m):
        x = xg_ref[m].reshape(-1, xg_ref.shape[3])
        return dot(x, grads[m])

    total[...] = block(me)

    def add(k):
        group_copy(k).wait_recv()
        total[...] += block(lax.rem(me + members - 1 - k, members))

    each(members - 1, add)
    rows = out_ref.shape[0]

    def send_copy(k):
        slot = lax.rem(chip + 1 + k, n_chip)
        return remote(part.at[slot], got.at[k], send.at[k], recv.at[k], chip_device(k))

    def ship(k):
        slot = lax.rem(chip + 1 + k, n_chip)
        part[slot] = total[pl.ds(pl.multiple_of(slot * rows, rows), rows), :].astype(BF16)
        send_copy(k).start()

    each(n_chip - 1, ship)
    out_ref[...] = total[pl.ds(pl.multiple_of(chip * rows, rows), rows), :]

    def collect(k):
        send_copy(k).wait_recv()
        out_ref[...] += got[k].astype(F32)

    each(n_chip - 1, collect)
    each(n_chip - 1, lambda k: send_copy(k).wait_send())
    each(members - 1, lambda k: group_copy(k).wait_send())


def weight_gradient(xg, dproj, n_chip, n_dp):
    rows = xg.shape[2]
    cols = dproj.shape[1]
    dma = pltpu.SemaphoreType.DMA
    members = 2 * n_dp
    return pl.pallas_call(
        functools.partial(weight_kernel, n_chip, n_dp),
        out_shape=jax.ShapeDtypeStruct((rows, cols), F32),
        in_specs=[VMEM, VMEM],
        out_specs=VMEM,
        scratch_shapes=[
            pltpu.VMEM((members,) + dproj.shape, BF16),
            pltpu.VMEM((n_chip, rows, cols), BF16),
            pltpu.VMEM((n_chip * rows, cols), F32),
            pltpu.VMEM((n_chip - 1, rows, cols), BF16),
            (dma((members - 1,)), dma((members - 1,)), dma((n_chip - 1,)), dma((n_chip - 1,))),
        ],
        compiler_params=pltpu.CompilerParams(
            collective_id=5, has_side_effects=True, vmem_limit_bytes=VMEM_BYTES
        ),
    )(xg, dproj)


def local(
    inputs, mixed, gate_in, entry_states, out_grad, doc_lengths, proj_weight, decay_rate, dt_bias, skip_gain
):
    n_chip = lax.axis_size("seg") // 2
    n_dp = lax.axis_size("dp")
    x = inputs[0, 0]
    xs = mixed[0, 0]
    gate = gate_in[0, 0]
    rows, width = x.shape
    state = entry_states.shape[-1]
    pairs = width // LANES
    s0 = entry_states.reshape(width, state)
    g1 = out_grad[0]
    w_own, w_one = gather_weights(proj_weight[0], n_chip, n_dp)
    bf, cf, log, logt, dt, dtt, sig, rho, mask, first, kept, s0t = prepare(
        x, w_own, dt_bias, decay_rate, doc_lengths, s0
    )
    xt = x.T.reshape(n_chip, 2, n_dp, -1, rows)
    skip = jnp.repeat(skip_gain, width // skip_gain.shape[1], axis=1)
    shared = (s0t, bf, cf, log, logt, dt, dtt, sig, rho, mask, first, kept, decay_rate)
    proj_cols = proj_weight.shape[2]

    (msg,) = own_adjoint(False, (g1, gate, cf, log, first), pairs, state)
    adj, xg = scan_states(msg, xt, n_chip, n_dp, 2)
    (dproj_later,) = segment_grads(False, (xs, gate, g1, adj) + shared, proj_cols)
    received = hand_over(dproj_later)

    msg, g = own_adjoint(True, (g1, received, w_one, gate, cf, log, first), pairs, state)
    (adj,) = scan_states(msg, None, n_chip, n_dp, 3)
    dproj, mixed_grad, gate_grad, input_grad = segment_grads(
        True, (xs, gate, g, adj) + shared + (skip, w_own), proj_cols
    )
    weight_grad = weight_gradient(xg, dproj, n_chip, n_dp)
    return (
        input_grad[None, None],
        mixed_grad[None, None],
        gate_grad[None, None],
        weight_grad[None],
    )


def solution(mesh):
    in_specs = (
        P("pipe", "dp", "seg", None),
        P("pipe", "dp", "seg", None),
        P("pipe", "dp", "seg", None),
        P("pipe", "dp", "seg", None, None, None),
        P("dp", "seg", None),
        P("dp", None),
        P("pipe", ("seg", "dp"), None),
        P("pipe", None),
        P("pipe", None),
        P("pipe", None),
    )
    out_specs = (
        P("pipe", "dp", "seg", None),
        P("pipe", "dp", "seg", None),
        P("pipe", "dp", "seg", None),
        P("pipe", ("seg", "dp"), None),
    )
    return jax.shard_map(local, mesh=mesh, in_specs=in_specs, out_specs=out_specs, check_vma=False)
```

```python
import functools

import jax
import jax.numpy as jnp
from jax import lax
from jax.experimental import pallas as pl
from jax.experimental.pallas import tpu as pltpu
from jax.sharding import PartitionSpec as P

MESH = pl.DeviceIdType.MESH
F32 = jnp.float32
BF16 = jnp.bfloat16
HIGH = lax.Precision.HIGHEST
LANES = 128
NEG = -1e30
UNROLL = 4
VMEM_BYTES = 56 * 1024 * 1024
VMEM = pl.BlockSpec(memory_space=pltpu.VMEM)
SMEM = pl.BlockSpec(memory_space=pltpu.SMEM)
NN = (((1,), (0,)), ((), ()))
NT = (((1,), (1,)), ((), ()))
TN = (((0,), (0,)), ((), ()))


def dot(a, b, dims=NN, precision=None):
    return lax.dot_general(a, b, dims, precision=precision, preferred_element_type=F32)


def iota(axis, shape=(LANES, LANES)):
    return lax.broadcasted_iota(jnp.int32, shape, axis)


def tile_at(j):
    return pl.ds(pl.multiple_of(j * LANES, LANES), LANES)


def split_two(value):
    high = value.astype(BF16)
    low = (value - high.astype(F32)).astype(BF16)
    return high, low


def split_three(value):
    high = value.astype(BF16)
    rest = value - high.astype(F32)
    mid = rest.astype(BF16)
    low = (rest - mid.astype(F32)).astype(BF16)
    return high, mid, low


def pass_rows(value):
    high, mid, low = split_three(value)
    row = iota(0, (16, LANES))
    zero = jnp.zeros((16, LANES), F32)
    out = jnp.where(row == 0, high.astype(F32), zero)
    out = jnp.where(row == 1, mid.astype(F32), out)
    out = jnp.where(row == 2, low.astype(F32), out)
    return out.astype(BF16)


def pass_value(rows):
    return jnp.sum(rows.astype(F32), axis=0, keepdims=True)


def place():
    seg = lax.axis_index("seg")
    chip = seg // 2
    core = seg - 2 * chip
    return lax.axis_index("pipe"), seg, chip, core, lax.axis_index("dp")


def greet(devices):
    barrier = pltpu.get_barrier_semaphore()
    for count, device_of in devices:
        def one(k, carry, device_of=device_of):
            pl.semaphore_signal(barrier, inc=1, device_id=device_of(k), device_id_type=MESH)
            return carry

        lax.fori_loop(0, count, one, 0)
    pl.semaphore_wait(barrier, sum(count for count, _ in devices))


def remote(src, dst, send_sem, recv_sem, device):
    return pltpu.make_async_remote_copy(
        src_ref=src, dst_ref=dst, send_sem=send_sem, recv_sem=recv_sem,
        device_id=device, device_id_type=MESH,
    )


def each(count, body, unroll=1):
    def step(k, carry):
        body(k)
        return carry

    lax.fori_loop(0, count, step, 0, unroll=unroll)


class Around:
    def __init__(self, n_chip, n_dp):
        self.n_chip, self.n_dp = n_chip, n_dp
        self.pipe, self.seg, self.chip, self.core, self.dp = place()

    def chip_slot(self, k):
        return lax.rem(self.chip + 1 + k, self.n_chip)

    def chip_device(self, k):
        return {"seg": self.chip_slot(k) * 2 + self.core}

    def dp_slot(self, k):
        return lax.rem(self.dp + 1 + k, self.n_dp)

    def dp_device(self, k):
        return {"dp": self.dp_slot(k)}

    def sibling(self, k=0):
        return {"seg": self.seg + 1 - 2 * self.core}

    def partner(self, k=0):
        return {"pipe": 1 - self.pipe}

    def greet(self, with_pipe):
        met = [(self.n_chip - 1, self.chip_device), (self.n_dp - 1, self.dp_device), (1, self.sibling)]
        greet(met + ([(1, self.partner)] if with_pipe else []))


class Gather:
    def __init__(self, near, dst, sems):
        self.near, self.dst = near, dst
        self.chip_send, self.chip_recv, self.dp_send, self.dp_recv, self.core_sems = sems

    def chip_copy(self, k):
        near = self.near
        block = self.dst.at[near.chip, near.core, near.dp]
        return remote(block, block, self.chip_send.at[k], self.chip_recv.at[k], near.chip_device(k))

    def dp_copy(self, k):
        block = self.dst.at[:, self.near.core, self.near.dp]
        return remote(block, block, self.dp_send.at[k], self.dp_recv.at[k], self.near.dp_device(k))

    def core_copy(self):
        block = self.dst.at[:, self.near.core]
        return remote(block, block, self.core_sems.at[0], self.core_sems.at[1], self.near.sibling())

    def start(self, src):
        near = self.near
        self.dst[near.chip, near.core, near.dp] = src[...]
        each(near.n_chip - 1, lambda k: self.chip_copy(k).start())

    def second(self):
        each(self.near.n_chip - 1, lambda k: self.chip_copy(k).wait_recv())
        each(self.near.n_dp - 1, lambda k: self.dp_copy(k).start())

    def third(self):
        each(self.near.n_dp - 1, lambda k: self.dp_copy(k).wait_recv())
        self.core_copy().start()

    def end(self):
        self.core_copy().wait()
        each(self.near.n_chip - 1, lambda k: self.chip_copy(k).wait_send())
        each(self.near.n_dp - 1, lambda k: self.dp_copy(k).wait_send())


def gather_sems(n_chip, n_dp):
    dma = pltpu.SemaphoreType.DMA
    return (dma((n_chip - 1,)), dma((n_chip - 1,)), dma((n_dp - 1,)), dma((n_dp - 1,)), dma((2,)))


def prep_kernel(
    n_chip, n_dp, shard_ref, x_ref, bias_ref, rate_ref, doc_ref, s0_ref,
    own_ref, bf_ref, cf_ref, log_ref, logt_ref, dt_ref, dtt_ref, sig_ref, rho_ref, mask_ref, first_ref, kept_ref,
    s0t_ref, xt_ref, pad, projected, sems,
):
    near = Around(n_chip, n_dp)
    near.greet(False)
    gather = Gather(near, own_ref, sems)
    gather.start(shard_ref)
    rows = x_ref.shape[0]
    heads = bias_ref.shape[1]
    state = bf_ref.shape[1]

    def turn_state(j):
        s0t_ref[j] = s0_ref[tile_at(j), :].T.astype(BF16)

    def turn_x(chip):
        for core in range(2):
            xt_ref[chip, core] = x_ref[:, tile_at(2 * chip + core)].T

    each(s0t_ref.shape[0], turn_state, UNROLL)
    begin = near.seg * rows
    count_t = jnp.zeros((rows, rows), jnp.int32)
    count_s = jnp.zeros((rows, rows), jnp.int32)
    count_last = jnp.zeros((rows, rows), jnp.int32)
    start = jnp.int32(0)
    for k in range(doc_ref.shape[1] - 1):
        start = start + doc_ref[0, k]
        offset = jnp.broadcast_to(start - begin, (rows, rows))
        inside = offset >= 0
        count_t += (inside & (iota(0) >= offset)).astype(jnp.int32)
        count_s += (inside & (iota(1) >= offset)).astype(jnp.int32)
        count_last += (inside & (offset <= rows - 1)).astype(jnp.int32)
    allowed = (iota(0) >= iota(1)) & (count_t == count_s)
    mask_ref[...] = jnp.where(allowed, 0.0, NEG)
    first_ref[...] = jnp.where(count_t == 0, 0.0, NEG)
    kept_ref[...] = jnp.where(count_t == count_last, 0.0, NEG)
    gather.second()
    each(n_chip, turn_x, 2)
    gather.third()
    projected[...] = jnp.zeros_like(projected)

    def project(core):
        def one(chip):
            w = own_ref[chip, core].reshape(-1, projected.shape[1])
            projected[...] += dot(x_ref[:, tile_at(2 * chip + core)], w)

        each(n_chip, one, UNROLL)

    project(near.core)
    gather.end()
    project(1 - near.core)
    bf_ref[...] = projected[:, :state]
    cf_ref[...] = projected[:, state : 2 * state]
    pad[...] = jnp.zeros_like(pad)
    pad[0, 0:1, :heads] = bias_ref[...]
    pad[1, 0:1, :heads] = rate_ref[...]
    raw = projected[:, 2 * state :] + pad[0, 0:1, :]
    rate = pad[1, 0:1, :]
    soft = jnp.maximum(raw, 0.0) + jnp.log1p(jnp.exp(-jnp.abs(raw)))
    sig = 1.0 / (1.0 + jnp.exp(-jnp.abs(raw)))
    sig = jnp.where(raw >= 0, sig, 1.0 - sig)
    small = raw < -15.0
    exp_raw = jnp.exp(jnp.minimum(raw, 0.0))
    sig = jnp.where(small, exp_raw, sig)
    soft = jnp.where(small, exp_raw, soft)
    rho = jnp.where(small, 1.0, sig / jnp.where(small, 1.0, soft))
    lower = (iota(0) >= iota(1)).astype(F32)
    log = dot(lower, -soft * rate, precision=HIGH)
    log_ref[...] = log
    logt_ref[...] = log.T
    dt_ref[...] = soft
    dtt_ref[...] = soft.T
    sig_ref[...] = sig
    rho_ref[...] = rho


def prepare(shard, x, bias, rate, docs, s0, n_chip, n_dp):
    rows, width = x.shape
    state = s0.shape[1]
    pairs = width // LANES
    cols = shard.shape[1]
    square = jax.ShapeDtypeStruct((rows, LANES), F32)
    return pl.pallas_call(
        functools.partial(prep_kernel, n_chip, n_dp),
        out_shape=(jax.ShapeDtypeStruct((n_chip, 2, n_dp) + shard.shape, BF16),)
        + (square,) * 11
        + (
            jax.ShapeDtypeStruct((pairs, state, LANES), BF16),
            jax.ShapeDtypeStruct((n_chip, 2, LANES, rows), BF16),
        ),
        in_specs=[VMEM, VMEM, VMEM, VMEM, SMEM, VMEM],
        out_specs=(VMEM,) * 14,
        scratch_shapes=[
            pltpu.VMEM((2, 8, LANES), F32),
            pltpu.VMEM((rows, cols), F32),
            gather_sems(n_chip, n_dp),
        ],
        compiler_params=pltpu.CompilerParams(
            collective_id=1, has_side_effects=True, vmem_limit_bytes=VMEM_BYTES
        ),
    )(shard, x, bias, rate, docs, s0)


def pair_columns(ref, j):
    turned = pltpu.roll(ref[...], lax.rem(LANES - 2 * j, LANES), 1)
    shape = (turned.shape[0], LANES)
    return jnp.broadcast_to(turned[:, 0:1], shape), jnp.broadcast_to(turned[:, 1:2], shape)


def by_half(first, second):
    return jnp.where(iota(1, (1, LANES)) < LANES // 2, first, second)


def heads_of(value, j):
    select = (iota(1) == 2 * j + (iota(0) >= LANES // 2).astype(jnp.int32)).astype(BF16)
    high, low = split_two(value)
    return dot(high, select) + dot(low, select)


def layer_kernel(n_chip, n_dp, *refs):
    (
        shard_ref, x_ref, gate_ref, out_grad_ref, w_ref, xt_ref, s0t_ref, bf_ref, cf_ref, log_ref, logt_ref,
        dt_ref, dtt_ref, sig_ref, rho_ref, mask_ref, first_ref, kept_ref, rate_ref, skip_ref,
    ) = refs[:20]
    dproj_ref, mixed_grad_ref, gate_grad_ref, input_grad_ref, group_ref = refs[20:25]
    (
        one_shard, one_ref, later, g_ref, msg, both, total, got, back, exits, other, adj_ref, base, weights,
        x_stage, acc_scores, acc_b, acc_c, acc_y, acc_x, acc_s, acc_a, pad, sems,
    ) = refs[25:]
    (
        gather_set, shard_sems, later_sems, core_sems, local_sems, send, recv, back_send, back_recv,
        other_send, other_recv, xt_sems, xg_send, xg_recv,
    ) = sems
    near = Around(n_chip, n_dp)
    near.greet(True)
    pipe, chip, core, dp = near.pipe, near.chip, near.core, near.dp
    rows = x_ref.shape[0]
    width = x_ref.shape[1]
    state = s0t_ref.shape[1]
    half = n_chip
    chunk = 512
    heads = rate_ref.shape[1]
    proj = w_ref.shape[-1]
    w_rows = w_ref.shape[1] * w_ref.shape[2] * w_ref.shape[3]
    part = shard_ref.shape[0]

    xt_copy = remote(xt_ref.at[:, 1 - core], x_stage, xt_sems.at[0], xt_sems.at[1], near.sibling())
    xt_copy.start()

    shard_copy = remote(shard_ref, one_shard, shard_sems.at[0], shard_sems.at[1], near.partner())
    later_copy = remote(dproj_ref, later, later_sems.at[0], later_sems.at[1], near.partner())

    for ref in (acc_scores, acc_b, acc_c, acc_y, acc_x, acc_s, acc_a):
        ref[...] = jnp.zeros_like(ref)

    @pl.when(pipe == 1)
    def _():
        shard_copy.start()

        def keep(k):
            cols = pl.ds(pl.multiple_of(k * chunk, chunk), chunk)
            g_ref[:, cols] = out_grad_ref[:, cols]

        each(width // chunk, keep)
        shard_copy.wait_send()

    @pl.when(pipe == 0)
    def _():
        shard_copy.wait_recv()
        gather = Gather(near, one_ref, gather_set)
        gather.start(one_shard)
        gather.second()
        gather.third()
        gather.end()
        later_copy.wait_recv()

        def recompute(k):
            cols = pl.ds(pl.multiple_of(k * w_rows, w_rows), w_rows)
            sent = dot(later[...], one_ref[k].reshape(w_rows, proj), NT)
            g_ref[:, cols] = (out_grad_ref[:, cols].astype(F32) + sent).astype(BF16)

        each(n_chip, recompute, 2)

    ct = cf_ref[...].T.astype(BF16)

    def own(j):
        cols = tile_at(j)
        gate = gate_ref[:, cols].astype(F32)
        grad_y = g_ref[:, cols].astype(F32) * gate * jax.nn.sigmoid(gate)
        log0, log1 = pair_columns(log_ref, j)
        entry = jnp.exp(by_half(log0, log1) + first_ref[...])
        msg[j, 0:state] = dot(ct, (entry * grad_y).astype(BF16)).astype(BF16)
        msg[j, state : state + 16] = pass_rows(entry[-1:, :])

    mine = pl.ds(core * half, half)
    theirs = pl.ds((1 - core) * half, half)
    swap = remote(msg.at[theirs], both.at[core], core_sems.at[0], core_sems.at[1], near.sibling())
    keep_mine = pltpu.make_async_copy(msg.at[mine], both.at[core], local_sems.at[0])
    each(half, lambda j: own((1 - core) * half + j), UNROLL)
    swap.start()
    each(half, lambda j: own(core * half + j), UNROLL)
    keep_mine.start()
    keep_mine.wait()
    swap.wait()

    def combine(j):
        pass0 = pass_value(both[0, j, state : state + 16])
        pass1 = pass_value(both[1, j, state : state + 16])
        joined = both[0, j, :state].astype(F32) + pass0 * both[1, j, :state].astype(F32)
        total[j, :state] = joined.astype(BF16)
        total[j, state : state + 16] = pass_rows(pass0 * pass1)

    def send_copy(k):
        return remote(
            total.at[near.chip_slot(k)], got.at[chip], send.at[k], recv.at[chip], near.chip_device(k)
        )

    def combine_send(k):
        combine(near.chip_slot(k))
        send_copy(k).start()

    each(n_chip - 1, combine_send)
    combine(chip)
    got[chip] = total[chip]

    xt_copy.wait()

    def x_copy(k, src, from_core):
        to = near.dp_slot(k)
        cut = pl.ds(pl.multiple_of(to * part, part), part)
        return remote(
            src.at[:, cut], group_ref.at[dp, from_core],
            xg_send.at[from_core, k], xg_recv.at[from_core, k], near.dp_device(k),
        )

    def x_start(k):
        x_copy(k, xt_ref.at[:, core], core).start()
        x_copy(k, x_stage, 1 - core).start()

    each(n_dp - 1, x_start)
    cut = pl.ds(pl.multiple_of(dp * part, part), part)
    group_ref[dp, core] = xt_ref[:, core, cut]
    group_ref[dp, 1 - core] = x_stage[:, cut]

    scores = dot(cf_ref[...], bf_ref[...], NT, precision=HIGH)
    b_low = bf_ref[...].astype(BF16)
    c_low = cf_ref[...].astype(BF16)
    first = iota(1, (1, LANES)) < LANES // 2

    def before(j):
        cols = tile_at(j)
        x_pair = x_ref[:, cols]
        x_f = x_pair.astype(F32)
        gate = gate_ref[:, cols].astype(F32)
        sig = jax.nn.sigmoid(gate)
        g = g_ref[:, cols].astype(F32)
        grad_y = g * gate * sig
        grad_low = grad_y.astype(BF16)
        zero = jnp.zeros_like(x_pair)
        x0, x1 = jnp.where(first, x_pair, zero), jnp.where(first, zero, x_pair)
        y0, y1 = jnp.where(first, grad_low, zero), jnp.where(first, zero, grad_low)
        log0, log1 = pair_columns(log_ref, j)
        dt0, dt1 = pair_columns(dt_ref, j)
        mask = mask_ref[...]
        decay0 = jnp.exp(log0 - logt_ref[pl.ds(2 * j, 1), :] + mask) * dtt_ref[pl.ds(2 * j, 1), :]
        decay1 = jnp.exp(log1 - logt_ref[pl.ds(2 * j + 1, 1), :] + mask) * dtt_ref[pl.ds(2 * j + 1, 1), :]
        mix0 = (decay0 * scores).astype(BF16)
        mix1 = (decay1 * scores).astype(BF16)
        acc_scores[...] += dot(y0, x_pair, NT) * decay0 + dot(y1, x_pair, NT) * decay1
        log_pair = jnp.where(first, log0, log1)
        entry = jnp.exp(log_pair + first_ref[...])
        s0t = s0t_ref[j]
        y = dot(mix0, x0) + dot(mix1, x1) + entry * dot(c_low, s0t)
        acc_c[...] += dot((entry * grad_y).astype(BF16), s0t, NT)
        inner = dot(mix0, y0, TN) + dot(mix1, y1, TN)
        weights[j] = jnp.exp(log_pair[-1:, :] - log_pair + kept_ref[...]) * jnp.where(first, dt0, dt1)
        x_inner = x_f * inner
        acc_y[...] += heads_of(grad_low.astype(F32) * y - x_inner, j)
        acc_x[...] += heads_of(x_inner, j)
        skip = skip_ref[:, cols]
        slope = sig * (1.0 + gate * (1.0 - sig))
        gate_grad_ref[:, cols] = (g * (y + skip * x_f) * slope).astype(BF16)
        base[j] = inner + skip * grad_y

    each(half, before, UNROLL)

    def back_copy(k):
        return remote(
            back.at[k], exits.at[chip], back_send.at[k], back_recv.at[chip], {"seg": k * 2 + core}
        )

    def scan(step, carry):
        k = n_chip - 1 - step

        @pl.when(k != chip)
        def _():
            remote(got.at[k], got.at[k], send.at[0], recv.at[k], near.sibling()).wait_recv()

        back[k] = carry.astype(BF16)

        @pl.when(k != chip)
        def _():
            back_copy(k).start()

        return got[k, :state].astype(F32) + pass_value(got[k, state : state + 16]) * carry

    lax.fori_loop(0, n_chip, scan, jnp.zeros((state, LANES), F32))
    exits[chip] = back[chip]
    each(half, lambda j: before(half + j), UNROLL)

    def other_copy(j):
        return remote(
            other.at[j], adj_ref.at[core * half + j], other_send.at[j], other_recv.at[j], near.sibling()
        )

    def finish(j):
        @pl.when(j != chip)
        def _():
            remote(back.at[j], exits.at[j], back_send.at[0], back_recv.at[j], near.sibling()).wait_recv()

        after = exits[j].astype(F32)
        pass1 = pass_value(both[1, j, state : state + 16])
        earlier = both[1, j, :state].astype(F32) + pass1 * after
        is_later = core == 1
        adj_ref[core * half + j] = jnp.where(is_later, after, earlier).astype(BF16)
        other[j] = jnp.where(is_later, earlier, after).astype(BF16)
        other_copy(j).start()

    each(n_chip, finish)

    def after_scan(j):
        cols = tile_at(j)
        adj = adj_ref[j]
        weight = weights[j]
        x_f = x_ref[:, cols].astype(F32)
        outer = weight * dot(b_low, adj)
        acc_b[...] += dot((x_f * weight).astype(BF16), adj, NT)
        acc_s[...] += heads_of(x_f * outer, j)
        log0, log1 = pair_columns(log_ref, j)
        last = jnp.exp(by_half(log0[-8:], log1[-8:]) + first_ref[rows - 8 :, :])[-1:]
        passed = last * jnp.sum(adj.astype(F32) * s0t_ref[j].astype(F32), axis=0, keepdims=True)
        select = (iota(1) == 2 * j + (iota(0) >= LANES // 2).astype(jnp.int32)).astype(BF16)
        high, low = split_two(jnp.broadcast_to(passed, (8, LANES)))
        acc_a[...] += dot(high, select) + dot(low, select)
        mixed_grad_ref[:, cols] = (base[j] + outer).astype(BF16)

    each(half, lambda j: after_scan(core * half + j), UNROLL)
    each(half, lambda j: other_copy(j).wait())
    each(half, lambda j: after_scan((1 - core) * half + j), UNROLL)

    pad[...] = jnp.zeros_like(pad)
    pad[0:1, :heads] = rate_ref[...]
    u = acc_x[...] + acc_s[...]
    last = jnp.sum(acc_s[...], axis=0, keepdims=True) + acc_a[0:1, :]
    upper = (iota(0) <= iota(1)).astype(F32)
    log_grad = dot(upper, acc_y[...] - acc_s[...], precision=HIGH) + last
    raw_grad = u * rho_ref[...] - pad[0:1, :] * log_grad * sig_ref[...]
    b_grad = acc_b[...] + dot(acc_scores[...].T, cf_ref[...], precision=HIGH)
    c_grad = acc_c[...] + dot(acc_scores[...], bf_ref[...], precision=HIGH)
    dproj_ref[:, 0:LANES] = b_grad.astype(BF16)
    dproj_ref[:, LANES : 2 * LANES] = c_grad.astype(BF16)
    dproj_ref[:, 2 * LANES :] = raw_grad.astype(BF16)

    @pl.when(pipe == 1)
    def _():
        later_copy.start()

    def give(k):
        cols = pl.ds(pl.multiple_of(k * w_rows, w_rows), w_rows)
        sent = dot(dproj_ref[...], w_ref[k].reshape(w_rows, proj), NT)
        input_grad_ref[:, cols] = (g_ref[:, cols].astype(F32) + sent).astype(BF16)

    each(n_chip, give, 2)

    @pl.when(pipe == 1)
    def _():
        later_copy.wait_send()

    each(n_chip - 1, lambda k: send_copy(k).wait_send())

    def sent_back(k):
        @pl.when(k != chip)
        def _():
            back_copy(k).wait_send()

    each(n_chip, sent_back)

    def x_wait(k):
        x_copy(k, xt_ref.at[:, core], core).wait()
        x_copy(k, x_stage, 1 - core).wait()

    each(n_dp - 1, x_wait)


def layer_grads(args, n_chip, n_dp):
    shard, x = args[:2]
    rows, width = x.shape
    pairs = width // LANES
    state = args[6].shape[1]
    cols = shard.shape[1]
    part = shard.shape[0]
    dma = pltpu.SemaphoreType.DMA
    square = pltpu.VMEM((rows, LANES), F32)
    line = jax.ShapeDtypeStruct((rows, width), BF16)
    return pl.pallas_call(
        functools.partial(layer_kernel, n_chip, n_dp),
        out_shape=(
            jax.ShapeDtypeStruct((rows, cols), BF16), line, line, line,
            jax.ShapeDtypeStruct((n_dp, 2, n_chip, part, rows), BF16),
        ),
        in_specs=[VMEM] * len(args),
        out_specs=(VMEM,) * 5,
        scratch_shapes=[
            pltpu.VMEM(shard.shape, BF16),
            pltpu.VMEM((n_chip, 2, n_dp) + shard.shape, BF16),
            pltpu.VMEM((rows, cols), BF16),
            pltpu.VMEM((rows, width), BF16),
            pltpu.VMEM((pairs, state + 16, LANES), BF16),
            pltpu.VMEM((2, n_chip, state + 16, LANES), BF16),
            pltpu.VMEM((n_chip, state + 16, LANES), BF16),
            pltpu.VMEM((n_chip, state + 16, LANES), BF16),
            pltpu.VMEM((n_chip, state, LANES), BF16),
            pltpu.VMEM((n_chip, state, LANES), BF16),
            pltpu.VMEM((n_chip, state, LANES), BF16),
            pltpu.VMEM((pairs, state, LANES), BF16),
            pltpu.VMEM((pairs, rows, LANES), F32),
            pltpu.VMEM((pairs, rows, LANES), F32),
            pltpu.VMEM((n_chip, LANES, rows), BF16),
        ]
        + [square] * 6
        + [pltpu.VMEM((8, LANES), F32)] * 2
        + [
            (
                gather_sems(n_chip, n_dp), dma((2,)), dma((2,)), dma((2,)), dma((1,)), dma((n_chip,)),
                dma((n_chip,)), dma((n_chip,)), dma((n_chip,)), dma((n_chip,)), dma((n_chip,)), dma((2,)),
                dma((2, n_dp - 1)), dma((2, n_dp - 1)),
            )
        ],
        compiler_params=pltpu.CompilerParams(
            collective_id=2, has_side_effects=True, vmem_limit_bytes=VMEM_BYTES
        ),
    )(*args)


def weight_kernel(n_chip, n_dp, xg_ref, dproj_ref, out_ref, grads, part, total, got, sems):
    near = Around(n_chip, n_dp)
    near.greet(False)
    chip, core, dp = near.chip, near.core, near.dp
    dp_send, dp_recv, core_sems, send, recv = sems
    rows = out_ref.shape[0]
    cols = out_ref.shape[1]
    grads[core, dp] = dproj_ref[...]

    def dp_copy(k):
        return remote(dproj_ref, grads.at[core, dp], dp_send.at[k], dp_recv.at[k], near.dp_device(k))

    each(n_dp - 1, lambda k: dp_copy(k).start())
    total[...] = jnp.zeros_like(total)

    def add(from_core, k):
        total[...] += dot(xg_ref[k, from_core].reshape(-1, xg_ref.shape[4]), grads[from_core, k])

    add(core, dp)
    each(n_dp - 1, lambda k: dp_copy(k).wait_recv())
    swap = remote(grads.at[core], grads.at[core], core_sems.at[0], core_sems.at[1], near.sibling())
    swap.start()
    each(n_dp - 1, lambda k: add(core, near.dp_slot(k)))
    swap.wait()
    each(n_dp, lambda k: add(1 - core, k))

    def send_copy(k):
        return remote(part.at[near.chip_slot(k)], got.at[k], send.at[k], recv.at[k], near.chip_device(k))

    def ship(k):
        slot = near.chip_slot(k)
        part[slot] = total[pl.ds(pl.multiple_of(slot * rows, rows), rows), :].astype(BF16)
        send_copy(k).start()

    each(n_chip - 1, ship)
    out_ref[...] = total[pl.ds(pl.multiple_of(chip * rows, rows), rows), :cols]

    def collect(k):
        send_copy(k).wait_recv()
        out_ref[...] += got[k, :, :cols].astype(F32)

    each(n_chip - 1, collect)
    each(n_chip - 1, lambda k: send_copy(k).wait_send())
    each(n_dp - 1, lambda k: dp_copy(k).wait_send())


def weight_gradient(xg, dproj, proj_cols, n_chip, n_dp):
    rows = xg.shape[3]
    cols = dproj.shape[1]
    dma = pltpu.SemaphoreType.DMA
    return pl.pallas_call(
        functools.partial(weight_kernel, n_chip, n_dp),
        out_shape=jax.ShapeDtypeStruct((rows, proj_cols), F32),
        in_specs=[VMEM, VMEM],
        out_specs=VMEM,
        scratch_shapes=[
            pltpu.VMEM((2, n_dp) + dproj.shape, BF16),
            pltpu.VMEM((n_chip, rows, cols), BF16),
            pltpu.VMEM((n_chip * rows, cols), F32),
            pltpu.VMEM((n_chip - 1, rows, cols), BF16),
            (dma((n_dp - 1,)), dma((n_dp - 1,)), dma((2,)), dma((n_chip - 1,)), dma((n_chip - 1,))),
        ],
        compiler_params=pltpu.CompilerParams(
            collective_id=3, has_side_effects=True, vmem_limit_bytes=VMEM_BYTES
        ),
    )(xg, dproj)


def local(
    inputs, mixed, gate_in, entry_states, out_grad, doc_lengths, proj_weight, decay_rate, dt_bias, skip_gain
):
    n_chip = lax.axis_size("seg") // 2
    n_dp = lax.axis_size("dp")
    x = inputs[0, 0]
    width = x.shape[1]
    s0 = entry_states.reshape(width, entry_states.shape[-1])
    proj_cols = proj_weight.shape[2]
    shard = jnp.pad(proj_weight[0], ((0, 0), (0, -proj_cols % LANES)))
    w, bf, cf, log, logt, dt, dtt, sig, rho, mask, first, kept, s0t, xt = prepare(
        shard, x, dt_bias, decay_rate, doc_lengths, s0, n_chip, n_dp
    )
    skip = jnp.repeat(skip_gain, width // skip_gain.shape[1], axis=1)
    dproj, mixed_grad, gate_grad, input_grad, group = layer_grads(
        (
            shard, mixed[0, 0], gate_in[0, 0], out_grad[0], w, xt, s0t, bf, cf, log, logt, dt, dtt, sig, rho,
            mask, first, kept, decay_rate, skip,
        ),
        n_chip,
        n_dp,
    )
    weight_grad = weight_gradient(group, dproj, proj_cols, n_chip, n_dp)
    return (
        input_grad[None, None],
        mixed_grad[None, None],
        gate_grad[None, None],
        weight_grad[None],
    )


def solution(mesh):
    in_specs = (
        P("pipe", "dp", "seg", None),
        P("pipe", "dp", "seg", None),
        P("pipe", "dp", "seg", None),
        P("pipe", "dp", "seg", None, None, None),
        P("dp", "seg", None),
        P("dp", None),
        P("pipe", ("seg", "dp"), None),
        P("pipe", None),
        P("pipe", None),
        P("pipe", None),
    )
    out_specs = (
        P("pipe", "dp", "seg", None),
        P("pipe", "dp", "seg", None),
        P("pipe", "dp", "seg", None),
        P("pipe", ("seg", "dp"), None),
    )
    return jax.shard_map(local, mesh=mesh, in_specs=in_specs, out_specs=out_specs, check_vma=False)
```

```python
import functools

import jax
import jax.numpy as jnp
from jax import lax
from jax.experimental import pallas as pl
from jax.experimental.pallas import tpu as pltpu
from jax.sharding import PartitionSpec as P

MESH = pl.DeviceIdType.MESH
F32 = jnp.float32
BF16 = jnp.bfloat16
HIGH = lax.Precision.HIGHEST
LANES = 128
NEG = -1e30
UNROLL = 4
VMEM_BYTES = 56 * 1024 * 1024
VMEM = pl.BlockSpec(memory_space=pltpu.VMEM)
SMEM = pl.BlockSpec(memory_space=pltpu.SMEM)
NN = (((1,), (0,)), ((), ()))
NT = (((1,), (1,)), ((), ()))
TN = (((0,), (0,)), ((), ()))


def dot(a, b, dims=NN, precision=None):
    return lax.dot_general(a, b, dims, precision=precision, preferred_element_type=F32)


def iota(axis, shape=(LANES, LANES)):
    return lax.broadcasted_iota(jnp.int32, shape, axis)


def tile_at(j):
    return pl.ds(pl.multiple_of(j * LANES, LANES), LANES)


def split_two(value):
    high = value.astype(BF16)
    low = (value - high.astype(F32)).astype(BF16)
    return high, low


def split_three(value):
    high = value.astype(BF16)
    rest = value - high.astype(F32)
    mid = rest.astype(BF16)
    low = (rest - mid.astype(F32)).astype(BF16)
    return high, mid, low


def pass_rows(value):
    high, mid, low = split_three(value)
    row = iota(0, (16, LANES))
    zero = jnp.zeros((16, LANES), F32)
    out = jnp.where(row == 0, high.astype(F32), zero)
    out = jnp.where(row == 1, mid.astype(F32), out)
    out = jnp.where(row == 2, low.astype(F32), out)
    return out.astype(BF16)


def pass_value(rows):
    return jnp.sum(rows.astype(F32), axis=0, keepdims=True)


def place():
    seg = lax.axis_index("seg")
    chip = seg // 2
    core = seg - 2 * chip
    return lax.axis_index("pipe"), seg, chip, core, lax.axis_index("dp")


def greet(devices):
    barrier = pltpu.get_barrier_semaphore()
    for count, device_of in devices:
        def one(k, carry, device_of=device_of):
            pl.semaphore_signal(barrier, inc=1, device_id=device_of(k), device_id_type=MESH)
            return carry

        lax.fori_loop(0, count, one, 0)
    pl.semaphore_wait(barrier, sum(count for count, _ in devices))


def remote(src, dst, send_sem, recv_sem, device):
    return pltpu.make_async_remote_copy(
        src_ref=src, dst_ref=dst, send_sem=send_sem, recv_sem=recv_sem,
        device_id=device, device_id_type=MESH,
    )


def each(count, body, unroll=1):
    def step(k, carry):
        body(k)
        return carry

    lax.fori_loop(0, count, step, 0, unroll=unroll)


class Around:
    def __init__(self, n_chip, n_dp):
        self.n_chip, self.n_dp = n_chip, n_dp
        self.pipe, self.seg, self.chip, self.core, self.dp = place()

    def chip_slot(self, k):
        return lax.rem(self.chip + 1 + k, self.n_chip)

    def chip_device(self, k):
        return {"seg": self.chip_slot(k) * 2 + self.core}

    def dp_slot(self, k):
        return lax.rem(self.dp + 1 + k, self.n_dp)

    def dp_device(self, k):
        return {"dp": self.dp_slot(k)}

    def sibling(self, k=0):
        return {"seg": self.seg + 1 - 2 * self.core}

    def partner(self, k=0):
        return {"pipe": 1 - self.pipe}

    def greet(self, with_pipe):
        met = [(self.n_chip - 1, self.chip_device), (self.n_dp - 1, self.dp_device), (1, self.sibling)]
        greet(met + ([(1, self.partner)] if with_pipe else []))


class Gather:
    def __init__(self, near, dst, sems):
        self.near, self.dst = near, dst
        self.chip_send, self.chip_recv, self.dp_send, self.dp_recv, self.core_sems = sems

    def chip_copy(self, k):
        near = self.near
        block = self.dst.at[near.chip, near.core, near.dp]
        return remote(block, block, self.chip_send.at[k], self.chip_recv.at[k], near.chip_device(k))

    def dp_copy(self, k):
        block = self.dst.at[:, self.near.core, self.near.dp]
        return remote(block, block, self.dp_send.at[k], self.dp_recv.at[k], self.near.dp_device(k))

    def core_copy(self):
        block = self.dst.at[:, self.near.core]
        return remote(block, block, self.core_sems.at[0], self.core_sems.at[1], self.near.sibling())

    def start(self, src):
        near = self.near
        self.dst[near.chip, near.core, near.dp] = src[...]
        each(near.n_chip - 1, lambda k: self.chip_copy(k).start())

    def second(self):
        each(self.near.n_chip - 1, lambda k: self.chip_copy(k).wait_recv())
        each(self.near.n_dp - 1, lambda k: self.dp_copy(k).start())

    def third(self):
        each(self.near.n_dp - 1, lambda k: self.dp_copy(k).wait_recv())
        self.core_copy().start()

    def end(self):
        self.core_copy().wait()
        each(self.near.n_chip - 1, lambda k: self.chip_copy(k).wait_send())
        each(self.near.n_dp - 1, lambda k: self.dp_copy(k).wait_send())


def gather_sems(n_chip, n_dp):
    dma = pltpu.SemaphoreType.DMA
    return (dma((n_chip - 1,)), dma((n_chip - 1,)), dma((n_dp - 1,)), dma((n_dp - 1,)), dma((2,)))


def pair_columns(ref, j):
    turned = pltpu.roll(ref[...], lax.rem(LANES - 2 * j, LANES), 1)
    shape = (turned.shape[0], LANES)
    return jnp.broadcast_to(turned[:, 0:1], shape), jnp.broadcast_to(turned[:, 1:2], shape)


def by_half(first, second):
    return jnp.where(iota(1, (1, LANES)) < LANES // 2, first, second)


def heads_of(value, j):
    select = (iota(1) == 2 * j + (iota(0) >= LANES // 2).astype(jnp.int32)).astype(BF16)
    high, low = split_two(value)
    return dot(high, select) + dot(low, select)


def layer_kernel(n_chip, n_dp, *refs):
    (
        shard_ref, x_hbm, mixed_hbm, gate_hbm, out_grad_hbm, s0_hbm, rate_ref, bias_ref, skip_ref, doc_ref,
        input_out, mixed_out, gate_out, weight_out,
        x_ref, xs_ref, gate_ref, g_ref, s0_ref, shard, own_ref, one_shard, one_ref, later,
        s0t_ref, xt_ref, x_stage, group_ref, act_ref, es_ref, weights, projected, bf_ref, cf_ref,
        log_ref, logt_ref, dt_ref, dtt_ref, sig_ref, rho_ref, mask_ref, first_ref, kept_ref, small,
        msg, both, total, got, back, exits, other, adj_ref, base, dproj_ref,
        input_grad_ref, mixed_grad_ref, gate_grad_ref,
        acc_scores, acc_b, acc_c, acc_y, acc_x, acc_s, acc_a, grads, part, whole, arrived, sems,
    ) = refs
    (
        in_sems, out_sems, own_set, one_set, shard_sems, later_sems, core_send, core_recv, send, recv,
        back_send, back_recv, other_send, other_recv, xt_sems, xg_send, xg_recv,
        dp_send, dp_recv, grad_sems, sum_send, sum_recv,
    ) = sems
    rows, width = x_ref.shape
    state = bf_ref.shape[1]
    heads = rate_ref.shape[1]
    cols_w = shard_ref.shape[1]
    piece = shard_ref.shape[0]
    proj = shard.shape[1]
    w_rows = 2 * n_dp * piece
    half = n_chip

    loads = [
        pltpu.make_async_copy(src, dst, in_sems.at[i])
        for i, (src, dst) in enumerate(
            ((gate_hbm, gate_ref), (s0_hbm, s0_ref), (x_hbm, x_ref), (out_grad_hbm, g_ref), (mixed_hbm, xs_ref))
        )
    ]
    for load in loads:
        load.start()
    shard[...] = jnp.zeros_like(shard)
    shard[:, :cols_w] = shard_ref[...]

    near = Around(n_chip, n_dp)
    near.greet(True)
    pipe, chip, core, dp = near.pipe, near.chip, near.core, near.dp
    shard_copy = remote(shard, one_shard, shard_sems.at[0], shard_sems.at[1], near.partner())
    later_copy = remote(dproj_ref, later, later_sems.at[0], later_sems.at[1], near.partner())

    gather = Gather(near, own_ref, own_set)
    gather.start(shard)

    @pl.when(pipe == 1)
    def _():
        shard_copy.start()

    for ref in (acc_scores, acc_b, acc_c, acc_y, acc_x, acc_s, acc_a, small, projected, whole):
        ref[...] = jnp.zeros_like(ref)
    small[0:1, :heads] = rate_ref[...]
    small[8:9, :heads] = bias_ref[...]
    small[16:17, :heads] = skip_ref[...]
    begin = near.seg * rows
    count_t = jnp.zeros((rows, rows), jnp.int32)
    count_s = jnp.zeros((rows, rows), jnp.int32)
    count_last = jnp.zeros((rows, rows), jnp.int32)
    start = jnp.int32(0)
    for k in range(doc_ref.shape[1] - 1):
        start = start + doc_ref[0, k]
        offset = jnp.broadcast_to(start - begin, (rows, rows))
        inside = offset >= 0
        count_t += (inside & (iota(0) >= offset)).astype(jnp.int32)
        count_s += (inside & (iota(1) >= offset)).astype(jnp.int32)
        count_last += (inside & (offset <= rows - 1)).astype(jnp.int32)
    allowed = (iota(0) >= iota(1)) & (count_t == count_s)
    mask_ref[...] = jnp.where(allowed, 0.0, NEG)
    first_ref[...] = jnp.where(count_t == 0, 0.0, NEG)
    kept_ref[...] = jnp.where(count_t == count_last, 0.0, NEG)

    def activate(j):
        gate = gate_ref[:, tile_at(j)].astype(F32)
        act_ref[j] = gate * jax.nn.sigmoid(gate)

    def turn_state(j):
        s0t_ref[j] = s0_ref[tile_at(j), :].T.astype(BF16)

    def turn_x(k):
        for c in range(2):
            xt_ref[k, c] = x_ref[:, tile_at(2 * k + c)].T

    loads[0].wait()
    each(2 * half, activate, UNROLL)
    loads[1].wait()
    each(2 * half, turn_state, UNROLL)
    gather.second()
    loads[2].wait()
    each(n_chip, turn_x, 2)
    xt_copy = remote(xt_ref.at[:, 1 - core], x_stage, xt_sems.at[0], xt_sems.at[1], near.sibling())
    xt_copy.start()
    gather.third()

    def project(c):
        def one(k):
            projected[...] += dot(x_ref[:, tile_at(2 * k + c)], own_ref[k, c].reshape(-1, proj))

        each(n_chip, one, UNROLL)

    project(core)
    gather.end()
    project(1 - core)
    bf_ref[...] = projected[:, :state]
    cf_ref[...] = projected[:, state : 2 * state]
    raw = projected[:, 2 * state :] + small[8:9, :]
    soft = jnp.maximum(raw, 0.0) + jnp.log1p(jnp.exp(-jnp.abs(raw)))
    sig = 1.0 / (1.0 + jnp.exp(-jnp.abs(raw)))
    sig = jnp.where(raw >= 0, sig, 1.0 - sig)
    tiny = raw < -15.0
    exp_raw = jnp.exp(jnp.minimum(raw, 0.0))
    sig = jnp.where(tiny, exp_raw, sig)
    soft = jnp.where(tiny, exp_raw, soft)
    sig_ref[...] = sig
    rho_ref[...] = jnp.where(tiny, 1.0, sig / jnp.where(tiny, 1.0, soft))
    lower = (iota(0) >= iota(1)).astype(F32)
    log = dot(lower, -soft * small[0:1, :], precision=HIGH)
    log_ref[...] = log
    logt_ref[...] = log.T
    dt_ref[...] = soft
    dtt_ref[...] = soft.T
    first = iota(1, (1, LANES)) < LANES // 2

    def decays(j):
        log0, log1 = pair_columns(log_ref, j)
        log_pair = jnp.where(first, log0, log1)
        entry = jnp.exp(log_pair + first_ref[...])
        es_ref[j] = entry * act_ref[j]
        msg[j, state : state + 16] = pass_rows(entry[-1:, :])

    each(2 * half, decays, UNROLL)
    loads[3].wait()

    @pl.when(pipe == 0)
    def _():
        shard_copy.wait_recv()
        later_gather = Gather(near, one_ref, one_set)
        later_gather.start(one_shard)
        later_gather.second()
        later_gather.third()
        later_gather.end()
        later_copy.wait_recv()

        def recompute(k):
            cols = pl.ds(pl.multiple_of(k * w_rows, w_rows), w_rows)
            sent = dot(later[...], one_ref[k].reshape(w_rows, proj), NT)
            g_ref[:, cols] = (g_ref[:, cols].astype(F32) + sent).astype(BF16)

        each(n_chip, recompute, 4)

    ct = cf_ref[...].T.astype(BF16)

    def own(j):
        grad = (g_ref[:, tile_at(j)].astype(F32) * es_ref[j]).astype(BF16)
        msg[j, 0:state] = dot(ct, grad).astype(BF16)

    def swap_copy(slot):
        return remote(
            msg.at[(1 - core) * half + slot], both.at[core, slot],
            core_send.at[slot], core_recv.at[slot], near.sibling(),
        )

    def combine(j):
        both[core, j] = msg[core * half + j]
        pass0 = pass_value(both[0, j, state : state + 16])
        pass1 = pass_value(both[1, j, state : state + 16])
        joined = both[0, j, :state].astype(F32) + pass0 * both[1, j, :state].astype(F32)
        total[j, :state] = joined.astype(BF16)
        total[j, state : state + 16] = pass_rows(pass0 * pass1)

    def send_copy(k):
        return remote(
            total.at[near.chip_slot(k)], got.at[chip], send.at[k], recv.at[chip], near.chip_device(k)
        )

    group = 4

    def own_group(c):
        slots = [near.chip_slot(c * group + i) for i in range(group)]
        for slot in slots:
            own((1 - core) * half + slot)
        for slot in slots:
            swap_copy(slot).start()
        for slot in slots:
            own(core * half + slot)
        for slot in slots:
            swap_copy(slot).wait()
        for slot in slots:
            combine(slot)
        for i in range(group):
            @pl.when(c * group + i < n_chip - 1)
            def _(i=i):
                send_copy(c * group + i).start()

    each(n_chip // group, own_group)
    got[chip] = total[chip]

    xt_copy.wait()

    def x_copy(k, src, from_core):
        cut = pl.ds(pl.multiple_of(near.dp_slot(k) * piece, piece), piece)
        return remote(
            src.at[:, cut], group_ref.at[dp, from_core],
            xg_send.at[from_core, k], xg_recv.at[from_core, k], near.dp_device(k),
        )

    def x_start(k):
        x_copy(k, xt_ref.at[:, core], core).start()
        x_copy(k, x_stage, 1 - core).start()

    each(n_dp - 1, x_start)
    cut = pl.ds(pl.multiple_of(dp * piece, piece), piece)
    group_ref[dp, core] = xt_ref[:, core, cut]
    group_ref[dp, 1 - core] = x_stage[:, cut]

    loads[4].wait()
    scores = dot(cf_ref[...], bf_ref[...], NT, precision=HIGH)
    b_low = bf_ref[...].astype(BF16)
    c_low = cf_ref[...].astype(BF16)

    def before(j):
        cols = tile_at(j)
        x_pair = xs_ref[:, cols]
        x_f = x_pair.astype(F32)
        gate = gate_ref[:, cols].astype(F32)
        sig = jax.nn.sigmoid(gate)
        g = g_ref[:, cols].astype(F32)
        grad_y = g * act_ref[j]
        grad_low = grad_y.astype(BF16)
        zero = jnp.zeros_like(x_pair)
        x0, x1 = jnp.where(first, x_pair, zero), jnp.where(first, zero, x_pair)
        y0, y1 = jnp.where(first, grad_low, zero), jnp.where(first, zero, grad_low)
        log0, log1 = pair_columns(log_ref, j)
        dt0, dt1 = pair_columns(dt_ref, j)
        mask = mask_ref[...]
        decay0 = jnp.exp(log0 - logt_ref[pl.ds(2 * j, 1), :] + mask) * dtt_ref[pl.ds(2 * j, 1), :]
        decay1 = jnp.exp(log1 - logt_ref[pl.ds(2 * j + 1, 1), :] + mask) * dtt_ref[pl.ds(2 * j + 1, 1), :]
        mix0 = (decay0 * scores).astype(BF16)
        mix1 = (decay1 * scores).astype(BF16)
        acc_scores[...] += dot(y0, x_pair, NT) * decay0 + dot(y1, x_pair, NT) * decay1
        log_pair = jnp.where(first, log0, log1)
        entry = jnp.exp(log_pair + first_ref[...])
        s0t = s0t_ref[j]
        y = dot(mix0, x0) + dot(mix1, x1) + entry * dot(c_low, s0t)
        acc_c[...] += dot((entry * grad_y).astype(BF16), s0t, NT)
        inner = dot(mix0, y0, TN) + dot(mix1, y1, TN)
        weights[j] = jnp.exp(log_pair[-1:, :] - log_pair + kept_ref[...]) * jnp.where(first, dt0, dt1)
        x_inner = x_f * inner
        acc_y[...] += heads_of(grad_low.astype(F32) * y - x_inner, j)
        acc_x[...] += heads_of(x_inner, j)
        skip = pltpu.roll(small[16:24, :], lax.rem(LANES - 2 * j, LANES), 1)
        skip = by_half(skip[0:1, 0:1], skip[0:1, 1:2])
        slope = sig * (1.0 + gate * (1.0 - sig))
        gate_grad_ref[:, cols] = (g * (y + skip * x_f) * slope).astype(BF16)
        base[j] = inner + skip * grad_y

    each(half, before, UNROLL)

    def back_copy(k):
        return remote(
            back.at[k], exits.at[chip], back_send.at[k], back_recv.at[chip], {"seg": k * 2 + core}
        )

    def scan(step, carry):
        k = n_chip - 1 - step

        @pl.when(k != chip)
        def _():
            remote(got.at[k], got.at[k], send.at[0], recv.at[k], near.sibling()).wait_recv()

        back[k] = carry.astype(BF16)

        @pl.when(k != chip)
        def _():
            back_copy(k).start()

        return got[k, :state].astype(F32) + pass_value(got[k, state : state + 16]) * carry

    lax.fori_loop(0, n_chip, scan, jnp.zeros((state, LANES), F32))
    exits[chip] = back[chip]
    each(half, lambda j: before(half + j), UNROLL)
    gate_copy = pltpu.make_async_copy(gate_grad_ref, gate_out, out_sems.at[0])
    gate_copy.start()

    def other_copy(j):
        return remote(
            other.at[j], adj_ref.at[core * half + j], other_send.at[j], other_recv.at[j], near.sibling()
        )

    def finish(j):
        @pl.when(j != chip)
        def _():
            remote(back.at[j], exits.at[j], back_send.at[0], back_recv.at[j], near.sibling()).wait_recv()

        after = exits[j].astype(F32)
        pass1 = pass_value(both[1, j, state : state + 16])
        earlier = both[1, j, :state].astype(F32) + pass1 * after
        is_later = core == 1
        adj_ref[core * half + j] = jnp.where(is_later, after, earlier).astype(BF16)
        other[j] = jnp.where(is_later, earlier, after).astype(BF16)
        other_copy(j).start()

    each(n_chip, finish)

    def after_scan(j):
        cols = tile_at(j)
        adj = adj_ref[j]
        weight = weights[j]
        x_f = xs_ref[:, cols].astype(F32)
        outer = weight * dot(b_low, adj)
        acc_b[...] += dot((x_f * weight).astype(BF16), adj, NT)
        acc_s[...] += heads_of(x_f * outer, j)
        last = pass_value(msg[j, state : state + 16])
        passed = last * jnp.sum(adj.astype(F32) * s0t_ref[j].astype(F32), axis=0, keepdims=True)
        select = (iota(1) == 2 * j + (iota(0) >= LANES // 2).astype(jnp.int32)).astype(BF16)
        high, low = split_two(jnp.broadcast_to(passed, (8, LANES)))
        acc_a[...] += dot(high, select) + dot(low, select)
        mixed_grad_ref[:, cols] = (base[j] + outer).astype(BF16)

    each(half, lambda j: after_scan(core * half + j), UNROLL)
    each(half, lambda j: other_copy(j).wait())
    each(half, lambda j: after_scan((1 - core) * half + j), UNROLL)

    u = acc_x[...] + acc_s[...]
    last = jnp.sum(acc_s[...], axis=0, keepdims=True) + acc_a[0:1, :]
    upper = (iota(0) <= iota(1)).astype(F32)
    log_grad = dot(upper, acc_y[...] - acc_s[...], precision=HIGH) + last
    raw_grad = u * rho_ref[...] - small[0:1, :] * log_grad * sig_ref[...]
    b_grad = acc_b[...] + dot(acc_scores[...].T, cf_ref[...], precision=HIGH)
    c_grad = acc_c[...] + dot(acc_scores[...], bf_ref[...], precision=HIGH)
    dproj_ref[:, 0:LANES] = b_grad.astype(BF16)
    dproj_ref[:, LANES : 2 * LANES] = c_grad.astype(BF16)
    dproj_ref[:, 2 * LANES :] = raw_grad.astype(BF16)

    @pl.when(pipe == 1)
    def _():
        later_copy.start()

    def dp_copy(k):
        return remote(dproj_ref, grads.at[core, dp], dp_send.at[k], dp_recv.at[k], near.dp_device(k))

    each(n_dp - 1, lambda k: dp_copy(k).start())
    mixed_copy = pltpu.make_async_copy(mixed_grad_ref, mixed_out, out_sems.at[1])
    mixed_copy.start()
    grads[core, dp] = dproj_ref[...]

    def give(k):
        cols = pl.ds(pl.multiple_of(k * w_rows, w_rows), w_rows)
        sent = dot(dproj_ref[...], own_ref[k].reshape(w_rows, proj), NT)
        input_grad_ref[:, cols] = (g_ref[:, cols].astype(F32) + sent).astype(BF16)

    each(n_chip, give, 4)
    input_copy = pltpu.make_async_copy(input_grad_ref, input_out, out_sems.at[2])
    input_copy.start()

    def x_wait(k):
        x_copy(k, xt_ref.at[:, core], core).wait()
        x_copy(k, x_stage, 1 - core).wait()

    each(n_dp - 1, x_wait)

    def add(c, k):
        whole[...] += dot(group_ref[k, c].reshape(-1, rows), grads[c, k])

    each(n_dp - 1, lambda k: dp_copy(k).wait_recv())
    grad_swap = remote(grads.at[core], grads.at[core], grad_sems.at[0], grad_sems.at[1], near.sibling())
    grad_swap.start()
    each(n_dp, lambda k: add(core, k), 2)
    grad_swap.wait()
    each(n_dp, lambda k: add(1 - core, k), 2)

    def sum_copy(k):
        return remote(
            part.at[near.chip_slot(k)], arrived.at[k], sum_send.at[k], sum_recv.at[k], near.chip_device(k)
        )

    def ship(k):
        slot = near.chip_slot(k)
        part[slot] = whole[pl.ds(pl.multiple_of(slot * piece, piece), piece), :].astype(BF16)
        sum_copy(k).start()

    each(n_chip - 1, ship)
    weight_out[...] = whole[pl.ds(pl.multiple_of(chip * piece, piece), piece), :cols_w]

    @pl.when(pipe == 1)
    def _():
        shard_copy.wait_send()
        later_copy.wait_send()

    each(n_chip - 1, lambda k: send_copy(k).wait_send())

    def sent_back(k):
        @pl.when(k != chip)
        def _():
            back_copy(k).wait_send()

    each(n_chip, sent_back)
    each(n_dp - 1, lambda k: dp_copy(k).wait_send())

    def collect(k):
        sum_copy(k).wait_recv()
        weight_out[...] += arrived[k, :, :cols_w].astype(F32)

    each(n_chip - 1, collect)
    each(n_chip - 1, lambda k: sum_copy(k).wait_send())
    gate_copy.wait()
    mixed_copy.wait()
    input_copy.wait()


def layer_grads(shard, x, mixed, gate, out_grad, s0, rate, bias, skip, docs, n_chip, n_dp):
    rows, width = x.shape
    pairs = width // LANES
    state = s0.shape[1]
    piece, cols = shard.shape
    proj = cols + -cols % LANES
    dma = pltpu.SemaphoreType.DMA
    line = jax.ShapeDtypeStruct((rows, width), BF16)
    whole_line = pltpu.VMEM((rows, width), BF16)
    square = pltpu.VMEM((rows, LANES), F32)
    full_w = pltpu.VMEM((n_chip, 2, n_dp, piece, proj), BF16)
    wide = pltpu.VMEM((pairs, rows, LANES), F32)
    message = pltpu.VMEM((n_chip, state + 16, LANES), BF16)
    plain = pltpu.VMEM((n_chip, state, LANES), BF16)
    anywhere = pl.BlockSpec(memory_space=pl.ANY)
    chips, dps = dma((n_chip,)), dma((n_dp - 1,))
    return pl.pallas_call(
        functools.partial(layer_kernel, n_chip, n_dp),
        out_shape=(line, line, line, jax.ShapeDtypeStruct((piece, cols), F32)),
        in_specs=[VMEM] + [anywhere] * 5 + [VMEM] * 3 + [SMEM],
        out_specs=(anywhere, anywhere, anywhere, VMEM),
        scratch_shapes=[
            whole_line, whole_line, whole_line, whole_line,
            pltpu.VMEM((width, state), F32),
            pltpu.VMEM((piece, proj), BF16),
            full_w,
            pltpu.VMEM((piece, proj), BF16),
            full_w,
            pltpu.VMEM((rows, proj), BF16),
            pltpu.VMEM((pairs, state, LANES), BF16),
            pltpu.VMEM((n_chip, 2, LANES, rows), BF16),
            pltpu.VMEM((n_chip, LANES, rows), BF16),
            pltpu.VMEM((n_dp, 2, n_chip, piece, rows), BF16),
            wide, wide, wide,
            pltpu.VMEM((rows, proj), F32),
        ]
        + [square] * 11
        + [
            pltpu.VMEM((24, LANES), F32),
            pltpu.VMEM((pairs, state + 16, LANES), BF16),
            pltpu.VMEM((2, n_chip, state + 16, LANES), BF16),
            message, message, plain, plain, plain,
            pltpu.VMEM((pairs, state, LANES), BF16),
            wide,
            pltpu.VMEM((rows, proj), BF16),
            whole_line, whole_line, whole_line,
        ]
        + [square] * 6
        + [
            pltpu.VMEM((8, LANES), F32),
            pltpu.VMEM((2, n_dp, rows, proj), BF16),
            pltpu.VMEM((n_chip, piece, proj), BF16),
            pltpu.VMEM((n_chip * piece, proj), F32),
            pltpu.VMEM((n_chip - 1, piece, proj), BF16),
            (
                dma((5,)), dma((3,)), gather_sems(n_chip, n_dp), gather_sems(n_chip, n_dp), dma((2,)), dma((2,)),
                chips, chips, chips, chips, chips, chips, chips, chips, dma((2,)),
                dma((2, n_dp - 1)), dma((2, n_dp - 1)), dps, dps, dma((2,)), chips, chips,
            ),
        ],
        compiler_params=pltpu.CompilerParams(
            collective_id=1, has_side_effects=True, vmem_limit_bytes=VMEM_BYTES
        ),
    )(shard, x, mixed, gate, out_grad, s0, rate, bias, skip, docs)


def deliver_kernel(*refs):
    count = len(refs) // 2
    for i in range(count):
        refs[count + i][...] = refs[i][...]


def deliver(values):
    steps = 4
    specs = [
        pl.BlockSpec((value.shape[0] // steps, value.shape[1]), lambda i: (i, 0)) for value in values
    ]
    return pl.pallas_call(
        deliver_kernel,
        grid=(steps,),
        out_shape=tuple(jax.ShapeDtypeStruct(value.shape, value.dtype) for value in values),
        in_specs=specs,
        out_specs=tuple(specs),
    )(*values)


def local(
    inputs, mixed, gate_in, entry_states, out_grad, doc_lengths, proj_weight, decay_rate, dt_bias, skip_gain
):
    n_chip = lax.axis_size("seg") // 2
    n_dp = lax.axis_size("dp")
    width = inputs.shape[-1]
    s0 = entry_states.reshape(width, entry_states.shape[-1])
    outs = layer_grads(
        proj_weight[0], inputs[0, 0], mixed[0, 0], gate_in[0, 0], out_grad[0], s0,
        decay_rate, dt_bias, skip_gain, doc_lengths, n_chip, n_dp,
    )
    input_grad, mixed_grad, gate_grad, weight_grad = deliver(outs)
    return (
        input_grad[None, None],
        mixed_grad[None, None],
        gate_grad[None, None],
        weight_grad[None],
    )


def solution(mesh):
    in_specs = (
        P("pipe", "dp", "seg", None),
        P("pipe", "dp", "seg", None),
        P("pipe", "dp", "seg", None),
        P("pipe", "dp", "seg", None, None, None),
        P("dp", "seg", None),
        P("dp", None),
        P("pipe", ("seg", "dp"), None),
        P("pipe", None),
        P("pipe", None),
        P("pipe", None),
    )
    out_specs = (
        P("pipe", "dp", "seg", None),
        P("pipe", "dp", "seg", None),
        P("pipe", "dp", "seg", None),
        P("pipe", ("seg", "dp"), None),
    )
    return jax.shard_map(local, mesh=mesh, in_specs=in_specs, out_specs=out_specs, check_vma=False)
```

```python
import functools

import jax
import jax.numpy as jnp
from jax import lax
from jax.experimental import pallas as pl
from jax.experimental.pallas import tpu as pltpu
from jax.sharding import PartitionSpec as P

MESH = pl.DeviceIdType.MESH
F32 = jnp.float32
BF16 = jnp.bfloat16
HIGH = lax.Precision.HIGHEST
LANES = 128
NEG = -1e30
UNROLL = 4
VMEM_BYTES = 56 * 1024 * 1024
VMEM = pl.BlockSpec(memory_space=pltpu.VMEM)
SMEM = pl.BlockSpec(memory_space=pltpu.SMEM)
NN = (((1,), (0,)), ((), ()))
NT = (((1,), (1,)), ((), ()))
TN = (((0,), (0,)), ((), ()))


def dot(a, b, dims=NN, precision=None):
    return lax.dot_general(a, b, dims, precision=precision, preferred_element_type=F32)


def iota(axis, shape=(LANES, LANES)):
    return lax.broadcasted_iota(jnp.int32, shape, axis)


def tile_at(j):
    return pl.ds(pl.multiple_of(j * LANES, LANES), LANES)


def split_two(value):
    high = value.astype(BF16)
    low = (value - high.astype(F32)).astype(BF16)
    return high, low


def place():
    seg = lax.axis_index("seg")
    chip = seg // 2
    core = seg - 2 * chip
    return lax.axis_index("pipe"), seg, chip, core, lax.axis_index("dp")


def greet(devices):
    barrier = pltpu.get_barrier_semaphore()
    for count, device_of in devices:
        def one(k, carry, device_of=device_of):
            pl.semaphore_signal(barrier, inc=1, device_id=device_of(k), device_id_type=MESH)
            return carry

        lax.fori_loop(0, count, one, 0)
    pl.semaphore_wait(barrier, sum(count for count, _ in devices))


def remote(src, dst, send_sem, recv_sem, device):
    return pltpu.make_async_remote_copy(
        src_ref=src, dst_ref=dst, send_sem=send_sem, recv_sem=recv_sem,
        device_id=device, device_id_type=MESH,
    )


def each(count, body, unroll=1):
    def step(k, carry):
        body(k)
        return carry

    lax.fori_loop(0, count, step, 0, unroll=unroll)


class Around:
    def __init__(self, n_chip, n_dp):
        self.n_chip, self.n_dp = n_chip, n_dp
        self.pipe, self.seg, self.chip, self.core, self.dp = place()

    def chip_slot(self, k):
        return lax.rem(self.chip + 1 + k, self.n_chip)

    def chip_device(self, k):
        return {"seg": self.chip_slot(k) * 2 + self.core}

    def dp_slot(self, k):
        return lax.rem(self.dp + 1 + k, self.n_dp)

    def dp_device(self, k):
        return {"dp": self.dp_slot(k)}

    def sibling(self, k=0):
        return {"seg": self.seg + 1 - 2 * self.core}

    def partner(self, k=0):
        return {"pipe": 1 - self.pipe}

    def greet(self, with_pipe):
        met = [(self.n_chip - 1, self.chip_device), (self.n_dp - 1, self.dp_device), (1, self.sibling)]
        greet(met + ([(1, self.partner)] if with_pipe else []))


class Gather:
    def __init__(self, near, dst, sems):
        self.near, self.dst = near, dst
        self.chip_send, self.chip_recv, self.dp_send, self.dp_recv, self.core_send, self.core_recv = sems

    def source(self, k):
        near = self.near
        return lax.rem(near.chip + 2 * near.n_chip - 1 - k, near.n_chip)

    def chip_copy(self, k):
        near = self.near
        block = self.dst.at[near.chip, near.core, near.dp]
        return remote(block, block, self.chip_send.at[k], self.chip_recv.at[k], near.chip_device(k))

    def dp_copy(self, k, i):
        near = self.near
        block = self.dst.at[self.source(k), near.core, near.dp]
        return remote(block, block, self.dp_send.at[k, i], self.dp_recv.at[k, i], near.dp_device(i))

    def core_copy(self, k):
        block = self.dst.at[self.source(k), self.near.core]
        return remote(block, block, self.core_send.at[k], self.core_recv.at[k], self.near.sibling())

    def start(self, src):
        near = self.near
        self.dst[near.chip, near.core, near.dp] = src[...]
        each(near.n_chip - 1, lambda k: self.chip_copy(k).start())
        each(near.n_dp - 1, lambda i: self.dp_copy(near.n_chip - 1, i).start())

    def spread(self):
        near = self.near

        def pass_on(k):
            self.chip_copy(k).wait_recv()
            for i in range(near.n_dp - 1):
                self.dp_copy(k, i).start()

        each(near.n_chip - 1, pass_on)

    def over(self, use):
        near = self.near

        def pass_on(step):
            k = lax.rem(step + near.n_chip - 1, near.n_chip)
            for i in range(near.n_dp - 1):
                self.dp_copy(k, i).wait_recv()
            self.core_copy(k).start()
            use(self.source(k), near.core)

        each(near.n_chip, pass_on)

    def end(self, use):
        near = self.near

        def take(step):
            k = lax.rem(step + near.n_chip - 1, near.n_chip)
            self.core_copy(k).wait()
            use(self.source(k), 1 - near.core)

        each(near.n_chip, take)

    def sent(self):
        near = self.near
        each(near.n_chip - 1, lambda k: self.chip_copy(k).wait_send())

        def one(k):
            for i in range(near.n_dp - 1):
                self.dp_copy(k, i).wait_send()

        each(near.n_chip, one)


def gather_sems(n_chip, n_dp):
    dma = pltpu.SemaphoreType.DMA
    return (
        dma((n_chip - 1,)), dma((n_chip - 1,)), dma((n_chip, n_dp - 1)), dma((n_chip, n_dp - 1)),
        dma((n_chip,)), dma((n_chip,)),
    )


def packed(value):
    piece = value.shape[0]
    tail = value[:, 2 * LANES :]
    top, low = tail[: piece // 2], tail[piece // 2 :]
    beside = top + pltpu.roll(low, LANES // 2, 1)
    return jnp.concatenate([value[:, :LANES], value[:, LANES : 2 * LANES], beside], axis=0)


def unpacked(value, piece):
    beside = value[2 * piece :]
    first = iota(1, (1, LANES)) < LANES // 2
    top = jnp.where(first, beside, 0.0)
    low = jnp.where(first, pltpu.roll(beside, LANES // 2, 1), 0.0)
    return value[:piece], value[piece : 2 * piece], jnp.concatenate([top, low], axis=0)


def weight_tiles(ref, chip, core, piece):
    block = ref[chip, core]
    tail = block[:, 2 * piece :]
    return (
        block[:, :piece].reshape(-1, LANES),
        block[:, piece : 2 * piece].reshape(-1, LANES),
        jnp.concatenate([tail, tail], axis=1).reshape(-1, LANES),
    )


def in_top(piece):
    lane = iota(1, (1, LANES))
    return lane - lane // piece * piece < piece // 2


def back_projected(dproj_ref, dt_low, ref, chip, core, piece):
    w_b, w_c, w_t = weight_tiles(ref, chip, core, piece)
    plain = dot(dproj_ref[:, :LANES], w_b, NT) + dot(dproj_ref[:, LANES : 2 * LANES], w_c, NT)
    top = dot(dproj_ref[:, 2 * LANES :], w_t, NT)
    low = dot(dt_low, w_t, NT)
    return plain + jnp.where(in_top(piece), top, low)


def lanes_turned(value):
    return pltpu.roll(value.astype(F32), LANES // 2, 1).astype(BF16)


def pair_columns(ref, j):
    turned = pltpu.roll(ref[...], lax.rem(LANES - 2 * j, LANES), 1)
    shape = (turned.shape[0], LANES)
    return jnp.broadcast_to(turned[:, 0:1], shape), jnp.broadcast_to(turned[:, 1:2], shape)


def by_half(first, second):
    return jnp.where(iota(1, (1, LANES)) < LANES // 2, first, second)


def heads_of(value, j):
    select = (iota(1) == 2 * j + (iota(0) >= LANES // 2).astype(jnp.int32)).astype(BF16)
    high, low = split_two(value)
    return dot(high, select) + dot(low, select)


def layer_kernel(n_chip, n_dp, *refs):
    (
        shard_ref, x_hbm, mixed_hbm, gate_hbm, out_grad_hbm, s0_hbm, rate_ref, bias_ref, skip_ref, doc_ref,
        input_out, mixed_out, gate_out, weight_out,
        x_ref, xs_ref, gate_ref, g_ref, s0_ref, shard, own_ref, one_shard, one_ref, later,
        s0t_ref, xt_ref, x_stage, group_ref, act_ref, weights, projected, bf_ref, cf_ref,
        log_ref, logt_ref, dt_ref, dtt_ref, sig_ref, rho_ref, mask_ref, first_ref, kept_ref, small,
        msg, both, total, got, back, exits, other, adj_ref, base, dproj_ref, passes, chip_passes,
        input_grad_ref, mixed_grad_ref, gate_grad_ref,
        acc_scores, acc_b, acc_c, acc_y, acc_x, acc_s, acc_a, grads, part, whole, arrived, spare, summed, sems,
    ) = refs
    (
        in_sems, out_sems, own_set, one_set, shard_sems, later_sems, pass_sems, pass_send, pass_recv, core_send, core_recv, send, recv,
        back_send, back_recv, other_send, other_recv, xt_sems, xg_send, xg_recv,
        dp_send, dp_recv, grad_send, grad_recv, sum_send, sum_recv,
    ) = sems
    rows, width = x_ref.shape
    state = bf_ref.shape[1]
    heads = rate_ref.shape[1]
    cols_w = shard_ref.shape[1]
    piece = shard_ref.shape[0]
    proj = projected.shape[1]
    half = n_chip

    loads = [
        pltpu.make_async_copy(src, dst, in_sems.at[i])
        for i, (src, dst) in enumerate(
            ((gate_hbm, gate_ref), (s0_hbm, s0_ref), (x_hbm, x_ref), (out_grad_hbm, g_ref), (mixed_hbm, xs_ref))
        )
    ]
    for load in loads:
        load.start()
    spare[...] = jnp.zeros_like(spare)
    spare[:, :cols_w] = shard_ref[...].astype(F32)
    shard[...] = packed(spare[...]).astype(BF16)

    near = Around(n_chip, n_dp)
    near.greet(True)
    pipe, chip, core, dp = near.pipe, near.chip, near.core, near.dp
    shard_copy = remote(shard, one_shard, shard_sems.at[0], shard_sems.at[1], near.partner())
    later_copy = remote(dproj_ref, later, later_sems.at[0], later_sems.at[1], near.partner())

    gather = Gather(near, own_ref, own_set)
    gather.start(shard)

    @pl.when(pipe == 1)
    def _():
        shard_copy.start()

    for ref in (acc_scores, acc_b, acc_c, acc_y, acc_x, acc_s, acc_a, small, projected, whole):
        ref[...] = jnp.zeros_like(ref)
    small[0:1, :heads] = rate_ref[...]
    small[8:9, :heads] = bias_ref[...]
    small[16:17, :heads] = skip_ref[...]
    begin = near.seg * rows
    count_t = jnp.zeros((rows, rows), jnp.int32)
    count_s = jnp.zeros((rows, rows), jnp.int32)
    count_last = jnp.zeros((rows, rows), jnp.int32)
    start = jnp.int32(0)
    for k in range(doc_ref.shape[1] - 1):
        start = start + doc_ref[0, k]
        offset = jnp.broadcast_to(start - begin, (rows, rows))
        inside = offset >= 0
        count_t += (inside & (iota(0) >= offset)).astype(jnp.int32)
        count_s += (inside & (iota(1) >= offset)).astype(jnp.int32)
        count_last += (inside & (offset <= rows - 1)).astype(jnp.int32)
    allowed = (iota(0) >= iota(1)) & (count_t == count_s)
    mask_ref[...] = jnp.where(allowed, 0.0, NEG)
    first_ref[...] = jnp.where(count_t == 0, 0.0, NEG)
    kept_ref[...] = jnp.where(count_t == count_last, 0.0, NEG)

    def activate(j):
        gate = gate_ref[:, tile_at(j)].astype(F32)
        act_ref[j] = gate * jax.nn.sigmoid(gate)

    def turn_state(j):
        s0t_ref[j] = s0_ref[tile_at(j), :].T.astype(BF16)

    def turn_x(k):
        for c in range(2):
            xt_ref[k, c] = x_ref[:, tile_at(2 * k + c)].T

    gather.spread()
    loads[0].wait()
    each(2 * half, activate, UNROLL)
    loads[1].wait()
    each(2 * half, turn_state, UNROLL)
    loads[2].wait()
    each(n_chip, turn_x, 2)

    def project(k, c):
        x_tile = x_ref[:, tile_at(2 * k + c)]
        zero = jnp.zeros_like(x_tile)
        w_b, w_c, w_t = weight_tiles(own_ref, k, c, piece)
        projected[:, :LANES] += dot(x_tile, w_b)
        projected[:, LANES : 2 * LANES] += dot(x_tile, w_c)
        projected[:, 2 * LANES : 3 * LANES] += dot(jnp.where(in_top(piece), x_tile, zero), w_t)
        projected[:, 3 * LANES :] += dot(jnp.where(in_top(piece), zero, x_tile), w_t)

    gather.over(project)
    gather.end(project)
    xt_copy = remote(xt_ref.at[:, 1 - core], x_stage, xt_sems.at[0], xt_sems.at[1], near.sibling())
    xt_copy.start()
    bf_ref[...] = projected[:, :state]
    cf_ref[...] = projected[:, state : 2 * state]
    raw = projected[:, 2 * LANES : 3 * LANES] + pltpu.roll(projected[:, 3 * LANES :], LANES // 2, 1)
    raw = jnp.where(iota(1) < heads, raw, 0.0) + small[8:9, :]
    soft = jnp.maximum(raw, 0.0) + jnp.log1p(jnp.exp(-jnp.abs(raw)))
    sig = 1.0 / (1.0 + jnp.exp(-jnp.abs(raw)))
    sig = jnp.where(raw >= 0, sig, 1.0 - sig)
    tiny = raw < -15.0
    exp_raw = jnp.exp(jnp.minimum(raw, 0.0))
    sig = jnp.where(tiny, exp_raw, sig)
    soft = jnp.where(tiny, exp_raw, soft)
    sig_ref[...] = sig
    rho_ref[...] = jnp.where(tiny, 1.0, sig / jnp.where(tiny, 1.0, soft))
    lower = (iota(0) >= iota(1)).astype(F32)
    log = dot(lower, -soft * small[0:1, :], precision=HIGH)
    log_ref[...] = log
    logt_ref[...] = log.T
    dt_ref[...] = soft
    dtt_ref[...] = soft.T
    first = iota(1, (1, LANES)) < LANES // 2

    passes[core] = jnp.broadcast_to(jnp.exp(log[rows - 1 :] + first_ref[rows - 1 :, :]), (8, LANES))
    pass_copy = remote(passes.at[core], passes.at[core], pass_sems.at[0], pass_sems.at[1], near.sibling())
    pass_copy.start()

    def pass_row(value, j):
        turned = pltpu.roll(value, lax.rem(LANES - 2 * j, LANES), 1)
        return by_half(turned[0:1, 0:1], turned[0:1, 1:2])

    loads[3].wait()
    pass_copy.wait()
    chip_passes[chip] = passes[0] * passes[1]

    def chip_pass_copy(k):
        block = chip_passes.at[chip]
        return remote(block, block, pass_send.at[k], pass_recv.at[k], near.chip_device(k))

    each(n_chip - 1, lambda k: chip_pass_copy(k).start())

    @pl.when(pipe == 0)
    def _():
        shard_copy.wait_recv()
        later_gather = Gather(near, one_ref, one_set)
        later_gather.start(one_shard)
        later_gather.spread()
        later_gather.over(lambda k, c: None)
        later_gather.end(lambda k, c: None)
        later_gather.sent()
        later_copy.wait_recv()
        dt_low = lanes_turned(later[:, 2 * LANES :])

        def recompute(k):
            for c in range(2):
                cols = tile_at(2 * k + c)
                sent = back_projected(later, dt_low, one_ref, k, c, piece)
                g_ref[:, cols] = (g_ref[:, cols].astype(F32) + sent).astype(BF16)

        each(n_chip, recompute, 2)

    ct = cf_ref[...].T.astype(BF16)

    def own(j):
        log0, log1 = pair_columns(log_ref, j)
        entry = jnp.exp(jnp.where(first, log0, log1) + first_ref[...])
        grad = (g_ref[:, tile_at(j)].astype(F32) * act_ref[j] * entry).astype(BF16)
        msg[j] = dot(ct, grad).astype(BF16)

    def swap_copy(slot):
        return remote(
            msg.at[(1 - core) * half + slot], both.at[core, slot],
            core_send.at[slot], core_recv.at[slot], near.sibling(),
        )

    def combine(j):
        both[core, j] = msg[core * half + j]
        pass0 = pass_row(passes[0], core * half + j)
        total[j] = (both[0, j].astype(F32) + pass0 * both[1, j].astype(F32)).astype(BF16)

    def send_copy(k):
        return remote(
            total.at[near.chip_slot(k)], got.at[chip], send.at[k], recv.at[chip], near.chip_device(k)
        )

    group = 4

    def own_group(c):
        slots = [near.chip_slot(c * group + i) for i in range(group)]
        for slot in slots:
            own((1 - core) * half + slot)
        for slot in slots:
            swap_copy(slot).start()
        for slot in slots:
            own(core * half + slot)
        for slot in slots:
            swap_copy(slot).wait()
        for slot in slots:
            combine(slot)
        for i in range(group):
            @pl.when(c * group + i < n_chip - 1)
            def _(i=i):
                send_copy(c * group + i).start()

    each(n_chip // group, own_group)
    got[chip] = total[chip]

    xt_copy.wait()

    def x_copy(k, src, from_core):
        cut = pl.ds(pl.multiple_of(near.dp_slot(k) * piece, piece), piece)
        return remote(
            src.at[:, cut], group_ref.at[dp, from_core],
            xg_send.at[from_core, k], xg_recv.at[from_core, k], near.dp_device(k),
        )

    def x_start(k):
        x_copy(k, xt_ref.at[:, core], core).start()
        x_copy(k, x_stage, 1 - core).start()

    each(n_dp - 1, x_start)
    cut = pl.ds(pl.multiple_of(dp * piece, piece), piece)
    group_ref[dp, core] = xt_ref[:, core, cut]
    group_ref[dp, 1 - core] = x_stage[:, cut]

    loads[4].wait()
    scores = dot(cf_ref[...], bf_ref[...], NT, precision=HIGH)
    b_low = bf_ref[...].astype(BF16)
    c_low = cf_ref[...].astype(BF16)

    def before(j):
        cols = tile_at(j)
        x_pair = xs_ref[:, cols]
        x_f = x_pair.astype(F32)
        gate = gate_ref[:, cols].astype(F32)
        sig = jax.nn.sigmoid(gate)
        g = g_ref[:, cols].astype(F32)
        grad_y = g * act_ref[j]
        grad_low = grad_y.astype(BF16)
        zero = jnp.zeros_like(x_pair)
        x0, x1 = jnp.where(first, x_pair, zero), jnp.where(first, zero, x_pair)
        y0, y1 = jnp.where(first, grad_low, zero), jnp.where(first, zero, grad_low)
        log0, log1 = pair_columns(log_ref, j)
        dt0, dt1 = pair_columns(dt_ref, j)
        mask = mask_ref[...]
        decay0 = jnp.exp(log0 - logt_ref[pl.ds(2 * j, 1), :] + mask) * dtt_ref[pl.ds(2 * j, 1), :]
        decay1 = jnp.exp(log1 - logt_ref[pl.ds(2 * j + 1, 1), :] + mask) * dtt_ref[pl.ds(2 * j + 1, 1), :]
        mix0 = (decay0 * scores).astype(BF16)
        mix1 = (decay1 * scores).astype(BF16)
        acc_scores[...] += dot(y0, x_pair, NT) * decay0 + dot(y1, x_pair, NT) * decay1
        log_pair = jnp.where(first, log0, log1)
        entry = jnp.exp(log_pair + first_ref[...])
        s0t = s0t_ref[j]
        y = dot(mix0, x0) + dot(mix1, x1) + entry * dot(c_low, s0t)
        acc_c[...] += dot((entry * grad_y).astype(BF16), s0t, NT)
        inner = dot(mix0, y0, TN) + dot(mix1, y1, TN)
        weights[j] = jnp.exp(log_pair[-1:, :] - log_pair + kept_ref[...]) * jnp.where(first, dt0, dt1)
        x_inner = x_f * inner
        acc_y[...] += heads_of(grad_low.astype(F32) * y - x_inner, j)
        acc_x[...] += heads_of(x_inner, j)
        skip = pltpu.roll(small[16:24, :], lax.rem(LANES - 2 * j, LANES), 1)
        skip = by_half(skip[0:1, 0:1], skip[0:1, 1:2])
        slope = sig * (1.0 + gate * (1.0 - sig))
        gate_grad_ref[:, cols] = (g * (y + skip * x_f) * slope).astype(BF16)
        base[j] = inner + skip * grad_y

    each(half, before, UNROLL)

    each(n_chip - 1, lambda k: chip_pass_copy(k).wait_recv())

    def back_copy(k):
        return remote(
            back.at[k], exits.at[chip], back_send.at[k], back_recv.at[chip], {"seg": k * 2 + core}
        )

    def scan(step, carry):
        k = n_chip - 1 - step

        @pl.when(k != chip)
        def _():
            remote(got.at[k], got.at[k], send.at[0], recv.at[k], near.sibling()).wait_recv()

        back[k] = carry.astype(BF16)

        @pl.when(k != chip)
        def _():
            back_copy(k).start()

        return got[k].astype(F32) + pass_row(chip_passes[k], core * half + chip) * carry

    lax.fori_loop(0, n_chip, scan, jnp.zeros((state, LANES), F32))
    exits[chip] = back[chip]
    each(half, lambda j: before(half + j), UNROLL)
    gate_copy = pltpu.make_async_copy(gate_grad_ref, gate_out, out_sems.at[0])
    gate_copy.start()

    def other_copy(j):
        return remote(
            other.at[j], adj_ref.at[core * half + j], other_send.at[j], other_recv.at[j], near.sibling()
        )

    def finish(j):
        @pl.when(j != chip)
        def _():
            remote(back.at[j], exits.at[j], back_send.at[0], back_recv.at[j], near.sibling()).wait_recv()

        after = exits[j].astype(F32)
        earlier = both[1, j].astype(F32) + pass_row(passes[1], core * half + j) * after
        is_later = core == 1
        adj_ref[core * half + j] = jnp.where(is_later, after, earlier).astype(BF16)
        other[j] = jnp.where(is_later, earlier, after).astype(BF16)
        other_copy(j).start()

    def near_first(i):
        x_off = i - i // 2 * 2
        m = i // 2
        odd = m - m // 2 * 2
        z_off = odd * ((m + 1) // 2) - (1 - odd) * (m // 2)
        ring = n_chip // 2
        my_x = chip // ring
        z = lax.rem(chip - my_x * ring + z_off + ring, ring)
        return lax.rem(my_x + x_off, 2) * ring + z

    def after_scan(j):
        cols = tile_at(j)
        adj = adj_ref[j]
        weight = weights[j]
        x_f = xs_ref[:, cols].astype(F32)
        outer = weight * dot(b_low, adj)
        acc_b[...] += dot((x_f * weight).astype(BF16), adj, NT)
        acc_s[...] += heads_of(x_f * outer, j)
        last = pass_row(passes[core], j)
        passed = last * jnp.sum(adj.astype(F32) * s0t_ref[j].astype(F32), axis=0, keepdims=True)
        select = (iota(1) == 2 * j + (iota(0) >= LANES // 2).astype(jnp.int32)).astype(BF16)
        high, low = split_two(jnp.broadcast_to(passed, (8, LANES)))
        acc_a[...] += dot(high, select) + dot(low, select)
        mixed_grad_ref[:, cols] = (base[j] + outer).astype(BF16)

    def mine_group(c):
        slots = [near_first(c * group + i) for i in range(group)]
        for slot in slots:
            finish(slot)
        for slot in slots:
            after_scan(core * half + slot)

    def other_group(c):
        slots = [near_first(c * group + i) for i in range(group)]
        for slot in slots:
            other_copy(slot).wait()
        for slot in slots:
            after_scan((1 - core) * half + slot)

    each(n_chip // group, mine_group)
    each(n_chip // group, other_group)

    u = acc_x[...] + acc_s[...]
    last = jnp.sum(acc_s[...], axis=0, keepdims=True) + acc_a[0:1, :]
    upper = (iota(0) <= iota(1)).astype(F32)
    log_grad = dot(upper, acc_y[...] - acc_s[...], precision=HIGH) + last
    raw_grad = u * rho_ref[...] - small[0:1, :] * log_grad * sig_ref[...]
    b_grad = acc_b[...] + dot(acc_scores[...].T, cf_ref[...], precision=HIGH)
    c_grad = acc_c[...] + dot(acc_scores[...], bf_ref[...], precision=HIGH)
    dproj_ref[:, 0:LANES] = b_grad.astype(BF16)
    dproj_ref[:, LANES : 2 * LANES] = c_grad.astype(BF16)
    dproj_ref[:, 2 * LANES :] = raw_grad.astype(BF16)

    @pl.when(pipe == 1)
    def _():
        later_copy.start()

    def dp_copy(k):
        return remote(dproj_ref, grads.at[core, dp], dp_send.at[k], dp_recv.at[k], near.dp_device(k))

    each(n_dp - 1, lambda k: dp_copy(k).start())

    def grad_swap(i, slot):
        block = grads.at[core, slot]
        return remote(block, block, grad_send.at[i], grad_recv.at[i], near.sibling())

    grads[core, dp] = dproj_ref[...]
    grad_swap(n_dp - 1, dp).start()
    mixed_copy = pltpu.make_async_copy(mixed_grad_ref, mixed_out, out_sems.at[1])
    mixed_copy.start()
    dt_low = lanes_turned(dproj_ref[:, 2 * LANES :])

    def give(k):
        for c in range(2):
            cols = tile_at(2 * k + c)
            sent = back_projected(dproj_ref, dt_low, own_ref, k, c, piece)
            input_grad_ref[:, cols] = (g_ref[:, cols].astype(F32) + sent).astype(BF16)

    each(n_chip, give, 2)
    input_copy = pltpu.make_async_copy(input_grad_ref, input_out, out_sems.at[2])
    input_copy.start()

    def x_wait(k):
        x_copy(k, xt_ref.at[:, core], core).wait()
        x_copy(k, x_stage, 1 - core).wait()

    each(n_dp - 1, x_wait)

    def add(c, k):
        whole[...] += dot(group_ref[k, c].reshape(-1, rows), grads[c, k])

    def grad_slot(i):
        return lax.rem(dp + 2 * n_dp - 1 - i, n_dp)

    for i in range(n_dp - 1):
        dp_copy(i).wait_recv()
        grad_swap(i, grad_slot(i)).start()
    each(n_dp, lambda i: add(core, i), 2)
    for i in range(n_dp):
        grad_swap(i, grad_slot(i)).wait()
    each(n_dp, lambda i: add(1 - core, i), 2)

    def sum_copy(k):
        return remote(
            part.at[near.chip_slot(k)], arrived.at[k], sum_send.at[k], sum_recv.at[k], near.chip_device(k)
        )

    def ship(k):
        slot = near.chip_slot(k)
        part[slot] = packed(whole[pl.ds(pl.multiple_of(slot * piece, piece), piece), :]).astype(BF16)
        sum_copy(k).start()

    each(n_chip - 1, ship)
    summed[...] = packed(whole[pl.ds(pl.multiple_of(chip * piece, piece), piece), :])

    @pl.when(pipe == 1)
    def _():
        shard_copy.wait_send()
        later_copy.wait_send()

    gather.sent()
    each(n_chip - 1, lambda k: chip_pass_copy(k).wait_send())
    each(n_chip - 1, lambda k: send_copy(k).wait_send())

    def sent_back(k):
        @pl.when(k != chip)
        def _():
            back_copy(k).wait_send()

    each(n_chip, sent_back)
    each(n_dp - 1, lambda k: dp_copy(k).wait_send())

    def collect(k):
        sum_copy(k).wait_recv()
        summed[...] += arrived[k].astype(F32)

    each(n_chip - 1, collect)
    out_b, out_c, out_t = unpacked(summed[...], piece)
    weight_out[:, :LANES] = out_b
    weight_out[:, LANES : 2 * LANES] = out_c
    weight_out[:, 2 * LANES :] = out_t[:, : cols_w - 2 * LANES]
    each(n_chip - 1, lambda k: sum_copy(k).wait_send())
    gate_copy.wait()
    mixed_copy.wait()
    input_copy.wait()


def layer_grads(shard, x, mixed, gate, out_grad, s0, rate, bias, skip, docs, n_chip, n_dp):
    rows, width = x.shape
    pairs = width // LANES
    state = s0.shape[1]
    piece, cols = shard.shape
    proj = cols + -cols % LANES
    dma = pltpu.SemaphoreType.DMA
    line = jax.ShapeDtypeStruct((rows, width), BF16)
    whole_line = pltpu.VMEM((rows, width), BF16)
    square = pltpu.VMEM((rows, LANES), F32)
    packed_rows = 2 * piece + piece // 2
    full_w = pltpu.VMEM((n_chip, 2, n_dp, packed_rows, LANES), BF16)
    wide = pltpu.VMEM((pairs, rows, LANES), F32)
    plain = pltpu.VMEM((n_chip, state, LANES), BF16)
    anywhere = pl.BlockSpec(memory_space=pl.ANY)
    chips, dps = dma((n_chip,)), dma((n_dp - 1,))
    return pl.pallas_call(
        functools.partial(layer_kernel, n_chip, n_dp),
        out_shape=(line, line, line, jax.ShapeDtypeStruct((piece, cols), F32)),
        in_specs=[VMEM] + [anywhere] * 5 + [VMEM] * 3 + [SMEM],
        out_specs=(anywhere, anywhere, anywhere, VMEM),
        scratch_shapes=[
            whole_line, whole_line, whole_line, whole_line,
            pltpu.VMEM((width, state), F32),
            pltpu.VMEM((packed_rows, LANES), BF16),
            full_w,
            pltpu.VMEM((packed_rows, LANES), BF16),
            full_w,
            pltpu.VMEM((rows, proj), BF16),
            pltpu.VMEM((pairs, state, LANES), BF16),
            pltpu.VMEM((n_chip, 2, LANES, rows), BF16),
            pltpu.VMEM((n_chip, LANES, rows), BF16),
            pltpu.VMEM((n_dp, 2, n_chip, piece, rows), BF16),
            wide, wide,
            pltpu.VMEM((rows, proj + LANES), F32),
        ]
        + [square] * 11
        + [
            pltpu.VMEM((24, LANES), F32),
            pltpu.VMEM((pairs, state, LANES), BF16),
            pltpu.VMEM((2, n_chip, state, LANES), BF16),
            plain, plain, plain, plain, plain,
            pltpu.VMEM((pairs, state, LANES), BF16),
            wide,
            pltpu.VMEM((rows, proj), BF16),
            pltpu.VMEM((2, 8, LANES), F32),
            pltpu.VMEM((n_chip, 8, LANES), F32),
            whole_line, whole_line, whole_line,
        ]
        + [square] * 6
        + [
            pltpu.VMEM((8, LANES), F32),
            pltpu.VMEM((2, n_dp, rows, proj), BF16),
            pltpu.VMEM((n_chip, packed_rows, LANES), BF16),
            pltpu.VMEM((n_chip * piece, proj), F32),
            pltpu.VMEM((n_chip - 1, packed_rows, LANES), BF16),
            pltpu.VMEM((piece, proj), F32),
            pltpu.VMEM((packed_rows, LANES), F32),
            (
                dma((5,)), dma((3,)), gather_sems(n_chip, n_dp), gather_sems(n_chip, n_dp), dma((2,)), dma((2,)),
                dma((2,)), chips, chips, chips, chips, chips, chips, chips, chips, chips, chips, dma((2,)),
                dma((2, n_dp - 1)), dma((2, n_dp - 1)), dps, dps, dma((n_dp,)), dma((n_dp,)), chips, chips,
            ),
        ],
        compiler_params=pltpu.CompilerParams(
            collective_id=1, has_side_effects=True, vmem_limit_bytes=VMEM_BYTES
        ),
    )(shard, x, mixed, gate, out_grad, s0, rate, bias, skip, docs)


def deliver_kernel(*refs):
    count = len(refs) // 2
    for i in range(count):
        refs[count + i][...] = refs[i][...]


def deliver(values):
    steps = 4
    specs = [
        pl.BlockSpec((value.shape[0] // steps, value.shape[1]), lambda i: (i, 0)) for value in values
    ]
    return pl.pallas_call(
        deliver_kernel,
        grid=(steps,),
        out_shape=tuple(jax.ShapeDtypeStruct(value.shape, value.dtype) for value in values),
        in_specs=specs,
        out_specs=tuple(specs),
    )(*values)


def local(
    inputs, mixed, gate_in, entry_states, out_grad, doc_lengths, proj_weight, decay_rate, dt_bias, skip_gain
):
    n_chip = lax.axis_size("seg") // 2
    n_dp = lax.axis_size("dp")
    width = inputs.shape[-1]
    s0 = entry_states.reshape(width, entry_states.shape[-1])
    outs = layer_grads(
        proj_weight[0], inputs[0, 0], mixed[0, 0], gate_in[0, 0], out_grad[0], s0,
        decay_rate, dt_bias, skip_gain, doc_lengths, n_chip, n_dp,
    )
    input_grad, mixed_grad, gate_grad, weight_grad = deliver(outs)
    return (
        input_grad[None, None],
        mixed_grad[None, None],
        gate_grad[None, None],
        weight_grad[None],
    )


def solution(mesh):
    in_specs = (
        P("pipe", "dp", "seg", None),
        P("pipe", "dp", "seg", None),
        P("pipe", "dp", "seg", None),
        P("pipe", "dp", "seg", None, None, None),
        P("dp", "seg", None),
        P("dp", None),
        P("pipe", ("seg", "dp"), None),
        P("pipe", None),
        P("pipe", None),
        P("pipe", None),
    )
    out_specs = (
        P("pipe", "dp", "seg", None),
        P("pipe", "dp", "seg", None),
        P("pipe", "dp", "seg", None),
        P("pipe", ("seg", "dp"), None),
    )
    return jax.shard_map(local, mesh=mesh, in_specs=in_specs, out_specs=out_specs, check_vma=False)
```

```python
import functools

import jax
import jax.numpy as jnp
from jax import lax
from jax.experimental import pallas as pl
from jax.experimental.pallas import tpu as pltpu
from jax.sharding import PartitionSpec as P

MESH = pl.DeviceIdType.MESH
F32 = jnp.float32
BF16 = jnp.bfloat16
HIGH = lax.Precision.HIGHEST
LANES = 128
NEG = -1e30
UNROLL = 4
VMEM_BYTES = 56 * 1024 * 1024
VMEM = pl.BlockSpec(memory_space=pltpu.VMEM)
SMEM = pl.BlockSpec(memory_space=pltpu.SMEM)
NN = (((1,), (0,)), ((), ()))
NT = (((1,), (1,)), ((), ()))
TN = (((0,), (0,)), ((), ()))


def dot(a, b, dims=NN, precision=None):
    return lax.dot_general(a, b, dims, precision=precision, preferred_element_type=F32)


def iota(axis, shape=(LANES, LANES)):
    return lax.broadcasted_iota(jnp.int32, shape, axis)


def tile_at(j):
    return pl.ds(pl.multiple_of(j * LANES, LANES), LANES)


def split_two(value):
    high = value.astype(BF16)
    low = (value - high.astype(F32)).astype(BF16)
    return high, low


def place():
    seg = lax.axis_index("seg")
    chip = seg // 2
    core = seg - 2 * chip
    return lax.axis_index("pipe"), seg, chip, core, lax.axis_index("dp")


def greet(devices):
    barrier = pltpu.get_barrier_semaphore()
    for count, device_of in devices:
        def one(k, carry, device_of=device_of):
            pl.semaphore_signal(barrier, inc=1, device_id=device_of(k), device_id_type=MESH)
            return carry

        lax.fori_loop(0, count, one, 0)
    pl.semaphore_wait(barrier, sum(count for count, _ in devices))


def remote(src, dst, send_sem, recv_sem, device):
    return pltpu.make_async_remote_copy(
        src_ref=src, dst_ref=dst, send_sem=send_sem, recv_sem=recv_sem,
        device_id=device, device_id_type=MESH,
    )


def each(count, body, unroll=1):
    def step(k, carry):
        body(k)
        return carry

    lax.fori_loop(0, count, step, 0, unroll=unroll)


class Around:
    def __init__(self, n_chip, n_dp):
        self.n_chip, self.n_dp = n_chip, n_dp
        self.pipe, self.seg, self.chip, self.core, self.dp = place()

    def chip_slot(self, k):
        return lax.rem(self.chip + 1 + k, self.n_chip)

    def chip_device(self, k):
        return {"seg": self.chip_slot(k) * 2 + self.core}

    def dp_slot(self, k):
        return lax.rem(self.dp + 1 + k, self.n_dp)

    def dp_device(self, k):
        return {"dp": self.dp_slot(k)}

    def dp_at(self, way):
        return {"dp": lax.rem(self.dp + way + self.n_dp, self.n_dp)}

    def sibling(self, k=0):
        return {"seg": self.seg + 1 - 2 * self.core}

    def partner(self, k=0):
        return {"pipe": 1 - self.pipe}

    def greet(self, with_pipe):
        met = [(self.n_chip - 1, self.chip_device), (self.n_dp - 1, self.dp_device), (1, self.sibling)]
        greet(met + ([(1, self.partner)] if with_pipe else []))


class Gather:
    def __init__(self, near, dst, sems):
        self.near, self.dst = near, dst
        self.sends, self.chip_recv, self.side_recv, self.far_recv, self.core_recv = sems

    def source(self, k):
        near = self.near
        return lax.rem(near.chip + 2 * near.n_chip - 1 - k, near.n_chip)

    def chip_copy(self, k):
        near = self.near
        block = self.dst.at[near.chip, near.core, near.dp]
        return remote(block, block, self.sends.at[0], self.chip_recv.at[k], near.chip_device(k))

    def side_copy(self, k, i):
        near = self.near
        block = self.dst.at[self.source(k), near.core, near.dp]
        return remote(block, block, self.sends.at[1], self.side_recv.at[k, i], near.dp_at(1 if i == 0 else -1))

    def far_copy(self, k):
        near = self.near
        way = 1 - 2 * (k - k // 2 * 2)
        block = self.dst.at[self.source(k), near.core, lax.rem(near.dp + near.n_dp - way, near.n_dp)]
        return remote(block, block, self.sends.at[2], self.far_recv.at[k], near.dp_at(way))

    def core_copy(self, k):
        block = self.dst.at[self.source(k), self.near.core]
        return remote(block, block, self.sends.at[3], self.core_recv.at[k], self.near.sibling())

    def in_order(self, body):
        count = self.near.n_chip
        each(count, lambda step: body(lax.rem(step + count - 1, count)))

    def start(self, src):
        near = self.near
        self.dst[near.chip, near.core, near.dp] = src[...]
        each(near.n_chip - 1, lambda k: self.chip_copy(k).start())
        for i in range(2):
            self.side_copy(near.n_chip - 1, i).start()

    def spread(self):
        def pass_on(k):
            self.chip_copy(k).wait_recv()
            for i in range(2):
                self.side_copy(k, i).start()

        each(self.near.n_chip - 1, pass_on)

        def further(k):
            odd = k - k // 2 * 2
            block = self.dst.at[0, 0, 0]
            remote(block, block, self.sends.at[1], self.side_recv.at[k, odd], self.near.dp_at(1)).wait_recv()
            self.far_copy(k).start()

        self.in_order(further)

    def over(self, use):
        def pass_on(k):
            odd = k - k // 2 * 2
            block = self.dst.at[0, 0, 0]
            remote(block, block, self.sends.at[1], self.side_recv.at[k, 1 - odd], self.near.dp_at(1)).wait_recv()
            self.far_copy(k).wait_recv()
            self.core_copy(k).start()
            use(self.source(k), self.near.core)

        self.in_order(pass_on)

    def end(self, use):
        def take(k):
            self.core_copy(k).wait_recv()
            use(self.source(k), 1 - self.near.core)

        self.in_order(take)

    def sent(self):
        near, dst = self.near, self.dst
        regions = (
            dst.at[pl.ds(0, near.n_chip - 1), near.core, near.dp],
            dst.at[:, near.core, pl.ds(0, 2)],
            dst.at[:, near.core, near.dp],
            dst.at[:, near.core],
        )
        for i, region in enumerate(regions):
            all_sent(region, self.sends.at[i], near)


def gather_sems(n_chip, n_dp):
    assert n_dp == 4
    dma = pltpu.SemaphoreType.DMA
    return (dma((4,)), dma((n_chip - 1,)), dma((n_chip, 2)), dma((n_chip,)), dma((n_chip,)))


def all_sent(region, sem, near):
    remote(region, region, sem, sem, near.sibling()).wait_send()


def all_here(region, sem, near):
    remote(region, region, sem, sem, near.sibling()).wait_recv()


class LateGather:
    def __init__(self, near, dst, sems):
        self.near, self.dst, self.sems = near, dst, sems

    def run(self, src):
        near, dst, sems = self.near, self.dst, self.sems
        dst[near.chip, near.core, near.dp] = src[...]
        block = dst.at[near.chip, near.core, near.dp]
        chips = dst.at[pl.ds(0, near.n_chip - 1), near.core, near.dp]
        column = dst.at[:, near.core, near.dp]
        columns = dst.at[:, near.core, pl.ds(0, near.n_dp - 1)]
        side = dst.at[:, near.core]
        each(near.n_chip - 1, lambda k: remote(block, block, sems.at[0], sems.at[1], near.chip_device(k)).start())
        all_here(chips, sems.at[1], near)
        each(near.n_dp - 1, lambda k: remote(column, column, sems.at[2], sems.at[3], near.dp_device(k)).start())
        all_here(columns, sems.at[3], near)
        last = remote(side, side, sems.at[4], sems.at[5], near.sibling())
        last.start()
        last.wait()
        all_sent(chips, sems.at[0], near)
        all_sent(columns, sems.at[2], near)


def packed(value):
    piece = value.shape[0]
    tail = value[:, 2 * LANES :]
    top, low = tail[: piece // 2], tail[piece // 2 :]
    beside = top + pltpu.roll(low, LANES // 2, 1)
    return jnp.concatenate([value[:, :LANES], value[:, LANES : 2 * LANES], beside], axis=0)


def unpacked(value, piece):
    beside = value[2 * piece :]
    first = iota(1, (1, LANES)) < LANES // 2
    top = jnp.where(first, beside, 0.0)
    low = jnp.where(first, pltpu.roll(beside, LANES // 2, 1), 0.0)
    return value[:piece], value[piece : 2 * piece], jnp.concatenate([top, low], axis=0)


def weight_tiles(ref, chip, core, piece):
    block = ref[chip, core]
    tail = block[:, 2 * piece :]
    return (
        block[:, :piece].reshape(-1, LANES),
        block[:, piece : 2 * piece].reshape(-1, LANES),
        jnp.concatenate([tail, tail], axis=1).reshape(-1, LANES),
    )


def in_top(piece):
    lane = iota(1, (1, LANES))
    return lane - lane // piece * piece < piece // 2


def back_projected(dproj_ref, dt_low, ref, chip, core, piece):
    w_b, w_c, w_t = weight_tiles(ref, chip, core, piece)
    plain = dot(dproj_ref[1], w_b, NT) + dot(dproj_ref[0], w_c, NT)
    top = dot(dproj_ref[2], w_t, NT)
    low = dot(dt_low, w_t, NT)
    return plain + jnp.where(in_top(piece), top, low)


def lanes_turned(value):
    return pltpu.roll(value.astype(F32), LANES // 2, 1).astype(BF16)


def pair_columns(ref, j):
    turned = pltpu.roll(ref[...], lax.rem(LANES - 2 * j, LANES), 1)
    shape = (turned.shape[0], LANES)
    return jnp.broadcast_to(turned[:, 0:1], shape), jnp.broadcast_to(turned[:, 1:2], shape)


def by_half(first, second):
    return jnp.where(iota(1, (1, LANES)) < LANES // 2, first, second)


def heads_of(value, j):
    select = (iota(1) == 2 * j + (iota(0) >= LANES // 2).astype(jnp.int32)).astype(BF16)
    high, low = split_two(value)
    return dot(high, select) + dot(low, select)


def layer_kernel(n_chip, n_dp, *refs):
    (
        shard_ref, x_hbm, mixed_hbm, gate_hbm, out_grad_hbm, s0_hbm, rate_ref, bias_ref, skip_ref, doc_ref,
        input_out, mixed_out, gate_out, weight_out,
        x_ref, xs_ref, gate_ref, g_ref, s0_ref, shard, own_ref, one_shard, one_ref, later,
        s0t_ref, xt_ref, x_stage, group_ref, act_ref, weights, projected, bf_ref, cf_ref,
        log_ref, logt_ref, dt_ref, dtt_ref, sig_ref, rho_ref, mask_ref, first_ref, kept_ref, small,
        msg, both, total, got, back, exits, other, adj_ref, base, dproj_ref, passes, chip_passes,
        input_grad_ref, mixed_grad_ref, gate_grad_ref,
        acc_scores, acc_b, acc_c, acc_y, acc_x, acc_s, acc_a, grads, part, whole, arrived, spare, summed, sems,
    ) = refs
    (
        in_sems, out_sems, own_set, one_set, shard_sems, later_sems, pass_sems, core_sems, core_recv,
        send_sems, recv, back_recv, other_recv, xt_sems, xg_sems, dp_recv, grad_sems, grad_recv,
    ) = sems
    rows, width = x_ref.shape
    state = bf_ref.shape[1]
    heads = rate_ref.shape[1]
    cols_w = shard_ref.shape[1]
    piece = shard_ref.shape[0]
    proj = projected.shape[1]
    half = n_chip

    loads = [
        pltpu.make_async_copy(src, dst, in_sems.at[i])
        for i, (src, dst) in enumerate(
            ((gate_hbm, gate_ref), (s0_hbm, s0_ref), (x_hbm, x_ref), (out_grad_hbm, g_ref), (mixed_hbm, xs_ref))
        )
    ]
    for load in loads:
        load.start()
    spare[...] = jnp.zeros_like(spare)
    spare[:, :cols_w] = shard_ref[...].astype(F32)
    shard[...] = packed(spare[...]).astype(BF16)

    near = Around(n_chip, n_dp)
    near.greet(True)
    pipe, chip, core, dp = near.pipe, near.chip, near.core, near.dp
    shard_copy = remote(shard, one_shard, shard_sems.at[0], shard_sems.at[1], near.partner())

    def later_copy(i):
        tiles = pl.ds(i, 1 + i)
        return remote(
            dproj_ref.at[tiles], later.at[tiles], later_sems.at[0, i], later_sems.at[1, i], near.partner()
        )


    gather = Gather(near, own_ref, own_set)
    gather.start(shard)

    @pl.when(pipe == 1)
    def _():
        shard_copy.start()

    for ref in (acc_scores, acc_b, acc_c, acc_y, acc_x, acc_s, acc_a, small, projected, whole):
        ref[...] = jnp.zeros_like(ref)
    small[0:1, :heads] = rate_ref[...]
    small[8:9, :heads] = bias_ref[...]
    small[16:17, :heads] = skip_ref[...]
    begin = near.seg * rows
    count_t = jnp.zeros((rows, rows), jnp.int32)
    count_s = jnp.zeros((rows, rows), jnp.int32)
    count_last = jnp.zeros((rows, rows), jnp.int32)
    start = jnp.int32(0)
    for k in range(doc_ref.shape[1] - 1):
        start = start + doc_ref[0, k]
        offset = jnp.broadcast_to(start - begin, (rows, rows))
        inside = offset >= 0
        count_t += (inside & (iota(0) >= offset)).astype(jnp.int32)
        count_s += (inside & (iota(1) >= offset)).astype(jnp.int32)
        count_last += (inside & (offset <= rows - 1)).astype(jnp.int32)
    allowed = (iota(0) >= iota(1)) & (count_t == count_s)
    mask_ref[...] = jnp.where(allowed, 0.0, NEG)
    first_ref[...] = jnp.where(count_t == 0, 0.0, NEG)
    kept_ref[...] = jnp.where(count_t == count_last, 0.0, NEG)

    def activate(j):
        gate = gate_ref[:, tile_at(j)].astype(F32)
        act_ref[j] = gate * jax.nn.sigmoid(gate)

    def turn_state(j):
        s0t_ref[j] = s0_ref[tile_at(j), :].T.astype(BF16)

    def turn_x(k):
        for c in range(2):
            xt_ref[k, c] = x_ref[:, tile_at(2 * k + c)].T

    loads[0].wait()
    each(2 * half, activate, UNROLL)
    gather.spread()
    loads[1].wait()
    each(2 * half, turn_state, UNROLL)
    loads[2].wait()
    each(n_chip, turn_x, 2)

    def project(k, c):
        x_tile = x_ref[:, tile_at(2 * k + c)]
        zero = jnp.zeros_like(x_tile)
        w_b, w_c, w_t = weight_tiles(own_ref, k, c, piece)
        projected[:, :LANES] += dot(x_tile, w_b)
        projected[:, LANES : 2 * LANES] += dot(x_tile, w_c)
        projected[:, 2 * LANES : 3 * LANES] += dot(jnp.where(in_top(piece), x_tile, zero), w_t)
        projected[:, 3 * LANES :] += dot(jnp.where(in_top(piece), zero, x_tile), w_t)

    gather.over(project)
    gather.end(project)
    xt_copy = remote(xt_ref.at[:, 1 - core], x_stage, xt_sems.at[0], xt_sems.at[1], near.sibling())
    xt_copy.start()
    bf_ref[...] = projected[:, :state]
    cf_ref[...] = projected[:, state : 2 * state]
    raw = projected[:, 2 * LANES : 3 * LANES] + pltpu.roll(projected[:, 3 * LANES :], LANES // 2, 1)
    raw = jnp.where(iota(1) < heads, raw, 0.0) + small[8:9, :]
    soft = jnp.maximum(raw, 0.0) + jnp.log1p(jnp.exp(-jnp.abs(raw)))
    sig = 1.0 / (1.0 + jnp.exp(-jnp.abs(raw)))
    sig = jnp.where(raw >= 0, sig, 1.0 - sig)
    tiny = raw < -15.0
    exp_raw = jnp.exp(jnp.minimum(raw, 0.0))
    sig = jnp.where(tiny, exp_raw, sig)
    soft = jnp.where(tiny, exp_raw, soft)
    sig_ref[...] = sig
    rho_ref[...] = jnp.where(tiny, 1.0, sig / jnp.where(tiny, 1.0, soft))
    lower = (iota(0) >= iota(1)).astype(F32)
    log = dot(lower, -soft * small[0:1, :], precision=HIGH)
    log_ref[...] = log
    logt_ref[...] = log.T
    dt_ref[...] = soft
    dtt_ref[...] = soft.T
    first = iota(1, (1, LANES)) < LANES // 2

    passes[core] = jnp.broadcast_to(jnp.exp(log[rows - 1 :] + first_ref[rows - 1 :, :]), (8, LANES))
    pass_copy = remote(passes.at[core], passes.at[core], pass_sems.at[0], pass_sems.at[1], near.sibling())
    pass_copy.start()

    def pass_row(value, j):
        turned = pltpu.roll(value, lax.rem(LANES - 2 * j, LANES), 1)
        return by_half(turned[0:1, 0:1], turned[0:1, 1:2])

    loads[3].wait()
    pass_copy.wait()
    chip_passes[chip] = passes[0] * passes[1]

    def chip_pass_copy(k):
        block = chip_passes.at[chip]
        return remote(block, block, pass_sems.at[2], pass_sems.at[3], near.chip_device(k))

    each(n_chip - 1, lambda k: chip_pass_copy(k).start())

    @pl.when(pipe == 0)
    def _():
        shard_copy.wait_recv()
        LateGather(near, one_ref, one_set).run(one_shard)
        later_copy(0).wait_recv()
        later_copy(1).wait_recv()
        dt_low = lanes_turned(later[2])

        def recompute(k):
            for c in range(2):
                cols = tile_at(2 * k + c)
                sent = back_projected(later, dt_low, one_ref, k, c, piece)
                g_ref[:, cols] = (g_ref[:, cols].astype(F32) + sent).astype(BF16)

        each(n_chip, recompute, 2)

    ct = cf_ref[...].T.astype(BF16)

    def own(j):
        log0, log1 = pair_columns(log_ref, j)
        entry = jnp.exp(jnp.where(first, log0, log1) + first_ref[...])
        grad = (g_ref[:, tile_at(j)].astype(F32) * act_ref[j] * entry).astype(BF16)
        msg[j] = dot(ct, grad).astype(BF16)

    def swap_copy(c, slot):
        return remote(
            msg.at[(1 - core) * half + slot], both.at[core, slot],
            core_sems.at[0], core_recv.at[c], near.sibling(),
        )

    def combine(j):
        both[core, j] = msg[core * half + j]
        pass0 = pass_row(passes[0], core * half + j)
        total[j] = (both[0, j].astype(F32) + pass0 * both[1, j].astype(F32)).astype(BF16)

    def send_copy(k):
        return remote(
            total.at[near.chip_slot(k)], got.at[chip], send_sems.at[0], recv.at[chip], near.chip_device(k)
        )

    group = 4

    def own_group(c):
        slots = [near.chip_slot(c * group + i) for i in range(group)]
        for slot in slots:
            own((1 - core) * half + slot)
        for slot in slots:
            swap_copy(c, slot).start()
        for slot in slots:
            own(core * half + slot)
        all_here(both.at[core, pl.ds(0, group)], core_recv.at[c], near)
        for slot in slots:
            combine(slot)
        for i in range(group):
            @pl.when(c * group + i < n_chip - 1)
            def _(i=i):
                send_copy(c * group + i).start()

    each(n_chip // group, own_group)
    got[chip] = total[chip]

    xt_copy.wait()

    def x_copy(k, src, from_core):
        cut = pl.ds(pl.multiple_of(near.dp_slot(k) * piece, piece), piece)
        return remote(
            src.at[:, cut], group_ref.at[dp, from_core],
            xg_sems.at[0], xg_sems.at[1], near.dp_device(k),
        )

    def x_start(k):
        x_copy(k, xt_ref.at[:, core], core).start()
        x_copy(k, x_stage, 1 - core).start()

    each(n_dp - 1, x_start)
    cut = pl.ds(pl.multiple_of(dp * piece, piece), piece)
    group_ref[dp, core] = xt_ref[:, core, cut]
    group_ref[dp, 1 - core] = x_stage[:, cut]

    loads[4].wait()
    scores = dot(cf_ref[...], bf_ref[...], NT, precision=HIGH)
    b_low = bf_ref[...].astype(BF16)
    c_low = cf_ref[...].astype(BF16)

    def before(j):
        cols = tile_at(j)
        x_pair = xs_ref[:, cols]
        x_f = x_pair.astype(F32)
        gate = gate_ref[:, cols].astype(F32)
        sig = jax.nn.sigmoid(gate)
        g = g_ref[:, cols].astype(F32)
        grad_y = g * act_ref[j]
        grad_low = grad_y.astype(BF16)
        zero = jnp.zeros_like(x_pair)
        x0, x1 = jnp.where(first, x_pair, zero), jnp.where(first, zero, x_pair)
        y0, y1 = jnp.where(first, grad_low, zero), jnp.where(first, zero, grad_low)
        log0, log1 = pair_columns(log_ref, j)
        dt0, dt1 = pair_columns(dt_ref, j)
        mask = mask_ref[...]
        decay0 = jnp.exp(log0 - logt_ref[pl.ds(2 * j, 1), :] + mask) * dtt_ref[pl.ds(2 * j, 1), :]
        decay1 = jnp.exp(log1 - logt_ref[pl.ds(2 * j + 1, 1), :] + mask) * dtt_ref[pl.ds(2 * j + 1, 1), :]
        mix0 = (decay0 * scores).astype(BF16)
        mix1 = (decay1 * scores).astype(BF16)
        acc_scores[...] += dot(y0, x_pair, NT) * decay0 + dot(y1, x_pair, NT) * decay1
        log_pair = jnp.where(first, log0, log1)
        entry = jnp.exp(log_pair + first_ref[...])
        s0t = s0t_ref[j]
        y = dot(mix0, x0) + dot(mix1, x1) + entry * dot(c_low, s0t)
        acc_c[...] += dot((entry * grad_y).astype(BF16), s0t, NT)
        inner = dot(mix0, y0, TN) + dot(mix1, y1, TN)
        weights[j] = jnp.exp(log_pair[-1:, :] - log_pair + kept_ref[...]) * jnp.where(first, dt0, dt1)
        x_inner = x_f * inner
        acc_y[...] += heads_of(grad_low.astype(F32) * y - x_inner, j)
        acc_x[...] += heads_of(x_inner, j)
        skip = pltpu.roll(small[16:24, :], lax.rem(LANES - 2 * j, LANES), 1)
        skip = by_half(skip[0:1, 0:1], skip[0:1, 1:2])
        slope = sig * (1.0 + gate * (1.0 - sig))
        gate_grad_ref[:, cols] = (g * (y + skip * x_f) * slope).astype(BF16)
        base[j] = inner + skip * grad_y

    each(half, before, UNROLL)

    all_here(chip_passes.at[pl.ds(0, n_chip - 1)], pass_sems.at[3], near)

    def back_copy(k):
        return remote(
            back.at[k], exits.at[chip], send_sems.at[1], back_recv.at[chip], {"seg": k * 2 + core}
        )

    def scan(step, carry):
        k = n_chip - 1 - step

        @pl.when(k != chip)
        def _():
            all_here(got.at[k], recv.at[k], near)

        back[k] = carry.astype(BF16)

        @pl.when(k != chip)
        def _():
            back_copy(k).start()

        return got[k].astype(F32) + pass_row(chip_passes[k], core * half + chip) * carry

    lax.fori_loop(0, n_chip, scan, jnp.zeros((state, LANES), F32))
    exits[chip] = back[chip]
    each(half, lambda j: before(half + j), UNROLL)
    c_grad = acc_c[...] + dot(acc_scores[...], bf_ref[...], precision=HIGH)
    dproj_ref[0] = c_grad.astype(BF16)
    acc_b[...] += dot(acc_scores[...].T, cf_ref[...], precision=HIGH)

    @pl.when(pipe == 1)
    def _():
        later_copy(0).start()

    gate_copy = pltpu.make_async_copy(gate_grad_ref, gate_out, out_sems.at[0])
    gate_copy.start()

    def other_copy(c, j):
        return remote(
            other.at[j], adj_ref.at[core * half + j], core_sems.at[1], other_recv.at[c], near.sibling()
        )

    def finish(c, j):
        @pl.when(j != chip)
        def _():
            all_here(exits.at[j], back_recv.at[j], near)

        after = exits[j].astype(F32)
        earlier = both[1, j].astype(F32) + pass_row(passes[1], core * half + j) * after
        is_later = core == 1
        adj_ref[core * half + j] = jnp.where(is_later, after, earlier).astype(BF16)
        other[j] = jnp.where(is_later, earlier, after).astype(BF16)
        other_copy(c, j).start()

    def near_first(i):
        x_off = i - i // 2 * 2
        m = i // 2
        odd = m - m // 2 * 2
        z_off = odd * ((m + 1) // 2) - (1 - odd) * (m // 2)
        ring = n_chip // 2
        my_x = chip // ring
        z = lax.rem(chip - my_x * ring + z_off + ring, ring)
        return lax.rem(my_x + x_off, 2) * ring + z

    def after_scan(j):
        cols = tile_at(j)
        adj = adj_ref[j]
        weight = weights[j]
        x_f = xs_ref[:, cols].astype(F32)
        outer = weight * dot(b_low, adj)
        acc_b[...] += dot((x_f * weight).astype(BF16), adj, NT)
        acc_s[...] += heads_of(x_f * outer, j)
        last = pass_row(passes[core], j)
        passed = last * jnp.sum(adj.astype(F32) * s0t_ref[j].astype(F32), axis=0, keepdims=True)
        select = (iota(1) == 2 * j + (iota(0) >= LANES // 2).astype(jnp.int32)).astype(BF16)
        high, low = split_two(jnp.broadcast_to(passed, (8, LANES)))
        acc_a[...] += dot(high, select) + dot(low, select)
        mixed_grad_ref[:, cols] = (base[j] + outer).astype(BF16)

    def mine_group(c):
        slots = [near_first(c * group + i) for i in range(group)]
        for slot in slots:
            finish(c, slot)
        for slot in slots:
            after_scan(core * half + slot)

    def other_group(c):
        slots = [near_first(c * group + i) for i in range(group)]
        all_here(other.at[pl.ds(0, group)], other_recv.at[c], near)
        for slot in slots:
            after_scan((1 - core) * half + slot)

    each(n_chip // group, mine_group)
    each(n_chip // group, other_group)

    u = acc_x[...] + acc_s[...]
    last = jnp.sum(acc_s[...], axis=0, keepdims=True) + acc_a[0:1, :]
    upper = (iota(0) <= iota(1)).astype(F32)
    log_grad = dot(upper, acc_y[...] - acc_s[...], precision=HIGH) + last
    raw_grad = u * rho_ref[...] - small[0:1, :] * log_grad * sig_ref[...]
    dproj_ref[1] = acc_b[...].astype(BF16)
    dproj_ref[2] = raw_grad.astype(BF16)

    @pl.when(pipe == 1)
    def _():
        later_copy(1).start()

    def dp_copy(k):
        return remote(dproj_ref, grads.at[core, dp], grad_sems.at[0], dp_recv.at[k], near.dp_device(k))

    each(n_dp - 1, lambda k: dp_copy(k).start())

    def grad_swap(i, slot):
        block = grads.at[core, slot]
        return remote(block, block, grad_sems.at[1], grad_recv.at[i], near.sibling())

    grads[core, dp] = dproj_ref[...]
    grad_swap(n_dp - 1, dp).start()
    mixed_copy = pltpu.make_async_copy(mixed_grad_ref, mixed_out, out_sems.at[1])
    mixed_copy.start()
    dt_low = lanes_turned(dproj_ref[2])

    def give(k):
        for c in range(2):
            cols = tile_at(2 * k + c)
            sent = back_projected(dproj_ref, dt_low, own_ref, k, c, piece)
            input_grad_ref[:, cols] = (g_ref[:, cols].astype(F32) + sent).astype(BF16)

    each(n_chip, give, 2)
    input_copy = pltpu.make_async_copy(input_grad_ref, input_out, out_sems.at[2])
    input_copy.start()

    all_here(group_ref.at[pl.ds(0, n_dp - 1)], xg_sems.at[1], near)

    def add(c, k):
        x = group_ref[k, c].reshape(-1, rows)
        whole[:, :LANES] += dot(x, grads[c, k, 1])
        whole[:, LANES : 2 * LANES] += dot(x, grads[c, k, 0])
        whole[:, 2 * LANES :] += dot(x, grads[c, k, 2])

    def grad_slot(i):
        return lax.rem(dp + 2 * n_dp - 1 - i, n_dp)

    for i in range(n_dp - 1):
        dp_copy(i).wait_recv()
        grad_swap(i, grad_slot(i)).start()
    each(n_dp, lambda i: add(core, i), 2)
    for i in range(n_dp):
        grad_swap(i, grad_slot(i)).wait_recv()
    each(n_dp, lambda i: add(1 - core, i), 2)

    def sum_copy(k):
        return remote(
            part.at[near.chip_slot(k)], arrived.at[k], grad_sems.at[2], grad_sems.at[3], near.chip_device(k)
        )

    def ship(k):
        slot = near.chip_slot(k)
        part[slot] = packed(whole[pl.ds(pl.multiple_of(slot * piece, piece), piece), :]).astype(BF16)
        sum_copy(k).start()

    each(n_chip - 1, ship)
    summed[...] = packed(whole[pl.ds(pl.multiple_of(chip * piece, piece), piece), :])

    @pl.when(pipe == 1)
    def _():
        shard_copy.wait_send()
        later_copy(0).wait_send()
        later_copy(1).wait_send()

    gather.sent()
    first_chips = pl.ds(0, n_chip - 1)
    all_sent(chip_passes.at[first_chips], pass_sems.at[2], near)
    all_sent(both.at[core], core_sems.at[0], near)
    all_sent(total.at[first_chips], send_sems.at[0], near)
    all_sent(back.at[first_chips], send_sems.at[1], near)
    all_sent(other, core_sems.at[1], near)
    all_sent(group_ref.at[pl.ds(0, n_dp - 1)], xg_sems.at[0], near)
    all_sent(grads.at[core, pl.ds(0, n_dp - 1)], grad_sems.at[0], near)
    all_sent(grads.at[core], grad_sems.at[1], near)

    def collect(k):
        summed[...] += arrived[k].astype(F32)

    all_here(arrived, grad_sems.at[3], near)
    each(n_chip - 1, collect, 5)
    out_b, out_c, out_t = unpacked(summed[...], piece)
    weight_out[:, :LANES] = out_b
    weight_out[:, LANES : 2 * LANES] = out_c
    weight_out[:, 2 * LANES :] = out_t[:, : cols_w - 2 * LANES]
    all_sent(arrived, grad_sems.at[2], near)
    gate_copy.wait()
    mixed_copy.wait()
    input_copy.wait()


def layer_grads(shard, x, mixed, gate, out_grad, s0, rate, bias, skip, docs, n_chip, n_dp):
    rows, width = x.shape
    pairs = width // LANES
    state = s0.shape[1]
    piece, cols = shard.shape
    proj = cols + -cols % LANES
    dma = pltpu.SemaphoreType.DMA
    line = jax.ShapeDtypeStruct((rows, width), BF16)
    whole_line = pltpu.VMEM((rows, width), BF16)
    square = pltpu.VMEM((rows, LANES), F32)
    packed_rows = 2 * piece + piece // 2
    full_w = pltpu.VMEM((n_chip, 2, n_dp, packed_rows, LANES), BF16)
    wide = pltpu.VMEM((pairs, rows, LANES), F32)
    tiles = pltpu.VMEM((proj // LANES, rows, LANES), BF16)
    plain = pltpu.VMEM((n_chip, state, LANES), BF16)
    anywhere = pl.BlockSpec(memory_space=pl.ANY)
    chips = dma((n_chip,))
    return pl.pallas_call(
        functools.partial(layer_kernel, n_chip, n_dp),
        out_shape=(line, line, line, jax.ShapeDtypeStruct((piece, cols), F32)),
        in_specs=[VMEM] + [anywhere] * 5 + [VMEM] * 3 + [SMEM],
        out_specs=(anywhere, anywhere, anywhere, VMEM),
        scratch_shapes=[
            whole_line, whole_line, whole_line, whole_line,
            pltpu.VMEM((width, state), F32),
            pltpu.VMEM((packed_rows, LANES), BF16),
            full_w,
            pltpu.VMEM((packed_rows, LANES), BF16),
            full_w,
            tiles,
            pltpu.VMEM((pairs, state, LANES), BF16),
            pltpu.VMEM((n_chip, 2, LANES, rows), BF16),
            pltpu.VMEM((n_chip, LANES, rows), BF16),
            pltpu.VMEM((n_dp, 2, n_chip, piece, rows), BF16),
            wide, wide,
            pltpu.VMEM((rows, proj + LANES), F32),
        ]
        + [square] * 11
        + [
            pltpu.VMEM((24, LANES), F32),
            pltpu.VMEM((pairs, state, LANES), BF16),
            pltpu.VMEM((2, n_chip, state, LANES), BF16),
            plain, plain, plain, plain, plain,
            pltpu.VMEM((pairs, state, LANES), BF16),
            wide,
            tiles,
            pltpu.VMEM((2, 8, LANES), F32),
            pltpu.VMEM((n_chip, 8, LANES), F32),
            whole_line, whole_line, whole_line,
        ]
        + [square] * 6
        + [
            pltpu.VMEM((8, LANES), F32),
            pltpu.VMEM((2, n_dp, proj // LANES, rows, LANES), BF16),
            pltpu.VMEM((n_chip, packed_rows, LANES), BF16),
            pltpu.VMEM((n_chip * piece, proj), F32),
            pltpu.VMEM((n_chip - 1, packed_rows, LANES), BF16),
            pltpu.VMEM((piece, proj), F32),
            pltpu.VMEM((packed_rows, LANES), F32),
            (
                dma((5,)), dma((3,)), gather_sems(n_chip, n_dp), dma((6,)), dma((2,)), dma((2, 2)), dma((4,)),
                dma((2,)), dma((4,)), dma((2,)), chips, chips, dma((4,)), dma((2,)), dma((2,)),
                dma((n_dp - 1,)), dma((4,)), dma((n_dp,)),
            ),
        ],
        compiler_params=pltpu.CompilerParams(
            collective_id=1, has_side_effects=True, vmem_limit_bytes=VMEM_BYTES
        ),
    )(shard, x, mixed, gate, out_grad, s0, rate, bias, skip, docs)


def deliver_kernel(cuts, *refs):
    count = len(cuts)
    held, sems = refs[2 * count : 3 * count], refs[-1]
    steps = []
    for i, cut in enumerate(cuts):
        size = held[i].shape[0] // cut
        for k in range(cut):
            rows = pl.ds(k * size, size)
            at = len(steps)
            load = pltpu.make_async_copy(refs[i].at[rows], held[i].at[rows], sems.at[0, at])
            store = pltpu.make_async_copy(held[i].at[rows], refs[count + i].at[rows], sems.at[1, at])
            steps.append((load, store))
    for load, _ in steps:
        load.start()
    for load, store in steps:
        load.wait()
        store.start()
    for _, store in steps:
        store.wait()


def deliver(values):
    anywhere = pl.BlockSpec(memory_space=pl.ANY)
    cuts = [2 if value.dtype == BF16 else 1 for value in values]
    return pl.pallas_call(
        functools.partial(deliver_kernel, cuts),
        out_shape=tuple(jax.ShapeDtypeStruct(value.shape, value.dtype) for value in values),
        in_specs=[anywhere] * len(values),
        out_specs=(anywhere,) * len(values),
        scratch_shapes=[pltpu.VMEM(value.shape, value.dtype) for value in values]
        + [pltpu.SemaphoreType.DMA((2, sum(cuts)))],
    )(*values)


def local(
    inputs, mixed, gate_in, entry_states, out_grad, doc_lengths, proj_weight, decay_rate, dt_bias, skip_gain
):
    n_chip = lax.axis_size("seg") // 2
    n_dp = lax.axis_size("dp")
    width = inputs.shape[-1]
    s0 = entry_states.reshape(width, entry_states.shape[-1])
    outs = layer_grads(
        proj_weight[0], inputs[0, 0], mixed[0, 0], gate_in[0, 0], out_grad[0], s0,
        decay_rate, dt_bias, skip_gain, doc_lengths, n_chip, n_dp,
    )
    input_grad, mixed_grad, gate_grad, weight_grad = deliver(outs)
    return (
        input_grad[None, None],
        mixed_grad[None, None],
        gate_grad[None, None],
        weight_grad[None],
    )


def solution(mesh):
    in_specs = (
        P("pipe", "dp", "seg", None),
        P("pipe", "dp", "seg", None),
        P("pipe", "dp", "seg", None),
        P("pipe", "dp", "seg", None, None, None),
        P("dp", "seg", None),
        P("dp", None),
        P("pipe", ("seg", "dp"), None),
        P("pipe", None),
        P("pipe", None),
        P("pipe", None),
    )
    out_specs = (
        P("pipe", "dp", "seg", None),
        P("pipe", "dp", "seg", None),
        P("pipe", "dp", "seg", None),
        P("pipe", ("seg", "dp"), None),
    )
    return jax.shard_map(local, mesh=mesh, in_specs=in_specs, out_specs=out_specs, check_vma=False)
```

```python
import functools

import jax
import jax.numpy as jnp
from jax import lax
from jax.experimental import pallas as pl
from jax.experimental.pallas import tpu as pltpu
from jax.sharding import PartitionSpec as P

MESH = pl.DeviceIdType.MESH
F32 = jnp.float32
BF16 = jnp.bfloat16
HIGH = lax.Precision.HIGHEST
LANES = 128
NEG = -1e30
UNROLL = 4
GROUP = 4
VMEM_BYTES = 56 * 1024 * 1024
VMEM = pl.BlockSpec(memory_space=pltpu.VMEM)
SMEM = pl.BlockSpec(memory_space=pltpu.SMEM)
NN = (((1,), (0,)), ((), ()))
NT = (((1,), (1,)), ((), ()))
TN = (((0,), (0,)), ((), ()))


def dot(a, b, dims=NN, precision=None):
    return lax.dot_general(a, b, dims, precision=precision, preferred_element_type=F32)


def iota(axis, shape=(LANES, LANES)):
    return lax.broadcasted_iota(jnp.int32, shape, axis)


def tile_at(j):
    return pl.ds(pl.multiple_of(j * LANES, LANES), LANES)


def split_two(value):
    high = value.astype(BF16)
    low = (value - high.astype(F32)).astype(BF16)
    return high, low


def place():
    seg = lax.axis_index("seg")
    chip = seg // 2
    core = seg - 2 * chip
    return lax.axis_index("pipe"), seg, chip, core, lax.axis_index("dp")


def greet(devices):
    barrier = pltpu.get_barrier_semaphore()
    for count, device_of in devices:
        def one(k, carry, device_of=device_of):
            pl.semaphore_signal(barrier, inc=1, device_id=device_of(k), device_id_type=MESH)
            return carry

        lax.fori_loop(0, count, one, 0)
    pl.semaphore_wait(barrier, sum(count for count, _ in devices))


def remote(src, dst, send_sem, recv_sem, device):
    return pltpu.make_async_remote_copy(
        src_ref=src, dst_ref=dst, send_sem=send_sem, recv_sem=recv_sem,
        device_id=device, device_id_type=MESH,
    )


def each(count, body, unroll=1):
    def step(k, carry):
        body(k)
        return carry

    lax.fori_loop(0, count, step, 0, unroll=unroll)


class Around:
    def __init__(self, n_chip, n_dp):
        self.n_chip, self.n_dp = n_chip, n_dp
        self.pipe, self.seg, self.chip, self.core, self.dp = place()

    def chip_slot(self, k):
        return lax.rem(self.chip + 1 + k, self.n_chip)

    def chip_device(self, k):
        return {"seg": self.chip_slot(k) * 2 + self.core}

    def dp_slot(self, k):
        return lax.rem(self.dp + 1 + k, self.n_dp)

    def dp_device(self, k):
        return {"dp": self.dp_slot(k)}

    def dp_at(self, way):
        return {"dp": lax.rem(self.dp + way + self.n_dp, self.n_dp)}

    def sibling(self, k=0):
        return {"seg": self.seg + 1 - 2 * self.core}

    def partner(self, k=0):
        return {"pipe": 1 - self.pipe}

    def greet(self, with_pipe):
        met = [(self.n_chip - 1, self.chip_device), (self.n_dp - 1, self.dp_device), (1, self.sibling)]
        greet(met + ([(1, self.partner)] if with_pipe else []))


class Gather:
    def __init__(self, near, dst, sems):
        self.near, self.dst = near, dst
        self.sends, self.chip_recv, self.side_recv, self.far_recv, self.core_recv = sems

    def source(self, k):
        near = self.near
        return lax.rem(near.chip + 2 * near.n_chip - 1 - k, near.n_chip)

    def chip_copy(self, k):
        near = self.near
        block = self.dst.at[near.chip, near.core, near.dp]
        return remote(block, block, self.sends.at[0], self.chip_recv.at[k], near.chip_device(k))

    def side_copy(self, k, i):
        near = self.near
        block = self.dst.at[self.source(k), near.core, near.dp]
        return remote(block, block, self.sends.at[1], self.side_recv.at[k, i], near.dp_at(1 if i == 0 else -1))

    def far_copy(self, k):
        near = self.near
        way = 1 - 2 * (k - k // 2 * 2)
        block = self.dst.at[self.source(k), near.core, lax.rem(near.dp + near.n_dp - way, near.n_dp)]
        return remote(block, block, self.sends.at[2], self.far_recv.at[k], near.dp_at(way))

    def core_copy(self, c, k):
        block = self.dst.at[self.source(k), self.near.core]
        return remote(block, block, self.sends.at[3], self.core_recv.at[c], self.near.sibling())

    def turn(self, step):
        return lax.rem(step + self.near.n_chip - 1, self.near.n_chip)

    def start(self, src):
        near = self.near
        self.dst[near.chip, near.core, near.dp] = src[...]
        each(near.n_chip - 1, lambda k: self.chip_copy(k).start())
        for i in range(2):
            self.side_copy(near.n_chip - 1, i).start()

    def spread(self):
        def pass_on(k):
            self.chip_copy(k).wait_recv()
            for i in range(2):
                self.side_copy(k, i).start()

        each(self.near.n_chip - 1, pass_on)

        def further(k):
            odd = k - k // 2 * 2
            block = self.dst.at[0, 0, 0]
            remote(block, block, self.sends.at[1], self.side_recv.at[k, odd], self.near.dp_at(1)).wait_recv()
            self.far_copy(k).start()

        each(self.near.n_chip, lambda step: further(self.turn(step)))

    def over(self, use):
        def pass_on(c):
            turns = [self.turn(c * GROUP + i) for i in range(GROUP)]
            block = self.dst.at[0, 0, 0]
            for k in turns:
                odd = k - k // 2 * 2
                all_here(block, self.side_recv.at[k, 1 - odd], self.near)
                all_here(block, self.far_recv.at[k], self.near)
                self.core_copy(c, k).start()
            use([self.source(k) for k in turns], self.near.core)

        each(self.near.n_chip // GROUP, pass_on)

    def end(self, use):
        def take(c):
            all_here(self.dst.at[pl.ds(0, GROUP), self.near.core], self.core_recv.at[c], self.near)
            use([self.source(self.turn(c * GROUP + i)) for i in range(GROUP)], 1 - self.near.core)

        each(self.near.n_chip // GROUP, take)

    def sent(self):
        near, dst = self.near, self.dst
        regions = (
            dst.at[pl.ds(0, near.n_chip - 1), near.core, near.dp],
            dst.at[:, near.core, pl.ds(0, 2)],
            dst.at[:, near.core, near.dp],
            dst.at[:, near.core],
        )
        for i, region in enumerate(regions):
            all_sent(region, self.sends.at[i], near)


def gather_sems(n_chip, n_dp):
    assert n_dp == 4
    dma = pltpu.SemaphoreType.DMA
    return (dma((4,)), dma((n_chip - 1,)), dma((n_chip, 2)), dma((n_chip,)), dma((n_chip // GROUP,)))


def all_sent(region, sem, near):
    remote(region, region, sem, sem, near.sibling()).wait_send()


def all_here(region, sem, near):
    remote(region, region, sem, sem, near.sibling()).wait_recv()


class LateGather:
    def __init__(self, near, dst, sems):
        self.near, self.dst, self.sems = near, dst, sems

    def run(self, src):
        near, dst, sems = self.near, self.dst, self.sems
        dst[near.chip, near.core, near.dp] = src[...]
        block = dst.at[near.chip, near.core, near.dp]
        chips = dst.at[pl.ds(0, near.n_chip - 1), near.core, near.dp]
        column = dst.at[:, near.core, near.dp]
        columns = dst.at[:, near.core, pl.ds(0, near.n_dp - 1)]
        side = dst.at[:, near.core]
        each(near.n_chip - 1, lambda k: remote(block, block, sems.at[0], sems.at[1], near.chip_device(k)).start())
        all_here(chips, sems.at[1], near)
        each(near.n_dp - 1, lambda k: remote(column, column, sems.at[2], sems.at[3], near.dp_device(k)).start())
        all_here(columns, sems.at[3], near)
        last = remote(side, side, sems.at[4], sems.at[5], near.sibling())
        last.start()
        last.wait()
        all_sent(chips, sems.at[0], near)
        all_sent(columns, sems.at[2], near)


def beside(tail):
    half = tail.shape[0] // 2
    return tail[:half] + pltpu.roll(tail[half:], LANES // 2, 1)


def below(value):
    first = iota(1, (1, LANES)) < LANES // 2
    top = jnp.where(first, value, 0.0)
    low = jnp.where(first, pltpu.roll(value, LANES // 2, 1), 0.0)
    return jnp.concatenate([top, low], axis=0)


def packed(value):
    tail = beside(value[:, 2 * LANES :])
    return jnp.concatenate([value[:, :LANES], value[:, LANES : 2 * LANES], tail], axis=0)


def weight_tiles(ref, chip, core, piece):
    block = ref[chip, core]
    tail = block[:, 2 * piece :]
    return (
        block[:, :piece].reshape(-1, LANES),
        block[:, piece : 2 * piece].reshape(-1, LANES),
        jnp.concatenate([tail, tail], axis=1).reshape(-1, LANES),
    )


def in_top(piece):
    lane = iota(1, (1, LANES))
    return lane - lane // piece * piece < piece // 2


def back_projected(dproj_ref, dt_low, ref, chip, core, piece):
    w_b, w_c, w_t = weight_tiles(ref, chip, core, piece)
    plain = dot(dproj_ref[1], w_b, NT) + dot(dproj_ref[0], w_c, NT)
    top = dot(dproj_ref[2], w_t, NT)
    low = dot(dt_low, w_t, NT)
    return plain + jnp.where(in_top(piece), top, low)


def lanes_turned(value):
    return pltpu.roll(value.astype(F32), LANES // 2, 1).astype(BF16)


def pair_columns(ref, j):
    turned = pltpu.roll(ref[...], lax.rem(LANES - 2 * j, LANES), 1)
    shape = (turned.shape[0], LANES)
    return jnp.broadcast_to(turned[:, 0:1], shape), jnp.broadcast_to(turned[:, 1:2], shape)


def by_half(first, second):
    return jnp.where(iota(1, (1, LANES)) < LANES // 2, first, second)


def heads_of(value, j):
    select = (iota(1) == 2 * j + (iota(0) >= LANES // 2).astype(jnp.int32)).astype(BF16)
    high, low = split_two(value)
    return dot(high, select) + dot(low, select)


def layer_kernel(n_chip, n_dp, *refs):
    (
        shard_ref, x_hbm, mixed_hbm, gate_hbm, out_grad_hbm, s0_hbm, rate_ref, bias_ref, skip_ref, doc_ref,
        input_out, mixed_out, gate_out, weight_out,
        x_ref, xs_ref, gate_ref, g_ref, s0_ref, shard, own_ref, one_shard, one_ref, later,
        s0t_ref, xt_ref, x_stage, group_ref, act_ref, weights, projected, bf_ref, cf_ref,
        log_ref, logt_ref, dt_ref, dtt_ref, sig_ref, rho_ref, mask_ref, first_ref, kept_ref, small,
        msg, both, total, got, back, exits, other, adj_ref, base, dproj_ref, passes, chip_passes,
        input_grad_ref, mixed_grad_ref, gate_grad_ref,
        acc_scores, acc_b, acc_c, acc_y, acc_x, acc_s, acc_a, grads, part_c, part_o, whole, arrived_c, arrived_o, spare, sems,
    ) = refs
    (
        in_sems, out_sems, own_set, one_set, shard_sems, later_sems, pass_sems, core_sems, core_recv,
        send_sems, recv, back_recv, other_recv, xt_sems, xg_sems, dp_recv, grad_sems, grad_recv,
    ) = sems
    rows, width = x_ref.shape
    state = bf_ref.shape[1]
    heads = rate_ref.shape[1]
    cols_w = shard_ref.shape[1]
    piece = shard_ref.shape[0]
    proj = projected.shape[1]
    half = n_chip

    loads = [
        pltpu.make_async_copy(src, dst, in_sems.at[i])
        for i, (src, dst) in enumerate(
            ((gate_hbm, gate_ref), (s0_hbm, s0_ref), (x_hbm, x_ref), (out_grad_hbm, g_ref), (mixed_hbm, xs_ref))
        )
    ]
    for load in loads:
        load.start()
    spare[...] = jnp.zeros_like(spare)
    spare[:, :cols_w] = shard_ref[...].astype(F32)
    shard[...] = packed(spare[...]).astype(BF16)

    near = Around(n_chip, n_dp)
    near.greet(True)
    pipe, chip, core, dp = near.pipe, near.chip, near.core, near.dp
    shard_copy = remote(shard, one_shard, shard_sems.at[0], shard_sems.at[1], near.partner())

    def later_copy(i):
        tiles = pl.ds(i, 1 + i)
        return remote(
            dproj_ref.at[tiles], later.at[tiles], later_sems.at[0, i], later_sems.at[1, i], near.partner()
        )


    gather = Gather(near, own_ref, own_set)
    gather.start(shard)

    @pl.when(pipe == 1)
    def _():
        shard_copy.start()

    for ref in (acc_scores, acc_b, acc_c, acc_y, acc_x, acc_s, acc_a, small, projected):
        ref[...] = jnp.zeros_like(ref)
    small[0:1, :heads] = rate_ref[...]
    small[8:9, :heads] = bias_ref[...]
    small[16:17, :heads] = skip_ref[...]
    begin = near.seg * rows
    count_t = jnp.zeros((rows, rows), jnp.int32)
    count_s = jnp.zeros((rows, rows), jnp.int32)
    count_last = jnp.zeros((rows, rows), jnp.int32)
    start = jnp.int32(0)
    for k in range(doc_ref.shape[1] - 1):
        start = start + doc_ref[0, k]
        offset = jnp.broadcast_to(start - begin, (rows, rows))
        inside = offset >= 0
        count_t += (inside & (iota(0) >= offset)).astype(jnp.int32)
        count_s += (inside & (iota(1) >= offset)).astype(jnp.int32)
        count_last += (inside & (offset <= rows - 1)).astype(jnp.int32)
    allowed = (iota(0) >= iota(1)) & (count_t == count_s)
    mask_ref[...] = jnp.where(allowed, 0.0, NEG)
    first_ref[...] = jnp.where(count_t == 0, 0.0, NEG)
    kept_ref[...] = jnp.where(count_t == count_last, 0.0, NEG)

    def activate(j):
        gate = gate_ref[:, tile_at(j)].astype(F32)
        act_ref[j] = gate * jax.nn.sigmoid(gate)

    def turn_state(j):
        s0t_ref[j] = s0_ref[tile_at(j), :].T.astype(BF16)

    def turn_x(k):
        for c in range(2):
            xt_ref[k, c] = x_ref[:, tile_at(2 * k + c)].T

    loads[0].wait()
    each(2 * half, activate, UNROLL)
    gather.spread()
    loads[1].wait()
    each(2 * half, turn_state, UNROLL)
    loads[2].wait()
    each(n_chip, turn_x, 2)

    def project(chips, c):
        top = in_top(piece)
        x_tiles = [x_ref[:, tile_at(2 * k + c)] for k in chips]
        zero = jnp.zeros_like(x_tiles[0])
        w_b, w_c, w_t = [
            jnp.concatenate(column, axis=0)
            for column in zip(*[weight_tiles(own_ref, k, c, piece) for k in chips])
        ]

        def lined(tiles):
            return jnp.concatenate(tiles, axis=1)

        x_all = lined(x_tiles)
        projected[:, :LANES] += dot(x_all, w_b)
        projected[:, LANES : 2 * LANES] += dot(x_all, w_c)
        projected[:, 2 * LANES : 3 * LANES] += dot(lined([jnp.where(top, x, zero) for x in x_tiles]), w_t)
        projected[:, 3 * LANES :] += dot(lined([jnp.where(top, zero, x) for x in x_tiles]), w_t)

    gather.over(project)
    gather.end(project)
    xt_copy = remote(xt_ref.at[:, 1 - core], x_stage, xt_sems.at[0], xt_sems.at[1], near.sibling())
    xt_copy.start()
    bf_ref[...] = projected[:, :state]
    cf_ref[...] = projected[:, state : 2 * state]
    raw = projected[:, 2 * LANES : 3 * LANES] + pltpu.roll(projected[:, 3 * LANES :], LANES // 2, 1)
    raw = jnp.where(iota(1) < heads, raw, 0.0) + small[8:9, :]
    soft = jnp.maximum(raw, 0.0) + jnp.log1p(jnp.exp(-jnp.abs(raw)))
    sig = 1.0 / (1.0 + jnp.exp(-jnp.abs(raw)))
    sig = jnp.where(raw >= 0, sig, 1.0 - sig)
    tiny = raw < -15.0
    exp_raw = jnp.exp(jnp.minimum(raw, 0.0))
    sig = jnp.where(tiny, exp_raw, sig)
    soft = jnp.where(tiny, exp_raw, soft)
    sig_ref[...] = sig
    rho_ref[...] = jnp.where(tiny, 1.0, sig / jnp.where(tiny, 1.0, soft))
    lower = (iota(0) >= iota(1)).astype(F32)
    log = dot(lower, -soft * small[0:1, :], precision=HIGH)
    log_ref[...] = log
    logt_ref[...] = log.T
    dt_ref[...] = soft
    dtt_ref[...] = soft.T
    first = iota(1, (1, LANES)) < LANES // 2

    passes[core] = jnp.broadcast_to(jnp.exp(log[rows - 1 :] + first_ref[rows - 1 :, :]), (8, LANES))
    pass_copy = remote(passes.at[core], passes.at[core], pass_sems.at[0], pass_sems.at[1], near.sibling())
    pass_copy.start()

    def pass_row(value, j):
        turned = pltpu.roll(value, lax.rem(LANES - 2 * j, LANES), 1)
        return by_half(turned[0:1, 0:1], turned[0:1, 1:2])

    loads[3].wait()
    pass_copy.wait()
    chip_passes[chip] = passes[0] * passes[1]

    def chip_pass_copy(k):
        block = chip_passes.at[chip]
        return remote(block, block, pass_sems.at[2], pass_sems.at[3], near.chip_device(k))

    each(n_chip - 1, lambda k: chip_pass_copy(k).start())

    @pl.when(pipe == 0)
    def _():
        shard_copy.wait_recv()
        LateGather(near, one_ref, one_set).run(one_shard)
        later_copy(0).wait_recv()
        later_copy(1).wait_recv()
        dt_low = lanes_turned(later[2])

        def recompute(k):
            for c in range(2):
                cols = tile_at(2 * k + c)
                sent = back_projected(later, dt_low, one_ref, k, c, piece)
                g_ref[:, cols] = (g_ref[:, cols].astype(F32) + sent).astype(BF16)

        each(n_chip, recompute, 2)

    ct = cf_ref[...].T.astype(BF16)

    def own(j):
        log0, log1 = pair_columns(log_ref, j)
        entry = jnp.exp(jnp.where(first, log0, log1) + first_ref[...])
        grad = (g_ref[:, tile_at(j)].astype(F32) * act_ref[j] * entry).astype(BF16)
        msg[j] = dot(ct, grad).astype(BF16)

    def swap_copy(c, slot):
        return remote(
            msg.at[(1 - core) * half + slot], both.at[core, slot],
            core_sems.at[0], core_recv.at[c], near.sibling(),
        )

    def combine(j):
        both[core, j] = msg[core * half + j]
        pass0 = pass_row(passes[0], core * half + j)
        total[j] = (both[0, j].astype(F32) + pass0 * both[1, j].astype(F32)).astype(BF16)

    def send_copy(k):
        return remote(
            total.at[near.chip_slot(k)], got.at[chip], send_sems.at[0], recv.at[chip], near.chip_device(k)
        )

    group = GROUP
    couple = 2

    def couple_slots(c):
        return [near.chip_slot(c * couple + i) for i in range(couple)]

    def own_theirs(c):
        slots = couple_slots(c)
        for slot in slots:
            own((1 - core) * half + slot)
        for slot in slots:
            swap_copy(c, slot).start()

    def own_mine(c, send_count):
        slots = couple_slots(c)
        for slot in slots:
            own(core * half + slot)
        all_here(both.at[core, pl.ds(0, couple)], core_recv.at[c], near)
        for slot in slots:
            combine(slot)
        for i in range(send_count):
            send_copy(c * couple + i).start()

    def own_step(c):
        own_theirs(c + 1)
        own_mine(c, couple)

    own_theirs(0)
    each(n_chip // couple - 1, own_step)
    own_mine(n_chip // couple - 1, couple - 1)
    got[chip] = total[chip]

    xt_copy.wait()

    def x_copy(k, src, from_core):
        cut = pl.ds(pl.multiple_of(near.dp_slot(k) * piece, piece), piece)
        return remote(
            src.at[:, cut], group_ref.at[dp, from_core],
            xg_sems.at[0], xg_sems.at[1], near.dp_device(k),
        )

    def x_start(k):
        x_copy(k, xt_ref.at[:, core], core).start()
        x_copy(k, x_stage, 1 - core).start()

    each(n_dp - 1, x_start)
    cut = pl.ds(pl.multiple_of(dp * piece, piece), piece)
    group_ref[dp, core] = xt_ref[:, core, cut]
    group_ref[dp, 1 - core] = x_stage[:, cut]

    loads[4].wait()
    scores = dot(cf_ref[...], bf_ref[...], NT, precision=HIGH)
    b_low = bf_ref[...].astype(BF16)
    c_low = cf_ref[...].astype(BF16)

    def before(j):
        cols = tile_at(j)
        x_pair = xs_ref[:, cols]
        x_f = x_pair.astype(F32)
        gate = gate_ref[:, cols].astype(F32)
        sig = jax.nn.sigmoid(gate)
        g = g_ref[:, cols].astype(F32)
        grad_y = g * act_ref[j]
        grad_low = grad_y.astype(BF16)
        zero = jnp.zeros_like(x_pair)
        x0, x1 = jnp.where(first, x_pair, zero), jnp.where(first, zero, x_pair)
        y0, y1 = jnp.where(first, grad_low, zero), jnp.where(first, zero, grad_low)
        log0, log1 = pair_columns(log_ref, j)
        dt0, dt1 = pair_columns(dt_ref, j)
        mask = mask_ref[...]
        decay0 = jnp.exp(log0 - logt_ref[pl.ds(2 * j, 1), :] + mask) * dtt_ref[pl.ds(2 * j, 1), :]
        decay1 = jnp.exp(log1 - logt_ref[pl.ds(2 * j + 1, 1), :] + mask) * dtt_ref[pl.ds(2 * j + 1, 1), :]
        mix0 = (decay0 * scores).astype(BF16)
        mix1 = (decay1 * scores).astype(BF16)
        acc_scores[...] += dot(y0, x_pair, NT) * decay0 + dot(y1, x_pair, NT) * decay1
        log_pair = jnp.where(first, log0, log1)
        entry = jnp.exp(log_pair + first_ref[...])
        s0t = s0t_ref[j]
        y = dot(mix0, x0) + dot(mix1, x1) + entry * dot(c_low, s0t)
        acc_c[...] += dot((entry * grad_y).astype(BF16), s0t, NT)
        inner = dot(mix0, y0, TN) + dot(mix1, y1, TN)
        weights[j] = jnp.exp(log_pair[-1:, :] - log_pair + kept_ref[...]) * jnp.where(first, dt0, dt1)
        x_inner = x_f * inner
        acc_y[...] += heads_of(grad_low.astype(F32) * y - x_inner, j)
        acc_x[...] += heads_of(x_inner, j)
        skip = pltpu.roll(small[16:24, :], lax.rem(LANES - 2 * j, LANES), 1)
        skip = by_half(skip[0:1, 0:1], skip[0:1, 1:2])
        slope = sig * (1.0 + gate * (1.0 - sig))
        gate_grad_ref[:, cols] = (g * (y + skip * x_f) * slope).astype(BF16)
        base[j] = inner + skip * grad_y

    each(half, before, UNROLL)

    all_here(chip_passes.at[pl.ds(0, n_chip - 1)], pass_sems.at[3], near)

    def back_copy(k):
        return remote(
            back.at[k], exits.at[chip], send_sems.at[1], back_recv.at[chip], {"seg": k * 2 + core}
        )

    def scan(step, carry):
        k = n_chip - 1 - step

        @pl.when(k != chip)
        def _():
            all_here(got.at[k], recv.at[k], near)

        back[k] = carry.astype(BF16)

        @pl.when(k != chip)
        def _():
            back_copy(k).start()

        return got[k].astype(F32) + pass_row(chip_passes[k], core * half + chip) * carry

    lax.fori_loop(0, n_chip, scan, jnp.zeros((state, LANES), F32))
    exits[chip] = back[chip]
    each(half, lambda j: before(half + j), UNROLL)
    c_grad = acc_c[...] + dot(acc_scores[...], bf_ref[...], precision=HIGH)
    dproj_ref[0] = c_grad.astype(BF16)
    acc_b[...] += dot(acc_scores[...].T, cf_ref[...], precision=HIGH)

    @pl.when(pipe == 1)
    def _():
        later_copy(0).start()

    def tiles_of(i):
        return pl.ds(i, 1 + i)

    def dp_copy(i, k):
        return remote(
            dproj_ref.at[tiles_of(i)], grads.at[core, dp, tiles_of(i)],
            grad_sems.at[0, i], dp_recv.at[i, k], near.dp_device(k),
        )

    def grad_swap(i, slot):
        block = grads.at[core, slot, tiles_of(i)]
        return remote(block, block, grad_sems.at[1, i], grad_recv.at[i], near.sibling())

    def share(i):
        each(n_dp - 1, lambda k: dp_copy(i, k).start())
        grads[core, dp, tiles_of(i)] = dproj_ref[tiles_of(i)]
        grad_swap(i, dp).start()

    share(0)
    gate_copy = pltpu.make_async_copy(gate_grad_ref, gate_out, out_sems.at[0])
    gate_copy.start()

    def other_copy(c, j):
        return remote(
            other.at[j], adj_ref.at[core * half + j], core_sems.at[1], other_recv.at[c], near.sibling()
        )

    def finish(c, j):
        @pl.when(j != chip)
        def _():
            all_here(exits.at[j], back_recv.at[j], near)

        after = exits[j].astype(F32)
        earlier = both[1, j].astype(F32) + pass_row(passes[1], core * half + j) * after
        is_later = core == 1
        adj_ref[core * half + j] = jnp.where(is_later, after, earlier).astype(BF16)
        other[j] = jnp.where(is_later, earlier, after).astype(BF16)
        other_copy(c, j).start()

    def near_first(i):
        x_off = i - i // 2 * 2
        m = i // 2
        odd = m - m // 2 * 2
        z_off = odd * ((m + 1) // 2) - (1 - odd) * (m // 2)
        ring = n_chip // 2
        my_x = chip // ring
        z = lax.rem(chip - my_x * ring + z_off + ring, ring)
        return lax.rem(my_x + x_off, 2) * ring + z

    def after_scan(pairs):
        def lined(tiles):
            return jnp.concatenate(tiles, axis=1)

        adj = lined([adj_ref[j] for j in pairs])
        weight = lined([weights[j] for j in pairs])
        x_f = lined([xs_ref[:, tile_at(j)] for j in pairs]).astype(F32)
        outer = weight * dot(b_low, adj)
        acc_b[...] += dot((x_f * weight).astype(BF16), adj, NT)
        lane, row = iota(1), (iota(0) >= LANES // 2).astype(jnp.int32)
        select = jnp.concatenate([(lane == 2 * j + row).astype(BF16) for j in pairs], axis=0)
        high, low = split_two(x_f * outer)
        acc_s[...] += dot(high, select) + dot(low, select)
        last = lined([pass_row(passes[core], j) for j in pairs])
        s0t = lined([s0t_ref[j] for j in pairs])
        passed = last * jnp.sum(adj.astype(F32) * s0t.astype(F32), axis=0, keepdims=True)
        high, low = split_two(jnp.broadcast_to(passed, (8, passed.shape[1])))
        acc_a[...] += dot(high, select) + dot(low, select)
        for i, j in enumerate(pairs):
            mixed_grad_ref[:, tile_at(j)] = (base[j] + outer[:, i * LANES : (i + 1) * LANES]).astype(BF16)

    def mine_group(c):
        slots = [near_first(c * group + i) for i in range(group)]
        for slot in slots:
            finish(c, slot)
        after_scan([core * half + slot for slot in slots])

    def other_group(c):
        slots = [near_first(c * group + i) for i in range(group)]
        all_here(other.at[pl.ds(0, group)], other_recv.at[c], near)
        after_scan([(1 - core) * half + slot for slot in slots])

    each(n_chip // group, mine_group)
    each(n_chip // group, other_group)

    u = acc_x[...] + acc_s[...]
    last = jnp.sum(acc_s[...], axis=0, keepdims=True) + acc_a[0:1, :]
    upper = (iota(0) <= iota(1)).astype(F32)
    log_grad = dot(upper, acc_y[...] - acc_s[...], precision=HIGH) + last
    raw_grad = u * rho_ref[...] - small[0:1, :] * log_grad * sig_ref[...]
    dproj_ref[1] = acc_b[...].astype(BF16)
    dproj_ref[2] = raw_grad.astype(BF16)

    @pl.when(pipe == 1)
    def _():
        later_copy(1).start()

    share(1)
    mixed_copy = pltpu.make_async_copy(mixed_grad_ref, mixed_out, out_sems.at[1])
    mixed_copy.start()
    all_here(group_ref.at[pl.ds(0, n_dp - 1)], xg_sems.at[1], near)

    def gathered(i):
        for k in range(n_dp - 1):
            dp_copy(i, k).wait_recv()
            grad_swap(i, lax.rem(dp + 2 * n_dp - 1 - k, n_dp)).start()

    def summed_over(c, tile):
        x = jnp.concatenate([group_ref[k, c].reshape(-1, rows) for k in range(n_dp)], axis=1)
        return dot(x, jnp.concatenate([grads[c, k, tile] for k in range(n_dp)], axis=0))

    def whole_tiles(i):
        for tile in range(i, 1 + 2 * i):
            whole[tile] = summed_over(core, tile)
        all_here(grads.at[1 - core, :, tiles_of(i)], grad_recv.at[i], near)
        for tile in range(i, 1 + 2 * i):
            whole[tile] += summed_over(1 - core, tile)

    def rows_of(slot):
        return pl.ds(pl.multiple_of(slot * piece, piece), piece)

    def c_rows(slot):
        return whole[0, rows_of(slot)]

    def other_rows(slot):
        return jnp.concatenate([whole[1, rows_of(slot)], beside(whole[2, rows_of(slot)])], axis=0)

    def sum_copy(i, k, part, arrived):
        return remote(
            part.at[near.chip_slot(k)], arrived.at[k], grad_sems.at[2, i], grad_sems.at[3, i],
            near.chip_device(k),
        )

    def ship(i, rows_at, part, arrived):
        def one(k):
            slot = near.chip_slot(k)
            part[slot] = rows_at(slot).astype(BF16)
            sum_copy(i, k, part, arrived).start()

        each(n_chip - 1, one)

    gathered(0)
    whole_tiles(0)
    ship(0, c_rows, part_c, arrived_c)
    dt_low = lanes_turned(dproj_ref[2])

    def give(k):
        for c in range(2):
            cols = tile_at(2 * k + c)
            sent = back_projected(dproj_ref, dt_low, own_ref, k, c, piece)
            input_grad_ref[:, cols] = (g_ref[:, cols].astype(F32) + sent).astype(BF16)

    each(n_chip, give, 2)
    input_copy = pltpu.make_async_copy(input_grad_ref, input_out, out_sems.at[2])
    input_copy.start()

    gathered(1)
    whole_tiles(1)
    ship(1, other_rows, part_o, arrived_o)

    @pl.when(pipe == 1)
    def _():
        shard_copy.wait_send()
        later_copy(0).wait_send()
        later_copy(1).wait_send()

    gather.sent()
    first_chips = pl.ds(0, n_chip - 1)
    all_sent(chip_passes.at[first_chips], pass_sems.at[2], near)
    all_sent(both.at[core], core_sems.at[0], near)
    all_sent(total.at[first_chips], send_sems.at[0], near)
    all_sent(back.at[first_chips], send_sems.at[1], near)
    all_sent(other, core_sems.at[1], near)
    all_sent(group_ref.at[pl.ds(0, n_dp - 1)], xg_sems.at[0], near)
    for i in range(2):
        all_sent(grads.at[core, pl.ds(0, n_dp - 1), tiles_of(i)], grad_sems.at[0, i], near)
        all_sent(grads.at[core, :, tiles_of(i)], grad_sems.at[1, i], near)

    def collected(i, rows_at, arrived):
        all_here(arrived, grad_sems.at[3, i], near)
        total_rows = rows_at(chip)
        for k in range(n_chip - 1):
            total_rows += arrived[k].astype(F32)
        return total_rows

    weight_out[:, LANES : 2 * LANES] = collected(0, c_rows, arrived_c)
    others = collected(1, other_rows, arrived_o)
    weight_out[:, :LANES] = others[:piece]
    weight_out[:, 2 * LANES :] = below(others[piece:])[:, : cols_w - 2 * LANES]
    all_sent(arrived_c, grad_sems.at[2, 0], near)
    all_sent(arrived_o, grad_sems.at[2, 1], near)
    gate_copy.wait()
    mixed_copy.wait()
    input_copy.wait()


def layer_grads(shard, x, mixed, gate, out_grad, s0, rate, bias, skip, docs, n_chip, n_dp):
    rows, width = x.shape
    pairs = width // LANES
    state = s0.shape[1]
    piece, cols = shard.shape
    proj = cols + -cols % LANES
    dma = pltpu.SemaphoreType.DMA
    line = jax.ShapeDtypeStruct((rows, width), BF16)
    whole_line = pltpu.VMEM((rows, width), BF16)
    square = pltpu.VMEM((rows, LANES), F32)
    packed_rows = 2 * piece + piece // 2
    full_w = pltpu.VMEM((n_chip, 2, n_dp, packed_rows, LANES), BF16)
    wide = pltpu.VMEM((pairs, rows, LANES), F32)
    tiles = pltpu.VMEM((proj // LANES, rows, LANES), BF16)
    plain = pltpu.VMEM((n_chip, state, LANES), BF16)
    anywhere = pl.BlockSpec(memory_space=pl.ANY)
    chips = dma((n_chip,))
    return pl.pallas_call(
        functools.partial(layer_kernel, n_chip, n_dp),
        out_shape=(line, line, line, jax.ShapeDtypeStruct((piece, cols), F32)),
        in_specs=[VMEM] + [anywhere] * 5 + [VMEM] * 3 + [SMEM],
        out_specs=(anywhere, anywhere, anywhere, VMEM),
        scratch_shapes=[
            whole_line, whole_line, whole_line, whole_line,
            pltpu.VMEM((width, state), F32),
            pltpu.VMEM((packed_rows, LANES), BF16),
            full_w,
            pltpu.VMEM((packed_rows, LANES), BF16),
            full_w,
            tiles,
            pltpu.VMEM((pairs, state, LANES), BF16),
            pltpu.VMEM((n_chip, 2, LANES, rows), BF16),
            pltpu.VMEM((n_chip, LANES, rows), BF16),
            pltpu.VMEM((n_dp, 2, n_chip, piece, rows), BF16),
            wide, wide,
            pltpu.VMEM((rows, proj + LANES), F32),
        ]
        + [square] * 11
        + [
            pltpu.VMEM((24, LANES), F32),
            pltpu.VMEM((pairs, state, LANES), BF16),
            pltpu.VMEM((2, n_chip, state, LANES), BF16),
            plain, plain, plain, plain, plain,
            pltpu.VMEM((pairs, state, LANES), BF16),
            wide,
            tiles,
            pltpu.VMEM((2, 8, LANES), F32),
            pltpu.VMEM((n_chip, 8, LANES), F32),
            whole_line, whole_line, whole_line,
        ]
        + [square] * 6
        + [
            pltpu.VMEM((8, LANES), F32),
            pltpu.VMEM((2, n_dp, proj // LANES, rows, LANES), BF16),
            pltpu.VMEM((n_chip, piece, LANES), BF16),
            pltpu.VMEM((n_chip, packed_rows - piece, LANES), BF16),
            pltpu.VMEM((proj // LANES, n_chip * piece, LANES), F32),
            pltpu.VMEM((n_chip - 1, piece, LANES), BF16),
            pltpu.VMEM((n_chip - 1, packed_rows - piece, LANES), BF16),
            pltpu.VMEM((piece, proj), F32),
            (
                dma((5,)), dma((3,)), gather_sems(n_chip, n_dp), dma((6,)), dma((2,)), dma((2, 2)), dma((4,)),
                dma((2,)), dma((n_chip // 2,)), dma((2,)), chips, chips, dma((n_chip // GROUP,)), dma((2,)),
                dma((2,)), dma((2, n_dp - 1)), dma((4, 2)), dma((2,)),
            ),
        ],
        compiler_params=pltpu.CompilerParams(
            collective_id=1, has_side_effects=True, vmem_limit_bytes=VMEM_BYTES
        ),
    )(shard, x, mixed, gate, out_grad, s0, rate, bias, skip, docs)


def deliver_kernel(cuts, *refs):
    count = len(cuts)
    held, sems = refs[2 * count : 3 * count], refs[-1]
    steps = []
    for i, cut in enumerate(cuts):
        size = held[i].shape[0] // cut
        for k in range(cut):
            rows = pl.ds(k * size, size)
            at = len(steps)
            load = pltpu.make_async_copy(refs[i].at[rows], held[i].at[rows], sems.at[0, at])
            store = pltpu.make_async_copy(held[i].at[rows], refs[count + i].at[rows], sems.at[1, at])
            steps.append((load, store))
    for load, _ in steps:
        load.start()
    for load, store in steps:
        load.wait()
        store.start()
    for _, store in steps:
        store.wait()


def deliver(values):
    anywhere = pl.BlockSpec(memory_space=pl.ANY)
    cuts = [2 if value.dtype == BF16 else 1 for value in values]
    return pl.pallas_call(
        functools.partial(deliver_kernel, cuts),
        out_shape=tuple(jax.ShapeDtypeStruct(value.shape, value.dtype) for value in values),
        in_specs=[anywhere] * len(values),
        out_specs=(anywhere,) * len(values),
        scratch_shapes=[pltpu.VMEM(value.shape, value.dtype) for value in values]
        + [pltpu.SemaphoreType.DMA((2, sum(cuts)))],
    )(*values)


def local(
    inputs, mixed, gate_in, entry_states, out_grad, doc_lengths, proj_weight, decay_rate, dt_bias, skip_gain
):
    n_chip = lax.axis_size("seg") // 2
    n_dp = lax.axis_size("dp")
    width = inputs.shape[-1]
    s0 = entry_states.reshape(width, entry_states.shape[-1])
    outs = layer_grads(
        proj_weight[0], inputs[0, 0], mixed[0, 0], gate_in[0, 0], out_grad[0], s0,
        decay_rate, dt_bias, skip_gain, doc_lengths, n_chip, n_dp,
    )
    input_grad, mixed_grad, gate_grad, weight_grad = deliver(outs)
    return (
        input_grad[None, None],
        mixed_grad[None, None],
        gate_grad[None, None],
        weight_grad[None],
    )


def solution(mesh):
    in_specs = (
        P("pipe", "dp", "seg", None),
        P("pipe", "dp", "seg", None),
        P("pipe", "dp", "seg", None),
        P("pipe", "dp", "seg", None, None, None),
        P("dp", "seg", None),
        P("dp", None),
        P("pipe", ("seg", "dp"), None),
        P("pipe", None),
        P("pipe", None),
        P("pipe", None),
    )
    out_specs = (
        P("pipe", "dp", "seg", None),
        P("pipe", "dp", "seg", None),
        P("pipe", "dp", "seg", None),
        P("pipe", ("seg", "dp"), None),
    )
    return jax.shard_map(local, mesh=mesh, in_specs=in_specs, out_specs=out_specs, check_vma=False)
```

```python
import functools

import jax
import jax.numpy as jnp
from jax import lax
from jax.experimental import pallas as pl
from jax.experimental.pallas import tpu as pltpu
from jax.sharding import PartitionSpec as P

MESH = pl.DeviceIdType.MESH
F32 = jnp.float32
BF16 = jnp.bfloat16
HIGH = lax.Precision.HIGHEST
LANES = 128
NEG = -1e30
UNROLL = 4
GROUP = 4
VMEM_BYTES = 56 * 1024 * 1024
VMEM = pl.BlockSpec(memory_space=pltpu.VMEM)
SMEM = pl.BlockSpec(memory_space=pltpu.SMEM)
NN = (((1,), (0,)), ((), ()))
NT = (((1,), (1,)), ((), ()))
TN = (((0,), (0,)), ((), ()))


def dot(a, b, dims=NN, precision=None):
    return lax.dot_general(a, b, dims, precision=precision, preferred_element_type=F32)


def iota(axis, shape=(LANES, LANES)):
    return lax.broadcasted_iota(jnp.int32, shape, axis)


def tile_at(j):
    return pl.ds(pl.multiple_of(j * LANES, LANES), LANES)


def split_two(value):
    high = value.astype(BF16)
    low = (value - high.astype(F32)).astype(BF16)
    return high, low


def place():
    seg = lax.axis_index("seg")
    chip = seg // 2
    core = seg - 2 * chip
    return lax.axis_index("pipe"), seg, chip, core, lax.axis_index("dp")


def greet(devices):
    barrier = pltpu.get_barrier_semaphore()
    for count, device_of in devices:
        for k in range(count):
            pl.semaphore_signal(barrier, inc=1, device_id=device_of(k), device_id_type=MESH)
    return lambda: pl.semaphore_wait(barrier, sum(count for count, _ in devices))


def remote(src, dst, send_sem, recv_sem, device):
    return pltpu.make_async_remote_copy(
        src_ref=src, dst_ref=dst, send_sem=send_sem, recv_sem=recv_sem,
        device_id=device, device_id_type=MESH,
    )


def each(count, body, unroll=1):
    def step(k, carry):
        body(k)
        return carry

    lax.fori_loop(0, count, step, 0, unroll=unroll)


class Around:
    def __init__(self, n_chip, n_dp):
        self.n_chip, self.n_dp = n_chip, n_dp
        self.pipe, self.seg, self.chip, self.core, self.dp = place()

    def chip_slot(self, k):
        return lax.rem(self.chip + 1 + k, self.n_chip)

    def chip_device(self, k):
        return {"seg": self.chip_slot(k) * 2 + self.core}

    def dp_slot(self, k):
        return lax.rem(self.dp + 1 + k, self.n_dp)

    def dp_device(self, k):
        return {"dp": self.dp_slot(k)}

    def dp_at(self, way):
        return {"dp": lax.rem(self.dp + way + self.n_dp, self.n_dp)}

    def sibling(self, k=0):
        return {"seg": self.seg + 1 - 2 * self.core}

    def partner(self, k=0):
        return {"pipe": 1 - self.pipe}

    def greet(self):
        return greet(
            [(self.n_chip - 1, self.chip_device), (self.n_dp - 1, self.dp_device), (1, self.sibling), (1, self.partner)]
        )


class Gather:
    def __init__(self, near, dst, sems):
        self.near, self.dst = near, dst
        self.sends, self.chip_recv, self.side_recv, self.far_recv, self.core_recv = sems

    def source(self, k):
        near = self.near
        return lax.rem(near.chip + 2 * near.n_chip - 1 - k, near.n_chip)

    def chip_copy(self, k):
        near = self.near
        block = self.dst.at[near.chip, near.core, near.dp]
        return remote(block, block, self.sends.at[0], self.chip_recv.at[k], near.chip_device(k))

    def side_copy(self, k, i):
        near = self.near
        block = self.dst.at[self.source(k), near.core, near.dp]
        return remote(block, block, self.sends.at[1], self.side_recv.at[k, i], near.dp_at(1 if i == 0 else -1))

    def far_copy(self, k):
        near = self.near
        way = 1 - 2 * (k - k // 2 * 2)
        block = self.dst.at[self.source(k), near.core, lax.rem(near.dp + near.n_dp - way, near.n_dp)]
        return remote(block, block, self.sends.at[2], self.far_recv.at[k], near.dp_at(way))

    def core_copy(self, c, k):
        block = self.dst.at[self.source(k), self.near.core]
        return remote(block, block, self.sends.at[3], self.core_recv.at[c], self.near.sibling())

    def turn(self, step):
        return lax.rem(step + self.near.n_chip - 1, self.near.n_chip)

    def start(self, src):
        near = self.near
        self.dst[near.chip, near.core, near.dp] = src[...]
        each(near.n_chip - 1, lambda k: self.chip_copy(k).start())
        for i in range(2):
            self.side_copy(near.n_chip - 1, i).start()

    def spread(self):
        def pass_on(k):
            self.chip_copy(k).wait_recv()
            for i in range(2):
                self.side_copy(k, i).start()

        each(self.near.n_chip - 1, pass_on)

        def further(k):
            odd = k - k // 2 * 2
            block = self.dst.at[0, 0, 0]
            remote(block, block, self.sends.at[1], self.side_recv.at[k, odd], self.near.dp_at(1)).wait_recv()
            self.far_copy(k).start()

        each(self.near.n_chip, lambda step: further(self.turn(step)))

    def over(self, use):
        def pass_on(c):
            turns = [self.turn(c * GROUP + i) for i in range(GROUP)]
            block = self.dst.at[0, 0, 0]
            for k in turns:
                odd = k - k // 2 * 2
                all_here(block, self.side_recv.at[k, 1 - odd], self.near)
                all_here(block, self.far_recv.at[k], self.near)
                self.core_copy(c, k).start()
            use([self.source(k) for k in turns], self.near.core)

        each(self.near.n_chip // GROUP, pass_on)

    def end(self, use):
        def take(c):
            all_here(self.dst.at[pl.ds(0, GROUP), self.near.core], self.core_recv.at[c], self.near)
            use([self.source(self.turn(c * GROUP + i)) for i in range(GROUP)], 1 - self.near.core)

        each(self.near.n_chip // GROUP, take)

    def sent(self):
        near, dst = self.near, self.dst
        regions = (
            dst.at[pl.ds(0, near.n_chip - 1), near.core, near.dp],
            dst.at[:, near.core, pl.ds(0, 2)],
            dst.at[:, near.core, near.dp],
            dst.at[:, near.core],
        )
        for i, region in enumerate(regions):
            all_sent(region, self.sends.at[i], near)


def gather_sems(n_chip, n_dp):
    assert n_dp == 4
    dma = pltpu.SemaphoreType.DMA
    return (dma((4,)), dma((n_chip - 1,)), dma((n_chip, 2)), dma((n_chip,)), dma((n_chip // GROUP,)))


def all_sent(region, sem, near):
    remote(region, region, sem, sem, near.sibling()).wait_send()


def all_here(region, sem, near):
    remote(region, region, sem, sem, near.sibling()).wait_recv()


class LateGather:
    def __init__(self, near, dst, sems):
        self.near, self.dst, self.sems = near, dst, sems

    def run(self, src):
        near, dst, sems = self.near, self.dst, self.sems
        dst[near.chip, near.core, near.dp] = src[...]
        block = dst.at[near.chip, near.core, near.dp]
        chips = dst.at[pl.ds(0, near.n_chip - 1), near.core, near.dp]
        column = dst.at[:, near.core, near.dp]
        columns = dst.at[:, near.core, pl.ds(0, near.n_dp - 1)]
        side = dst.at[:, near.core]
        each(near.n_chip - 1, lambda k: remote(block, block, sems.at[0], sems.at[1], near.chip_device(k)).start())
        all_here(chips, sems.at[1], near)
        each(near.n_dp - 1, lambda k: remote(column, column, sems.at[2], sems.at[3], near.dp_device(k)).start())
        all_here(columns, sems.at[3], near)
        last = remote(side, side, sems.at[4], sems.at[5], near.sibling())
        last.start()
        last.wait()
        all_sent(chips, sems.at[0], near)
        all_sent(columns, sems.at[2], near)


def beside(tail):
    half = tail.shape[0] // 2
    return tail[:half] + pltpu.roll(tail[half:], LANES // 2, 1)


def below(value):
    first = iota(1, (1, LANES)) < LANES // 2
    top = jnp.where(first, value, 0.0)
    low = jnp.where(first, pltpu.roll(value, LANES // 2, 1), 0.0)
    return jnp.concatenate([top, low], axis=0)


def packed(value):
    tail = beside(value[:, 2 * LANES :])
    return jnp.concatenate([value[:, :LANES], value[:, LANES : 2 * LANES], tail], axis=0)


def weight_tiles(ref, chip, core, piece):
    block = ref[chip, core]
    tail = block[:, 2 * piece :]
    return (
        block[:, :piece].reshape(-1, LANES),
        block[:, piece : 2 * piece].reshape(-1, LANES),
        jnp.concatenate([tail, tail], axis=1).reshape(-1, LANES),
    )


def in_top(piece):
    lane = iota(1, (1, LANES))
    return lane - lane // piece * piece < piece // 2


def back_projected(dproj_ref, dt_low, ref, chip, core, piece):
    w_b, w_c, w_t = weight_tiles(ref, chip, core, piece)
    plain = dot(dproj_ref[1], w_b, NT) + dot(dproj_ref[0], w_c, NT)
    top = dot(dproj_ref[2], w_t, NT)
    low = dot(dt_low, w_t, NT)
    return plain + jnp.where(in_top(piece), top, low)


def lanes_turned(value):
    return pltpu.roll(value.astype(F32), LANES // 2, 1).astype(BF16)


def pair_columns(ref, j):
    turned = pltpu.roll(ref[...], lax.rem(LANES - 2 * j, LANES), 1)
    shape = (turned.shape[0], LANES)
    return jnp.broadcast_to(turned[:, 0:1], shape), jnp.broadcast_to(turned[:, 1:2], shape)


def by_half(first, second):
    return jnp.where(iota(1, (1, LANES)) < LANES // 2, first, second)


def heads_of(value, j):
    select = (iota(1) == 2 * j + (iota(0) >= LANES // 2).astype(jnp.int32)).astype(BF16)
    high, low = split_two(value)
    return dot(high, select) + dot(low, select)


def layer_kernel(n_chip, n_dp, *refs):
    (
        shard_ref, x_hbm, mixed_hbm, gate_hbm, out_grad_hbm, s0_hbm, rate_ref, bias_ref, skip_ref, doc_ref,
        input_out, mixed_out, gate_out, weight_out,
        x_ref, xs_ref, gate_ref, g_ref, s0_ref, shard, own_ref, one_shard, one_ref, later,
        s0t_ref, xt_ref, x_stage, group_ref, act_ref, weights, projected, bf_ref, cf_ref,
        log_ref, logt_ref, dt_ref, dtt_ref, sig_ref, rho_ref, mask_ref, first_ref, kept_ref, small,
        msg, both, total, got, back, exits, other, adj_ref, base, dproj_ref, passes, chip_passes,
        input_grad_ref, mixed_grad_ref, gate_grad_ref,
        acc_scores, acc_b, acc_c, acc_y, acc_x, acc_s, acc_a, grads, part_c, part_o, whole, arrived_c, arrived_o, spare, sems,
    ) = refs
    (
        in_sems, out_sems, own_set, one_set, shard_sems, later_sems, pass_sems, core_sems, core_recv,
        send_sems, recv, back_recv, other_recv, xt_sems, xg_sems, dp_recv, grad_sems, grad_recv, sum_sems,
    ) = sems
    rows, width = x_ref.shape
    state = bf_ref.shape[1]
    heads = rate_ref.shape[1]
    cols_w = shard_ref.shape[1]
    piece = shard_ref.shape[0]
    proj = projected.shape[1]
    half = n_chip

    near = Around(n_chip, n_dp)
    pipe, chip, core, dp = near.pipe, near.chip, near.core, near.dp
    all_met = near.greet()
    loads = [
        pltpu.make_async_copy(src, dst, in_sems.at[i])
        for i, (src, dst) in enumerate(
            ((gate_hbm, gate_ref), (s0_hbm, s0_ref), (x_hbm, x_ref), (out_grad_hbm, g_ref), (mixed_hbm, xs_ref))
        )
    ]
    for load in loads:
        load.start()
    spare[...] = jnp.zeros_like(spare)
    spare[:, :cols_w] = shard_ref[...].astype(F32)
    shard[...] = packed(spare[...]).astype(BF16)

    all_met()
    shard_copy = remote(shard, one_shard, shard_sems.at[0], shard_sems.at[1], near.partner())

    def later_copy(i):
        return remote(
            dproj_ref.at[i], later.at[i], later_sems.at[0, i], later_sems.at[1, i], near.partner()
        )


    gather = Gather(near, own_ref, own_set)
    gather.start(shard)

    @pl.when(pipe == 1)
    def _():
        shard_copy.start()

    for ref in (acc_scores, acc_b, acc_c, acc_y, acc_x, acc_s, acc_a, small, projected):
        ref[...] = jnp.zeros_like(ref)
    small[0:1, :heads] = rate_ref[...]
    small[8:9, :heads] = bias_ref[...]
    small[16:17, :heads] = skip_ref[...]
    begin = near.seg * rows
    count_t = jnp.zeros((rows, rows), jnp.int32)
    count_s = jnp.zeros((rows, rows), jnp.int32)
    count_last = jnp.zeros((rows, rows), jnp.int32)
    start = jnp.int32(0)
    for k in range(doc_ref.shape[1] - 1):
        start = start + doc_ref[0, k]
        offset = jnp.broadcast_to(start - begin, (rows, rows))
        inside = offset >= 0
        count_t += (inside & (iota(0) >= offset)).astype(jnp.int32)
        count_s += (inside & (iota(1) >= offset)).astype(jnp.int32)
        count_last += (inside & (offset <= rows - 1)).astype(jnp.int32)
    allowed = (iota(0) >= iota(1)) & (count_t == count_s)
    mask_ref[...] = jnp.where(allowed, 0.0, NEG)
    first_ref[...] = jnp.where(count_t == 0, 0.0, NEG)
    kept_ref[...] = jnp.where(count_t == count_last, 0.0, NEG)

    def activate(j):
        gate = gate_ref[:, tile_at(j)].astype(F32)
        act_ref[j] = gate * jax.nn.sigmoid(gate)

    def turn_state(j):
        s0t_ref[j] = s0_ref[tile_at(j), :].T.astype(BF16)

    def turn_x(k):
        for c in range(2):
            xt_ref[k, c] = x_ref[:, tile_at(2 * k + c)].T

    loads[0].wait()
    each(2 * half, activate, UNROLL)
    gather.spread()
    loads[1].wait()
    each(2 * half, turn_state, UNROLL)
    loads[2].wait()
    each(n_chip, turn_x, 2)

    def project(chips, c):
        top = in_top(piece)
        x_tiles = [x_ref[:, tile_at(2 * k + c)] for k in chips]
        zero = jnp.zeros_like(x_tiles[0])
        w_b, w_c, w_t = [
            jnp.concatenate(column, axis=0)
            for column in zip(*[weight_tiles(own_ref, k, c, piece) for k in chips])
        ]

        def lined(tiles):
            return jnp.concatenate(tiles, axis=1)

        x_all = lined(x_tiles)
        projected[:, :LANES] += dot(x_all, w_b)
        projected[:, LANES : 2 * LANES] += dot(x_all, w_c)
        projected[:, 2 * LANES : 3 * LANES] += dot(lined([jnp.where(top, x, zero) for x in x_tiles]), w_t)
        projected[:, 3 * LANES :] += dot(lined([jnp.where(top, zero, x) for x in x_tiles]), w_t)

    gather.over(project)
    gather.end(project)
    xt_copy = remote(xt_ref.at[:, 1 - core], x_stage, xt_sems.at[0], xt_sems.at[1], near.sibling())
    xt_copy.start()
    bf_ref[...] = projected[:, :state]
    cf_ref[...] = projected[:, state : 2 * state]
    raw = projected[:, 2 * LANES : 3 * LANES] + pltpu.roll(projected[:, 3 * LANES :], LANES // 2, 1)
    raw = jnp.where(iota(1) < heads, raw, 0.0) + small[8:9, :]
    soft = jnp.maximum(raw, 0.0) + jnp.log1p(jnp.exp(-jnp.abs(raw)))
    sig = 1.0 / (1.0 + jnp.exp(-jnp.abs(raw)))
    sig = jnp.where(raw >= 0, sig, 1.0 - sig)
    tiny = raw < -15.0
    exp_raw = jnp.exp(jnp.minimum(raw, 0.0))
    sig = jnp.where(tiny, exp_raw, sig)
    soft = jnp.where(tiny, exp_raw, soft)
    sig_ref[...] = sig
    rho_ref[...] = jnp.where(tiny, 1.0, sig / jnp.where(tiny, 1.0, soft))
    lower = (iota(0) >= iota(1)).astype(F32)
    log = dot(lower, -soft * small[0:1, :], precision=HIGH)
    log_ref[...] = log
    logt_ref[...] = log.T
    dt_ref[...] = soft
    dtt_ref[...] = soft.T
    first = iota(1, (1, LANES)) < LANES // 2

    passes[core] = jnp.broadcast_to(jnp.exp(log[rows - 1 :] + first_ref[rows - 1 :, :]), (8, LANES))
    pass_copy = remote(passes.at[core], passes.at[core], pass_sems.at[0], pass_sems.at[1], near.sibling())
    pass_copy.start()

    def pass_row(value, j):
        turned = pltpu.roll(value, lax.rem(LANES - 2 * j, LANES), 1)
        return by_half(turned[0:1, 0:1], turned[0:1, 1:2])

    loads[3].wait()
    pass_copy.wait()
    chip_passes[chip] = passes[0] * passes[1]

    def chip_pass_copy(k):
        block = chip_passes.at[chip]
        return remote(block, block, pass_sems.at[2], pass_sems.at[3], near.chip_device(k))

    each(n_chip - 1, lambda k: chip_pass_copy(k).start())

    @pl.when(pipe == 0)
    def _():
        shard_copy.wait_recv()
        LateGather(near, one_ref, one_set).run(one_shard)
        later_copy(0).wait_recv()

        def first_part(k):
            for c in range(2):
                j = 2 * k + c
                w_c = one_ref[k, c, :, piece : 2 * piece].reshape(-1, LANES)
                base[j] = g_ref[:, tile_at(j)].astype(F32) + dot(later[0], w_c, NT)

        each(n_chip, first_part, 2)
        later_copy(1).wait_recv()
        later_copy(2).wait_recv()
        dt_low = lanes_turned(later[2])

        def recompute(k):
            for c in range(2):
                j = 2 * k + c
                w_b, _, w_t = weight_tiles(one_ref, k, c, piece)
                sent = base[j] + dot(later[1], w_b, NT)
                sent += jnp.where(in_top(piece), dot(later[2], w_t, NT), dot(dt_low, w_t, NT))
                g_ref[:, tile_at(j)] = sent.astype(BF16)

        each(n_chip, recompute, 2)

    ct = cf_ref[...].T.astype(BF16)

    def own(j):
        log0, log1 = pair_columns(log_ref, j)
        entry = jnp.exp(jnp.where(first, log0, log1) + first_ref[...])
        grad = (g_ref[:, tile_at(j)].astype(F32) * act_ref[j] * entry).astype(BF16)
        msg[j] = dot(ct, grad).astype(BF16)

    def swap_copy(c, slot):
        return remote(
            msg.at[(1 - core) * half + slot], both.at[core, slot],
            core_sems.at[0], core_recv.at[c], near.sibling(),
        )

    def combine(j):
        both[core, j] = msg[core * half + j]
        pass0 = pass_row(passes[0], core * half + j)
        total[j] = (both[0, j].astype(F32) + pass0 * both[1, j].astype(F32)).astype(BF16)

    def send_copy(k):
        return remote(
            total.at[near.chip_slot(k)], got.at[chip], send_sems.at[0], recv.at[chip], near.chip_device(k)
        )

    group = GROUP
    couple = 2

    def couple_slots(c):
        return [near.chip_slot(c * couple + i) for i in range(couple)]

    def own_theirs(c):
        slots = couple_slots(c)
        for slot in slots:
            own((1 - core) * half + slot)
        for slot in slots:
            swap_copy(c, slot).start()

    def own_mine(c, send_count):
        slots = couple_slots(c)
        for slot in slots:
            own(core * half + slot)
        all_here(both.at[core, pl.ds(0, couple)], core_recv.at[c], near)
        for slot in slots:
            combine(slot)
        for i in range(send_count):
            send_copy(c * couple + i).start()

    def own_step(c):
        own_theirs(c + 1)
        own_mine(c, couple)

    own_theirs(0)
    each(n_chip // couple - 1, own_step)
    own_mine(n_chip // couple - 1, couple - 1)
    got[chip] = total[chip]

    xt_copy.wait()

    def x_copy(k, src, from_core):
        cut = pl.ds(pl.multiple_of(near.dp_slot(k) * piece, piece), piece)
        return remote(
            src.at[:, cut], group_ref.at[dp, from_core],
            xg_sems.at[0], xg_sems.at[1], near.dp_device(k),
        )

    def x_start(k):
        x_copy(k, xt_ref.at[:, core], core).start()
        x_copy(k, x_stage, 1 - core).start()

    each(n_dp - 1, x_start)
    cut = pl.ds(pl.multiple_of(dp * piece, piece), piece)
    group_ref[dp, core] = xt_ref[:, core, cut]
    group_ref[dp, 1 - core] = x_stage[:, cut]

    loads[4].wait()
    scores = dot(cf_ref[...], bf_ref[...], NT, precision=HIGH)
    b_low = bf_ref[...].astype(BF16)
    c_low = cf_ref[...].astype(BF16)

    def before(j):
        cols = tile_at(j)
        x_pair = xs_ref[:, cols]
        x_f = x_pair.astype(F32)
        gate = gate_ref[:, cols].astype(F32)
        sig = jax.nn.sigmoid(gate)
        g = g_ref[:, cols].astype(F32)
        grad_y = g * act_ref[j]
        grad_low = grad_y.astype(BF16)
        zero = jnp.zeros_like(x_pair)
        x0, x1 = jnp.where(first, x_pair, zero), jnp.where(first, zero, x_pair)
        y0, y1 = jnp.where(first, grad_low, zero), jnp.where(first, zero, grad_low)
        log0, log1 = pair_columns(log_ref, j)
        dt0, dt1 = pair_columns(dt_ref, j)
        mask = mask_ref[...]
        decay0 = jnp.exp(log0 - logt_ref[pl.ds(2 * j, 1), :] + mask) * dtt_ref[pl.ds(2 * j, 1), :]
        decay1 = jnp.exp(log1 - logt_ref[pl.ds(2 * j + 1, 1), :] + mask) * dtt_ref[pl.ds(2 * j + 1, 1), :]
        mix0 = (decay0 * scores).astype(BF16)
        mix1 = (decay1 * scores).astype(BF16)
        acc_scores[...] += dot(y0, x_pair, NT) * decay0 + dot(y1, x_pair, NT) * decay1
        log_pair = jnp.where(first, log0, log1)
        entry = jnp.exp(log_pair + first_ref[...])
        s0t = s0t_ref[j]
        y = dot(mix0, x0) + dot(mix1, x1) + entry * dot(c_low, s0t)
        acc_c[...] += dot((entry * grad_y).astype(BF16), s0t, NT)
        inner = dot(mix0, y0, TN) + dot(mix1, y1, TN)
        weights[j] = jnp.exp(log_pair[-1:, :] - log_pair + kept_ref[...]) * jnp.where(first, dt0, dt1)
        x_inner = x_f * inner
        acc_y[...] += heads_of(grad_low.astype(F32) * y - x_inner, j)
        acc_x[...] += heads_of(x_inner, j)
        skip = pltpu.roll(small[16:24, :], lax.rem(LANES - 2 * j, LANES), 1)
        skip = by_half(skip[0:1, 0:1], skip[0:1, 1:2])
        slope = sig * (1.0 + gate * (1.0 - sig))
        gate_grad_ref[:, cols] = (g * (y + skip * x_f) * slope).astype(BF16)
        base[j] = inner + skip * grad_y

    early = 12
    each(early, before, UNROLL)

    all_here(chip_passes.at[pl.ds(0, n_chip - 1)], pass_sems.at[3], near)

    def back_copy(k):
        return remote(
            back.at[k], exits.at[chip], send_sems.at[1], back_recv.at[chip], {"seg": k * 2 + core}
        )

    def scan(step, carry):
        k = n_chip - 1 - step

        @pl.when(k != chip)
        def _():
            all_here(got.at[k], recv.at[k], near)

        back[k] = carry.astype(BF16)

        @pl.when(k != chip)
        def _():
            back_copy(k).start()

        return got[k].astype(F32) + pass_row(chip_passes[k], core * half + chip) * carry

    lax.fori_loop(0, n_chip, scan, jnp.zeros((state, LANES), F32))
    exits[chip] = back[chip]
    each(2 * half - early, lambda j: before(early + j), UNROLL)
    c_grad = acc_c[...] + dot(acc_scores[...], bf_ref[...], precision=HIGH)
    dproj_ref[0] = c_grad.astype(BF16)
    acc_b[...] += dot(acc_scores[...].T, cf_ref[...], precision=HIGH)

    @pl.when(pipe == 1)
    def _():
        later_copy(0).start()

    def dp_copy(i, k):
        return remote(
            dproj_ref.at[i], grads.at[core, dp, i],
            grad_sems.at[0, i], dp_recv.at[i, k], near.dp_device(k),
        )

    def grad_swap(i, slot):
        block = grads.at[core, slot, i]
        return remote(block, block, grad_sems.at[1, i], grad_recv.at[i], near.sibling())

    def share(i):
        each(n_dp - 1, lambda k: dp_copy(i, k).start())
        grads[core, dp, i] = dproj_ref[i]
        grad_swap(i, dp).start()

    share(0)
    gate_copy = pltpu.make_async_copy(gate_grad_ref, gate_out, out_sems.at[0])
    gate_copy.start()

    def other_copy(c, j):
        return remote(
            other.at[j], adj_ref.at[core * half + j], core_sems.at[1], other_recv.at[c], near.sibling()
        )

    def finish(c, j):
        @pl.when(j != chip)
        def _():
            all_here(exits.at[j], back_recv.at[j], near)

        after = exits[j].astype(F32)
        earlier = both[1, j].astype(F32) + pass_row(passes[1], core * half + j) * after
        is_later = core == 1
        adj_ref[core * half + j] = jnp.where(is_later, after, earlier).astype(BF16)
        other[j] = jnp.where(is_later, earlier, after).astype(BF16)
        other_copy(c, j).start()

    def near_first(i):
        x_off = i - i // 2 * 2
        m = i // 2
        odd = m - m // 2 * 2
        z_off = odd * ((m + 1) // 2) - (1 - odd) * (m // 2)
        ring = n_chip // 2
        my_x = chip // ring
        z = lax.rem(chip - my_x * ring + z_off + ring, ring)
        return lax.rem(my_x + x_off, 2) * ring + z

    def after_scan(pairs):
        def lined(tiles):
            return jnp.concatenate(tiles, axis=1)

        adj = lined([adj_ref[j] for j in pairs])
        weight = lined([weights[j] for j in pairs])
        x_f = lined([xs_ref[:, tile_at(j)] for j in pairs]).astype(F32)
        outer = weight * dot(b_low, adj)
        acc_b[...] += dot((x_f * weight).astype(BF16), adj, NT)
        lane, row = iota(1), (iota(0) >= LANES // 2).astype(jnp.int32)
        select = jnp.concatenate([(lane == 2 * j + row).astype(BF16) for j in pairs], axis=0)
        high, low = split_two(x_f * outer)
        acc_s[...] += dot(high, select) + dot(low, select)
        last = lined([pass_row(passes[core], j) for j in pairs])
        s0t = lined([s0t_ref[j] for j in pairs])
        passed = last * jnp.sum(adj.astype(F32) * s0t.astype(F32), axis=0, keepdims=True)
        high, low = split_two(jnp.broadcast_to(passed, (8, passed.shape[1])))
        acc_a[...] += dot(high, select) + dot(low, select)
        for i, j in enumerate(pairs):
            mixed_grad_ref[:, tile_at(j)] = (base[j] + outer[:, i * LANES : (i + 1) * LANES]).astype(BF16)

    def mine_group(c):
        slots = [near_first(c * group + i) for i in range(group)]
        for slot in slots:
            finish(c, slot)
        after_scan([core * half + slot for slot in slots])

    def other_group(c):
        slots = [near_first(c * group + i) for i in range(group)]
        all_here(other.at[pl.ds(0, group)], other_recv.at[c], near)
        after_scan([(1 - core) * half + slot for slot in slots])

    each(n_chip // group, mine_group)
    each(n_chip // group, other_group)

    dproj_ref[1] = acc_b[...].astype(BF16)

    @pl.when(pipe == 1)
    def _():
        later_copy(1).start()

    share(1)
    u = acc_x[...] + acc_s[...]
    last = jnp.sum(acc_s[...], axis=0, keepdims=True) + acc_a[0:1, :]
    upper = (iota(0) <= iota(1)).astype(F32)
    log_grad = dot(upper, acc_y[...] - acc_s[...], precision=HIGH) + last
    raw_grad = u * rho_ref[...] - small[0:1, :] * log_grad * sig_ref[...]
    dproj_ref[2] = raw_grad.astype(BF16)

    @pl.when(pipe == 1)
    def _():
        later_copy(2).start()

    share(2)

    mixed_copy = pltpu.make_async_copy(mixed_grad_ref, mixed_out, out_sems.at[1])
    mixed_copy.start()
    all_here(group_ref.at[pl.ds(0, n_dp - 1)], xg_sems.at[1], near)

    def gathered(i):
        for k in range(n_dp - 1):
            dp_copy(i, k).wait_recv()
            grad_swap(i, lax.rem(dp + 2 * n_dp - 1 - k, n_dp)).start()

    def summed_over(c, tile):
        x = jnp.concatenate([group_ref[k, c].reshape(-1, rows) for k in range(n_dp)], axis=1)
        return dot(x, jnp.concatenate([grads[c, k, tile] for k in range(n_dp)], axis=0))

    def whole_tile(i):
        whole[i] = summed_over(core, i)
        all_here(grads.at[1 - core, :, i], grad_recv.at[i], near)
        whole[i] += summed_over(1 - core, i)

    def rows_of(slot):
        return pl.ds(pl.multiple_of(slot * piece, piece), piece)

    def c_rows(slot):
        return whole[0, rows_of(slot)]

    def other_rows(slot):
        return jnp.concatenate([whole[1, rows_of(slot)], beside(whole[2, rows_of(slot)])], axis=0)

    def sum_copy(i, k, part, arrived):
        return remote(
            part.at[near.chip_slot(k)], arrived.at[k], sum_sems.at[0, i], sum_sems.at[1, i],
            near.chip_device(k),
        )

    def ship(i, rows_at, part, arrived):
        def one(k):
            slot = near.chip_slot(k)
            part[slot] = rows_at(slot).astype(BF16)
            sum_copy(i, k, part, arrived).start()

        each(n_chip - 1, one)

    gathered(0)
    whole_tile(0)
    ship(0, c_rows, part_c, arrived_c)
    dt_low = lanes_turned(dproj_ref[2])

    def give(k):
        for c in range(2):
            cols = tile_at(2 * k + c)
            sent = back_projected(dproj_ref, dt_low, own_ref, k, c, piece)
            input_grad_ref[:, cols] = (g_ref[:, cols].astype(F32) + sent).astype(BF16)

    each(n_chip, give, 2)
    input_copy = pltpu.make_async_copy(input_grad_ref, input_out, out_sems.at[2])
    input_copy.start()

    gathered(1)
    gathered(2)
    whole_tile(1)
    whole_tile(2)
    ship(1, other_rows, part_o, arrived_o)

    @pl.when(pipe == 1)
    def _():
        shard_copy.wait_send()
        for i in range(3):
            later_copy(i).wait_send()

    gather.sent()
    first_chips = pl.ds(0, n_chip - 1)
    all_sent(chip_passes.at[first_chips], pass_sems.at[2], near)
    all_sent(both.at[core], core_sems.at[0], near)
    all_sent(total.at[first_chips], send_sems.at[0], near)
    all_sent(back.at[first_chips], send_sems.at[1], near)
    all_sent(other, core_sems.at[1], near)
    all_sent(group_ref.at[pl.ds(0, n_dp - 1)], xg_sems.at[0], near)
    for i in range(3):
        all_sent(grads.at[core, pl.ds(0, n_dp - 1), i], grad_sems.at[0, i], near)
        all_sent(grads.at[core, :, i], grad_sems.at[1, i], near)

    def collected(i, rows_at, arrived):
        all_here(arrived, sum_sems.at[1, i], near)
        total_rows = rows_at(chip)
        for k in range(n_chip - 1):
            total_rows += arrived[k].astype(F32)
        return total_rows

    weight_out[:, LANES : 2 * LANES] = collected(0, c_rows, arrived_c)
    others = collected(1, other_rows, arrived_o)
    weight_out[:, :LANES] = others[:piece]
    weight_out[:, 2 * LANES :] = below(others[piece:])[:, : cols_w - 2 * LANES]
    all_sent(arrived_c, sum_sems.at[0, 0], near)
    all_sent(arrived_o, sum_sems.at[0, 1], near)
    gate_copy.wait()
    mixed_copy.wait()
    input_copy.wait()


def layer_grads(shard, x, mixed, gate, out_grad, s0, rate, bias, skip, docs, n_chip, n_dp):
    rows, width = x.shape
    pairs = width // LANES
    state = s0.shape[1]
    piece, cols = shard.shape
    proj = cols + -cols % LANES
    dma = pltpu.SemaphoreType.DMA
    line = jax.ShapeDtypeStruct((rows, width), BF16)
    whole_line = pltpu.VMEM((rows, width), BF16)
    square = pltpu.VMEM((rows, LANES), F32)
    packed_rows = 2 * piece + piece // 2
    full_w = pltpu.VMEM((n_chip, 2, n_dp, packed_rows, LANES), BF16)
    wide = pltpu.VMEM((pairs, rows, LANES), F32)
    tiles = pltpu.VMEM((proj // LANES, rows, LANES), BF16)
    plain = pltpu.VMEM((n_chip, state, LANES), BF16)
    anywhere = pl.BlockSpec(memory_space=pl.ANY)
    chips = dma((n_chip,))
    return pl.pallas_call(
        functools.partial(layer_kernel, n_chip, n_dp),
        out_shape=(line, line, line, jax.ShapeDtypeStruct((piece, cols), F32)),
        in_specs=[VMEM] + [anywhere] * 5 + [VMEM] * 3 + [SMEM],
        out_specs=(anywhere, anywhere, anywhere, VMEM),
        scratch_shapes=[
            whole_line, whole_line, whole_line, whole_line,
            pltpu.VMEM((width, state), F32),
            pltpu.VMEM((packed_rows, LANES), BF16),
            full_w,
            pltpu.VMEM((packed_rows, LANES), BF16),
            full_w,
            tiles,
            pltpu.VMEM((pairs, state, LANES), BF16),
            pltpu.VMEM((n_chip, 2, LANES, rows), BF16),
            pltpu.VMEM((n_chip, LANES, rows), BF16),
            pltpu.VMEM((n_dp, 2, n_chip, piece, rows), BF16),
            wide, wide,
            pltpu.VMEM((rows, proj + LANES), F32),
        ]
        + [square] * 11
        + [
            pltpu.VMEM((24, LANES), F32),
            pltpu.VMEM((pairs, state, LANES), BF16),
            pltpu.VMEM((2, n_chip, state, LANES), BF16),
            plain, plain, plain, plain, plain,
            pltpu.VMEM((pairs, state, LANES), BF16),
            wide,
            tiles,
            pltpu.VMEM((2, 8, LANES), F32),
            pltpu.VMEM((n_chip, 8, LANES), F32),
            whole_line, whole_line, whole_line,
        ]
        + [square] * 6
        + [
            pltpu.VMEM((8, LANES), F32),
            pltpu.VMEM((2, n_dp, proj // LANES, rows, LANES), BF16),
            pltpu.VMEM((n_chip, piece, LANES), BF16),
            pltpu.VMEM((n_chip, packed_rows - piece, LANES), BF16),
            pltpu.VMEM((proj // LANES, n_chip * piece, LANES), F32),
            pltpu.VMEM((n_chip - 1, piece, LANES), BF16),
            pltpu.VMEM((n_chip - 1, packed_rows - piece, LANES), BF16),
            pltpu.VMEM((piece, proj), F32),
            (
                dma((5,)), dma((3,)), gather_sems(n_chip, n_dp), dma((6,)), dma((2,)), dma((2, 3)), dma((4,)),
                dma((2,)), dma((n_chip // 2,)), dma((2,)), chips, chips, dma((n_chip // GROUP,)), dma((2,)),
                dma((2,)), dma((3, n_dp - 1)), dma((2, 3)), dma((3,)), dma((2, 2)),
            ),
        ],
        compiler_params=pltpu.CompilerParams(
            collective_id=1, has_side_effects=True, vmem_limit_bytes=VMEM_BYTES
        ),
    )(shard, x, mixed, gate, out_grad, s0, rate, bias, skip, docs)


def deliver_kernel(cuts, *refs):
    count = len(cuts)
    held, sems = refs[2 * count : 3 * count], refs[-1]
    steps = []
    for i, cut in enumerate(cuts):
        size = held[i].shape[0] // cut
        for k in range(cut):
            rows = pl.ds(k * size, size)
            at = len(steps)
            load = pltpu.make_async_copy(refs[i].at[rows], held[i].at[rows], sems.at[0, at])
            store = pltpu.make_async_copy(held[i].at[rows], refs[count + i].at[rows], sems.at[1, at])
            steps.append((load, store))
    for load, _ in steps:
        load.start()
    for load, store in steps:
        load.wait()
        store.start()
    for _, store in steps:
        store.wait()


def deliver(values):
    anywhere = pl.BlockSpec(memory_space=pl.ANY)
    cuts = [2 if value.dtype == BF16 else 1 for value in values]
    return pl.pallas_call(
        functools.partial(deliver_kernel, cuts),
        out_shape=tuple(jax.ShapeDtypeStruct(value.shape, value.dtype) for value in values),
        in_specs=[anywhere] * len(values),
        out_specs=(anywhere,) * len(values),
        scratch_shapes=[pltpu.VMEM(value.shape, value.dtype) for value in values]
        + [pltpu.SemaphoreType.DMA((2, sum(cuts)))],
    )(*values)


def local(
    inputs, mixed, gate_in, entry_states, out_grad, doc_lengths, proj_weight, decay_rate, dt_bias, skip_gain
):
    n_chip = lax.axis_size("seg") // 2
    n_dp = lax.axis_size("dp")
    width = inputs.shape[-1]
    s0 = entry_states.reshape(width, entry_states.shape[-1])
    outs = layer_grads(
        proj_weight[0], inputs[0, 0], mixed[0, 0], gate_in[0, 0], out_grad[0], s0,
        decay_rate, dt_bias, skip_gain, doc_lengths, n_chip, n_dp,
    )
    input_grad, mixed_grad, gate_grad, weight_grad = deliver(outs)
    return (
        input_grad[None, None],
        mixed_grad[None, None],
        gate_grad[None, None],
        weight_grad[None],
    )


def solution(mesh):
    in_specs = (
        P("pipe", "dp", "seg", None),
        P("pipe", "dp", "seg", None),
        P("pipe", "dp", "seg", None),
        P("pipe", "dp", "seg", None, None, None),
        P("dp", "seg", None),
        P("dp", None),
        P("pipe", ("seg", "dp"), None),
        P("pipe", None),
        P("pipe", None),
        P("pipe", None),
    )
    out_specs = (
        P("pipe", "dp", "seg", None),
        P("pipe", "dp", "seg", None),
        P("pipe", "dp", "seg", None),
        P("pipe", ("seg", "dp"), None),
    )
    return jax.shard_map(local, mesh=mesh, in_specs=in_specs, out_specs=out_specs, check_vma=False)
```

```python
import functools

import jax
import jax.numpy as jnp
from jax import lax
from jax.experimental import pallas as pl
from jax.experimental.pallas import tpu as pltpu
from jax.sharding import PartitionSpec as P

MESH = pl.DeviceIdType.MESH
F32 = jnp.float32
BF16 = jnp.bfloat16
HIGH = lax.Precision.HIGHEST
LANES = 128
NEG = -1e30
UNROLL = 4
GROUP = 4
VMEM_BYTES = 56 * 1024 * 1024
VMEM = pl.BlockSpec(memory_space=pltpu.VMEM)
SMEM = pl.BlockSpec(memory_space=pltpu.SMEM)
NN = (((1,), (0,)), ((), ()))
NT = (((1,), (1,)), ((), ()))
TN = (((0,), (0,)), ((), ()))


def dot(a, b, dims=NN, precision=None):
    return lax.dot_general(a, b, dims, precision=precision, preferred_element_type=F32)


def iota(axis, shape=(LANES, LANES)):
    return lax.broadcasted_iota(jnp.int32, shape, axis)


def tile_at(j):
    return pl.ds(pl.multiple_of(j * LANES, LANES), LANES)


def split_two(value):
    high = value.astype(BF16)
    low = (value - high.astype(F32)).astype(BF16)
    return high, low


def place():
    seg = lax.axis_index("seg")
    chip = seg // 2
    core = seg - 2 * chip
    return lax.axis_index("pipe"), seg, chip, core, lax.axis_index("dp")


def greet(devices):
    barrier = pltpu.get_barrier_semaphore()
    for count, device_of in devices:
        for k in range(count):
            pl.semaphore_signal(barrier, inc=1, device_id=device_of(k), device_id_type=MESH)
    return lambda: pl.semaphore_wait(barrier, sum(count for count, _ in devices))


def remote(src, dst, send_sem, recv_sem, device):
    return pltpu.make_async_remote_copy(
        src_ref=src, dst_ref=dst, send_sem=send_sem, recv_sem=recv_sem,
        device_id=device, device_id_type=MESH,
    )


def each(count, body, unroll=1):
    def step(k, carry):
        body(k)
        return carry

    lax.fori_loop(0, count, step, 0, unroll=unroll)


class Around:
    def __init__(self, n_chip, n_dp):
        self.n_chip, self.n_dp = n_chip, n_dp
        self.pipe, self.seg, self.chip, self.core, self.dp = place()

    def chip_slot(self, k):
        return lax.rem(self.chip + 1 + k, self.n_chip)

    def chip_device(self, k):
        return {"seg": self.chip_slot(k) * 2 + self.core}

    def dp_slot(self, k):
        return lax.rem(self.dp + 1 + k, self.n_dp)

    def dp_device(self, k):
        return {"dp": self.dp_slot(k)}

    def dp_at(self, way):
        return {"dp": lax.rem(self.dp + way + self.n_dp, self.n_dp)}

    def sibling(self, k=0):
        return {"seg": self.seg + 1 - 2 * self.core}

    def partner(self, k=0):
        return {"pipe": 1 - self.pipe}

    def greet(self):
        return greet(
            [(self.n_chip - 1, self.chip_device), (self.n_dp - 1, self.dp_device), (1, self.sibling), (1, self.partner)]
        )


class Gather:
    def __init__(self, near, dst, sems):
        self.near, self.dst = near, dst
        self.sends, self.chip_recv, self.side_recv, self.far_recv, self.core_recv = sems

    def source(self, k):
        near = self.near
        return lax.rem(near.chip + 2 * near.n_chip - 1 - k, near.n_chip)

    def chip_copy(self, k):
        near = self.near
        block = self.dst.at[near.chip, near.core, near.dp]
        return remote(block, block, self.sends.at[0], self.chip_recv.at[k], near.chip_device(k))

    def side_copy(self, k, i):
        near = self.near
        block = self.dst.at[self.source(k), near.core, near.dp]
        return remote(block, block, self.sends.at[1], self.side_recv.at[k, i], near.dp_at(1 if i == 0 else -1))

    def far_copy(self, k):
        near = self.near
        way = 1 - 2 * (k - k // 2 * 2)
        block = self.dst.at[self.source(k), near.core, lax.rem(near.dp + near.n_dp - way, near.n_dp)]
        return remote(block, block, self.sends.at[2], self.far_recv.at[k], near.dp_at(way))

    def core_copy(self, c, k):
        block = self.dst.at[self.source(k), self.near.core]
        return remote(block, block, self.sends.at[3], self.core_recv.at[c], self.near.sibling())

    def turn(self, step):
        return lax.rem(step + self.near.n_chip - 1, self.near.n_chip)

    def start(self, src):
        near = self.near
        self.dst[near.chip, near.core, near.dp] = src[...]
        each(near.n_chip - 1, lambda k: self.chip_copy(k).start())
        for i in range(2):
            self.side_copy(near.n_chip - 1, i).start()

    def spread(self):
        def pass_on(k):
            self.chip_copy(k).wait_recv()
            for i in range(2):
                self.side_copy(k, i).start()

        each(self.near.n_chip - 1, pass_on)

        def further(k):
            odd = k - k // 2 * 2
            block = self.dst.at[0, 0, 0]
            remote(block, block, self.sends.at[1], self.side_recv.at[k, odd], self.near.dp_at(1)).wait_recv()
            self.far_copy(k).start()

        each(self.near.n_chip, lambda step: further(self.turn(step)))

    def over(self, use):
        def pass_on(c):
            turns = [self.turn(c * GROUP + i) for i in range(GROUP)]
            block = self.dst.at[0, 0, 0]
            for k in turns:
                odd = k - k // 2 * 2
                all_here(block, self.side_recv.at[k, 1 - odd], self.near)
                all_here(block, self.far_recv.at[k], self.near)
                self.core_copy(c, k).start()
            use([self.source(k) for k in turns], self.near.core)

        each(self.near.n_chip // GROUP, pass_on)

    def end(self, use):
        def take(c):
            all_here(self.dst.at[pl.ds(0, GROUP), self.near.core], self.core_recv.at[c], self.near)
            use([self.source(self.turn(c * GROUP + i)) for i in range(GROUP)], 1 - self.near.core)

        each(self.near.n_chip // GROUP, take)

    def sent(self):
        near, dst = self.near, self.dst
        regions = (
            dst.at[pl.ds(0, near.n_chip - 1), near.core, near.dp],
            dst.at[:, near.core, pl.ds(0, 2)],
            dst.at[:, near.core, near.dp],
            dst.at[:, near.core],
        )
        for i, region in enumerate(regions):
            all_sent(region, self.sends.at[i], near)


def gather_sems(n_chip, n_dp):
    assert n_dp == 4
    dma = pltpu.SemaphoreType.DMA
    return (dma((4,)), dma((n_chip - 1,)), dma((n_chip, 2)), dma((n_chip,)), dma((n_chip // GROUP,)))


def all_sent(region, sem, near):
    remote(region, region, sem, sem, near.sibling()).wait_send()


def all_here(region, sem, near):
    remote(region, region, sem, sem, near.sibling()).wait_recv()


class LateGather:
    def __init__(self, near, dst, sems):
        self.near, self.dst, self.sems = near, dst, sems

    def run(self, src):
        near, dst, sems = self.near, self.dst, self.sems
        dst[near.chip, near.core, near.dp] = src[...]
        block = dst.at[near.chip, near.core, near.dp]
        chips = dst.at[pl.ds(0, near.n_chip - 1), near.core, near.dp]
        column = dst.at[:, near.core, near.dp]
        columns = dst.at[:, near.core, pl.ds(0, near.n_dp - 1)]
        side = dst.at[:, near.core]
        each(near.n_chip - 1, lambda k: remote(block, block, sems.at[0], sems.at[1], near.chip_device(k)).start())
        all_here(chips, sems.at[1], near)
        each(near.n_dp - 1, lambda k: remote(column, column, sems.at[2], sems.at[3], near.dp_device(k)).start())
        all_here(columns, sems.at[3], near)
        last = remote(side, side, sems.at[4], sems.at[5], near.sibling())
        last.start()
        last.wait()
        all_sent(chips, sems.at[0], near)
        all_sent(columns, sems.at[2], near)


def beside(tail):
    half = tail.shape[0] // 2
    return tail[:half] + pltpu.roll(tail[half:], LANES // 2, 1)


def below(value):
    first = iota(1, (1, LANES)) < LANES // 2
    top = jnp.where(first, value, 0.0)
    low = jnp.where(first, pltpu.roll(value, LANES // 2, 1), 0.0)
    return jnp.concatenate([top, low], axis=0)


def packed(value):
    tail = beside(value[:, 2 * LANES :])
    return jnp.concatenate([value[:, :LANES], value[:, LANES : 2 * LANES], tail], axis=0)


def weight_tiles(ref, chip, core, piece):
    block = ref[chip, core]
    tail = block[:, 2 * piece :]
    return (
        block[:, :piece].reshape(-1, LANES),
        block[:, piece : 2 * piece].reshape(-1, LANES),
        jnp.concatenate([tail, tail], axis=1).reshape(-1, LANES),
    )


def in_top(piece):
    lane = iota(1, (1, LANES))
    return lane - lane // piece * piece < piece // 2


def back_projected(dproj_ref, dt_low, ref, chip, core, piece):
    w_b, w_c, w_t = weight_tiles(ref, chip, core, piece)
    plain = dot(dproj_ref[1], w_b, NT) + dot(dproj_ref[0], w_c, NT)
    top = dot(dproj_ref[2], w_t, NT)
    low = dot(dt_low, w_t, NT)
    return plain + jnp.where(in_top(piece), top, low)


def lanes_turned(value):
    return pltpu.roll(value.astype(F32), LANES // 2, 1).astype(BF16)


def pair_columns(ref, j):
    turned = pltpu.roll(ref[...], lax.rem(LANES - 2 * j, LANES), 1)
    shape = (turned.shape[0], LANES)
    return jnp.broadcast_to(turned[:, 0:1], shape), jnp.broadcast_to(turned[:, 1:2], shape)


def by_half(first, second):
    return jnp.where(iota(1, (1, LANES)) < LANES // 2, first, second)


def heads_of(value, j):
    select = (iota(1) == 2 * j + (iota(0) >= LANES // 2).astype(jnp.int32)).astype(BF16)
    high, low = split_two(value)
    return dot(high, select) + dot(low, select)


def layer_kernel(n_chip, n_dp, *refs):
    (
        shard_ref, x_hbm, mixed_hbm, gate_hbm, out_grad_hbm, s0_hbm, rate_ref, bias_ref, skip_ref, doc_ref,
        input_out, mixed_out, gate_out, weight_out,
        x_ref, xs_ref, gate_ref, g_ref, s0_ref, shard, own_ref, one_shard, one_ref, later,
        s0t_ref, xt_ref, x_stage, group_ref, act_ref, weights, projected, bf_ref, cf_ref,
        log_ref, logt_ref, dt_ref, dtt_ref, sig_ref, rho_ref, mask_ref, first_ref, kept_ref, small,
        msg, both, total, got, back, exits, other, adj_ref, base, dproj_ref, passes, chip_passes,
        input_grad_ref, mixed_grad_ref, gate_grad_ref,
        acc_scores, acc_b, acc_c, acc_y, acc_x, acc_s, acc_a, grads, part_c, part_o, whole, arrived_c, arrived_o, spare, sems,
    ) = refs
    (
        in_sems, out_sems, own_set, one_set, shard_sems, later_sems, pass_sems, core_sems, core_recv,
        send_sems, recv, back_recv, other_recv, xt_sems, xg_sems, dp_recv, grad_sems, grad_recv, sum_sems,
    ) = sems
    rows, width = x_ref.shape
    state = bf_ref.shape[1]
    heads = rate_ref.shape[1]
    cols_w = shard_ref.shape[1]
    piece = shard_ref.shape[0]
    proj = projected.shape[1]
    half = n_chip

    near = Around(n_chip, n_dp)
    pipe, chip, core, dp = near.pipe, near.chip, near.core, near.dp
    all_met = near.greet()
    loads = [
        pltpu.make_async_copy(src, dst, in_sems.at[i])
        for i, (src, dst) in enumerate(
            ((gate_hbm, gate_ref), (s0_hbm, s0_ref), (x_hbm, x_ref), (out_grad_hbm, g_ref), (mixed_hbm, xs_ref))
        )
    ]
    for load in loads:
        load.start()
    spare[...] = jnp.zeros_like(spare)
    spare[:, :cols_w] = shard_ref[...].astype(F32)
    shard[...] = packed(spare[...]).astype(BF16)

    all_met()
    shard_copy = remote(shard, one_shard, shard_sems.at[0], shard_sems.at[1], near.partner())

    def later_copy(i):
        return remote(
            dproj_ref.at[i], later.at[i], later_sems.at[0, i], later_sems.at[1, i], near.partner()
        )


    gather = Gather(near, own_ref, own_set)
    gather.start(shard)

    @pl.when(pipe == 1)
    def _():
        shard_copy.start()

    for ref in (acc_scores, acc_b, acc_c, acc_y, acc_x, acc_s, acc_a, small, projected):
        ref[...] = jnp.zeros_like(ref)
    small[0:1, :heads] = rate_ref[...]
    small[8:9, :heads] = bias_ref[...]
    small[16:17, :heads] = skip_ref[...]
    begin = near.seg * rows
    count_t = jnp.zeros((rows, rows), jnp.int32)
    count_s = jnp.zeros((rows, rows), jnp.int32)
    count_last = jnp.zeros((rows, rows), jnp.int32)
    start = jnp.int32(0)
    for k in range(doc_ref.shape[1] - 1):
        start = start + doc_ref[0, k]
        offset = jnp.broadcast_to(start - begin, (rows, rows))
        inside = offset >= 0
        count_t += (inside & (iota(0) >= offset)).astype(jnp.int32)
        count_s += (inside & (iota(1) >= offset)).astype(jnp.int32)
        count_last += (inside & (offset <= rows - 1)).astype(jnp.int32)
    allowed = (iota(0) >= iota(1)) & (count_t == count_s)
    mask_ref[...] = jnp.where(allowed, 0.0, NEG)
    first_ref[...] = jnp.where(count_t == 0, 0.0, NEG)
    kept_ref[...] = jnp.where(count_t == count_last, 0.0, NEG)

    def activate(j):
        gate = gate_ref[:, tile_at(j)].astype(F32)
        act_ref[j] = gate * jax.nn.sigmoid(gate)

    def turn_state(j):
        s0t_ref[j] = s0_ref[tile_at(j), :].T.astype(BF16)

    def turn_x(k):
        for c in range(2):
            xt_ref[k, c] = x_ref[:, tile_at(2 * k + c)].T

    loads[0].wait()
    each(2 * half, activate, UNROLL)
    gather.spread()
    loads[1].wait()
    each(2 * half, turn_state, UNROLL)
    loads[2].wait()
    each(n_chip, turn_x, 2)

    def project(chips, c):
        top = in_top(piece)
        x_tiles = [x_ref[:, tile_at(2 * k + c)] for k in chips]
        zero = jnp.zeros_like(x_tiles[0])
        w_b, w_c, w_t = [
            jnp.concatenate(column, axis=0)
            for column in zip(*[weight_tiles(own_ref, k, c, piece) for k in chips])
        ]

        def lined(tiles):
            return jnp.concatenate(tiles, axis=1)

        x_all = lined(x_tiles)
        projected[:, :LANES] += dot(x_all, w_b)
        projected[:, LANES : 2 * LANES] += dot(x_all, w_c)
        projected[:, 2 * LANES : 3 * LANES] += dot(lined([jnp.where(top, x, zero) for x in x_tiles]), w_t)
        projected[:, 3 * LANES :] += dot(lined([jnp.where(top, zero, x) for x in x_tiles]), w_t)

    gather.over(project)
    gather.end(project)
    xt_copy = remote(xt_ref.at[:, 1 - core], x_stage, xt_sems.at[0], xt_sems.at[1], near.sibling())
    xt_copy.start()
    bf_ref[...] = projected[:, :state]
    cf_ref[...] = projected[:, state : 2 * state]
    raw = projected[:, 2 * LANES : 3 * LANES] + pltpu.roll(projected[:, 3 * LANES :], LANES // 2, 1)
    raw = jnp.where(iota(1) < heads, raw, 0.0) + small[8:9, :]
    soft = jnp.maximum(raw, 0.0) + jnp.log1p(jnp.exp(-jnp.abs(raw)))
    sig = 1.0 / (1.0 + jnp.exp(-jnp.abs(raw)))
    sig = jnp.where(raw >= 0, sig, 1.0 - sig)
    tiny = raw < -15.0
    exp_raw = jnp.exp(jnp.minimum(raw, 0.0))
    sig = jnp.where(tiny, exp_raw, sig)
    soft = jnp.where(tiny, exp_raw, soft)
    sig_ref[...] = sig
    rho_ref[...] = jnp.where(tiny, 1.0, sig / jnp.where(tiny, 1.0, soft))
    lower = (iota(0) >= iota(1)).astype(F32)
    log = dot(lower, -soft * small[0:1, :], precision=HIGH)
    log_ref[...] = log
    logt_ref[...] = log.T
    dt_ref[...] = soft
    dtt_ref[...] = soft.T
    first = iota(1, (1, LANES)) < LANES // 2

    passes[core] = jnp.broadcast_to(jnp.exp(log[rows - 1 :] + first_ref[rows - 1 :, :]), (8, LANES))
    pass_copy = remote(passes.at[core], passes.at[core], pass_sems.at[0], pass_sems.at[1], near.sibling())
    pass_copy.start()

    def pass_row(value, j):
        turned = pltpu.roll(value, lax.rem(LANES - 2 * j, LANES), 1)
        return by_half(turned[0:1, 0:1], turned[0:1, 1:2])

    loads[3].wait()

    def chip_pass_copy(k):
        block = chip_passes.at[chip]
        return remote(block, block, pass_sems.at[2], pass_sems.at[3], near.chip_device(k))

    def spread_passes():
        pass_copy.wait()
        chip_passes[chip] = passes[0] * passes[1]
        each(n_chip - 1, lambda k: chip_pass_copy(k).start())

    @pl.when(pipe == 0)
    def _():
        spread_passes()
        shard_copy.wait_recv()
        LateGather(near, one_ref, one_set).run(one_shard)
        later_copy(0).wait_recv()

        def first_part(k):
            for c in range(2):
                j = 2 * k + c
                w_c = one_ref[k, c, :, piece : 2 * piece].reshape(-1, LANES)
                base[j] = g_ref[:, tile_at(j)].astype(F32) + dot(later[0], w_c, NT)

        each(n_chip, first_part, 2)
        later_copy(1).wait_recv()
        later_copy(2).wait_recv()
        dt_low = lanes_turned(later[2])

        def recompute(k):
            for c in range(2):
                j = 2 * k + c
                w_b, _, w_t = weight_tiles(one_ref, k, c, piece)
                sent = base[j] + dot(later[1], w_b, NT)
                sent += jnp.where(in_top(piece), dot(later[2], w_t, NT), dot(dt_low, w_t, NT))
                g_ref[:, tile_at(j)] = sent.astype(BF16)

        each(n_chip, recompute, 2)

    ct = cf_ref[...].T.astype(BF16)

    def own(j):
        log0, log1 = pair_columns(log_ref, j)
        entry = jnp.exp(jnp.where(first, log0, log1) + first_ref[...])
        grad = (g_ref[:, tile_at(j)].astype(F32) * act_ref[j] * entry).astype(BF16)
        msg[j] = dot(ct, grad).astype(BF16)

    def swap_copy(c, slot):
        return remote(
            msg.at[(1 - core) * half + slot], both.at[core, slot],
            core_sems.at[0], core_recv.at[c], near.sibling(),
        )

    def combine(j):
        both[core, j] = msg[core * half + j]
        pass0 = pass_row(passes[0], core * half + j)
        total[j] = (both[0, j].astype(F32) + pass0 * both[1, j].astype(F32)).astype(BF16)

    def send_copy(k):
        return remote(
            total.at[near.chip_slot(k)], got.at[chip], send_sems.at[0], recv.at[chip], near.chip_device(k)
        )

    group = GROUP
    couple = 2

    def couple_slots(c):
        return [near.chip_slot(c * couple + i) for i in range(couple)]

    def own_theirs(c):
        slots = couple_slots(c)
        for slot in slots:
            own((1 - core) * half + slot)
        for slot in slots:
            swap_copy(c, slot).start()

    def own_mine(c, send_count):
        slots = couple_slots(c)
        for slot in slots:
            own(core * half + slot)
        all_here(both.at[core, pl.ds(0, couple)], core_recv.at[c], near)
        for slot in slots:
            combine(slot)
        for i in range(send_count):
            send_copy(c * couple + i).start()

    def own_step(c):
        own_theirs(c + 1)
        own_mine(c, couple)

    own_theirs(0)

    @pl.when(pipe == 1)
    def _():
        spread_passes()

    each(n_chip // couple - 1, own_step)
    own_mine(n_chip // couple - 1, couple - 1)
    got[chip] = total[chip]

    xt_copy.wait()

    def x_copy(k, src, from_core):
        cut = pl.ds(pl.multiple_of(near.dp_slot(k) * piece, piece), piece)
        return remote(
            src.at[:, cut], group_ref.at[dp, from_core],
            xg_sems.at[0], xg_sems.at[1], near.dp_device(k),
        )

    def x_start(k):
        x_copy(k, xt_ref.at[:, core], core).start()
        x_copy(k, x_stage, 1 - core).start()

    each(n_dp - 1, x_start)
    cut = pl.ds(pl.multiple_of(dp * piece, piece), piece)
    group_ref[dp, core] = xt_ref[:, core, cut]
    group_ref[dp, 1 - core] = x_stage[:, cut]

    loads[4].wait()
    scores = dot(cf_ref[...], bf_ref[...], NT, precision=HIGH)
    b_low = bf_ref[...].astype(BF16)
    c_low = cf_ref[...].astype(BF16)

    def before(j):
        cols = tile_at(j)
        x_pair = xs_ref[:, cols]
        x_f = x_pair.astype(F32)
        gate = gate_ref[:, cols].astype(F32)
        sig = jax.nn.sigmoid(gate)
        g = g_ref[:, cols].astype(F32)
        grad_y = g * act_ref[j]
        grad_low = grad_y.astype(BF16)
        zero = jnp.zeros_like(x_pair)
        x0, x1 = jnp.where(first, x_pair, zero), jnp.where(first, zero, x_pair)
        y0, y1 = jnp.where(first, grad_low, zero), jnp.where(first, zero, grad_low)
        log0, log1 = pair_columns(log_ref, j)
        dt0, dt1 = pair_columns(dt_ref, j)
        mask = mask_ref[...]
        decay0 = jnp.exp(log0 - logt_ref[pl.ds(2 * j, 1), :] + mask) * dtt_ref[pl.ds(2 * j, 1), :]
        decay1 = jnp.exp(log1 - logt_ref[pl.ds(2 * j + 1, 1), :] + mask) * dtt_ref[pl.ds(2 * j + 1, 1), :]
        mix0 = (decay0 * scores).astype(BF16)
        mix1 = (decay1 * scores).astype(BF16)
        acc_scores[...] += dot(y0, x_pair, NT) * decay0 + dot(y1, x_pair, NT) * decay1
        log_pair = jnp.where(first, log0, log1)
        entry = jnp.exp(log_pair + first_ref[...])
        s0t = s0t_ref[j]
        y = dot(mix0, x0) + dot(mix1, x1) + entry * dot(c_low, s0t)
        acc_c[...] += dot((entry * grad_y).astype(BF16), s0t, NT)
        inner = dot(mix0, y0, TN) + dot(mix1, y1, TN)
        weights[j] = jnp.exp(log_pair[-1:, :] - log_pair + kept_ref[...]) * jnp.where(first, dt0, dt1)
        x_inner = x_f * inner
        acc_y[...] += heads_of(grad_low.astype(F32) * y - x_inner, j)
        acc_x[...] += heads_of(x_inner, j)
        skip = pltpu.roll(small[16:24, :], lax.rem(LANES - 2 * j, LANES), 1)
        skip = by_half(skip[0:1, 0:1], skip[0:1, 1:2])
        slope = sig * (1.0 + gate * (1.0 - sig))
        gate_grad_ref[:, cols] = (g * (y + skip * x_f) * slope).astype(BF16)
        base[j] = inner + skip * grad_y

    early = 8
    each(early, before, UNROLL)

    all_here(chip_passes.at[pl.ds(0, n_chip - 1)], pass_sems.at[3], near)

    def back_copy(k):
        return remote(
            back.at[k], exits.at[chip], send_sems.at[1], back_recv.at[chip], {"seg": k * 2 + core}
        )

    def scan(step, carry):
        k = n_chip - 1 - step

        @pl.when(k != chip)
        def _():
            all_here(got.at[k], recv.at[k], near)

        back[k] = carry.astype(BF16)

        @pl.when(k != chip)
        def _():
            back_copy(k).start()

        return got[k].astype(F32) + pass_row(chip_passes[k], core * half + chip) * carry

    lax.fori_loop(0, n_chip, scan, jnp.zeros((state, LANES), F32))
    exits[chip] = back[chip]
    each(2 * half - early, lambda j: before(early + j), UNROLL)
    c_grad = acc_c[...] + dot(acc_scores[...], bf_ref[...], precision=HIGH)
    dproj_ref[0] = c_grad.astype(BF16)
    acc_b[...] += dot(acc_scores[...].T, cf_ref[...], precision=HIGH)

    @pl.when(pipe == 1)
    def _():
        later_copy(0).start()

    def dp_copy(i, k):
        return remote(
            dproj_ref.at[i], grads.at[core, dp, i],
            grad_sems.at[0, i], dp_recv.at[i, k], near.dp_device(k),
        )

    def grad_swap(i, slot):
        block = grads.at[core, slot, i]
        return remote(block, block, grad_sems.at[1, i], grad_recv.at[i], near.sibling())

    def share(i):
        each(n_dp - 1, lambda k: dp_copy(i, k).start())
        grads[core, dp, i] = dproj_ref[i]
        grad_swap(i, dp).start()

    share(0)
    gate_copy = pltpu.make_async_copy(gate_grad_ref, gate_out, out_sems.at[0])
    gate_copy.start()

    def other_copy(c, j):
        return remote(
            other.at[j], adj_ref.at[core * half + j], core_sems.at[1], other_recv.at[c], near.sibling()
        )

    def finish(c, j):
        @pl.when(j != chip)
        def _():
            all_here(exits.at[j], back_recv.at[j], near)

        after = exits[j].astype(F32)
        earlier = both[1, j].astype(F32) + pass_row(passes[1], core * half + j) * after
        is_later = core == 1
        adj_ref[core * half + j] = jnp.where(is_later, after, earlier).astype(BF16)
        other[j] = jnp.where(is_later, earlier, after).astype(BF16)
        other_copy(c, j).start()

    def near_first(i):
        x_off = i - i // 2 * 2
        m = i // 2
        odd = m - m // 2 * 2
        z_off = odd * ((m + 1) // 2) - (1 - odd) * (m // 2)
        ring = n_chip // 2
        my_x = chip // ring
        z = lax.rem(chip - my_x * ring + z_off + ring, ring)
        return lax.rem(my_x + x_off, 2) * ring + z

    def after_scan(pairs):
        def lined(tiles):
            return jnp.concatenate(tiles, axis=1)

        adj = lined([adj_ref[j] for j in pairs])
        weight = lined([weights[j] for j in pairs])
        x_f = lined([xs_ref[:, tile_at(j)] for j in pairs]).astype(F32)
        outer = weight * dot(b_low, adj)
        acc_b[...] += dot((x_f * weight).astype(BF16), adj, NT)
        lane, row = iota(1), (iota(0) >= LANES // 2).astype(jnp.int32)
        select = jnp.concatenate([(lane == 2 * j + row).astype(BF16) for j in pairs], axis=0)
        high, low = split_two(x_f * outer)
        acc_s[...] += dot(high, select) + dot(low, select)
        last = lined([pass_row(passes[core], j) for j in pairs])
        s0t = lined([s0t_ref[j] for j in pairs])
        passed = last * jnp.sum(adj.astype(F32) * s0t.astype(F32), axis=0, keepdims=True)
        high, low = split_two(jnp.broadcast_to(passed, (8, passed.shape[1])))
        acc_a[...] += dot(high, select) + dot(low, select)
        for i, j in enumerate(pairs):
            mixed_grad_ref[:, tile_at(j)] = (base[j] + outer[:, i * LANES : (i + 1) * LANES]).astype(BF16)

    def mine_group(c):
        slots = [near_first(c * group + i) for i in range(group)]
        for slot in slots:
            finish(c, slot)
        after_scan([core * half + slot for slot in slots])

    def other_group(c):
        slots = [near_first(c * group + i) for i in range(group)]
        all_here(other.at[pl.ds(0, group)], other_recv.at[c], near)
        after_scan([(1 - core) * half + slot for slot in slots])

    each(n_chip // group, mine_group)
    each(n_chip // group, other_group)

    dproj_ref[1] = acc_b[...].astype(BF16)

    @pl.when(pipe == 1)
    def _():
        later_copy(1).start()

    share(1)
    u = acc_x[...] + acc_s[...]
    last = jnp.sum(acc_s[...], axis=0, keepdims=True) + acc_a[0:1, :]
    upper = (iota(0) <= iota(1)).astype(F32)
    log_grad = dot(upper, acc_y[...] - acc_s[...], precision=HIGH) + last
    raw_grad = u * rho_ref[...] - small[0:1, :] * log_grad * sig_ref[...]
    dproj_ref[2] = raw_grad.astype(BF16)

    @pl.when(pipe == 1)
    def _():
        later_copy(2).start()

    share(2)

    mixed_copy = pltpu.make_async_copy(mixed_grad_ref, mixed_out, out_sems.at[1])
    mixed_copy.start()
    all_here(group_ref.at[pl.ds(0, n_dp - 1)], xg_sems.at[1], near)

    def gathered(i):
        for k in range(n_dp - 1):
            dp_copy(i, k).wait_recv()
            grad_swap(i, lax.rem(dp + 2 * n_dp - 1 - k, n_dp)).start()

    def summed_over(c, tile):
        x = jnp.concatenate([group_ref[k, c].reshape(-1, rows) for k in range(n_dp)], axis=1)
        return dot(x, jnp.concatenate([grads[c, k, tile] for k in range(n_dp)], axis=0))

    def whole_tile(i):
        whole[i] = summed_over(core, i)
        all_here(grads.at[1 - core, :, i], grad_recv.at[i], near)
        whole[i] += summed_over(1 - core, i)

    def rows_of(slot):
        return pl.ds(pl.multiple_of(slot * piece, piece), piece)

    def c_rows(slot):
        return whole[0, rows_of(slot)]

    def other_rows(slot):
        return jnp.concatenate([whole[1, rows_of(slot)], beside(whole[2, rows_of(slot)])], axis=0)

    def sum_copy(i, k, part, arrived):
        return remote(
            part.at[near.chip_slot(k)], arrived.at[k], sum_sems.at[0, i], sum_sems.at[1, i],
            near.chip_device(k),
        )

    def ship(i, rows_at, part, arrived):
        def one(k):
            slot = near.chip_slot(k)
            part[slot] = rows_at(slot).astype(BF16)
            sum_copy(i, k, part, arrived).start()

        each(n_chip - 1, one)

    gathered(0)
    whole_tile(0)
    ship(0, c_rows, part_c, arrived_c)
    dt_low = lanes_turned(dproj_ref[2])

    def give(k):
        for c in range(2):
            cols = tile_at(2 * k + c)
            sent = back_projected(dproj_ref, dt_low, own_ref, k, c, piece)
            input_grad_ref[:, cols] = (g_ref[:, cols].astype(F32) + sent).astype(BF16)

    each(n_chip, give, 2)
    input_copy = pltpu.make_async_copy(input_grad_ref, input_out, out_sems.at[2])
    input_copy.start()

    gathered(1)
    gathered(2)
    whole_tile(1)
    whole_tile(2)
    ship(1, other_rows, part_o, arrived_o)

    @pl.when(pipe == 1)
    def _():
        shard_copy.wait_send()
        for i in range(3):
            later_copy(i).wait_send()

    gather.sent()
    first_chips = pl.ds(0, n_chip - 1)
    all_sent(chip_passes.at[first_chips], pass_sems.at[2], near)
    all_sent(both.at[core], core_sems.at[0], near)
    all_sent(total.at[first_chips], send_sems.at[0], near)
    all_sent(back.at[first_chips], send_sems.at[1], near)
    all_sent(other, core_sems.at[1], near)
    all_sent(group_ref.at[pl.ds(0, n_dp - 1)], xg_sems.at[0], near)
    for i in range(3):
        all_sent(grads.at[core, pl.ds(0, n_dp - 1), i], grad_sems.at[0, i], near)
        all_sent(grads.at[core, :, i], grad_sems.at[1, i], near)

    def collected(i, rows_at, arrived):
        all_here(arrived, sum_sems.at[1, i], near)
        total_rows = rows_at(chip)
        for k in range(n_chip - 1):
            total_rows += arrived[k].astype(F32)
        return total_rows

    weight_out[:, LANES : 2 * LANES] = collected(0, c_rows, arrived_c)
    others = collected(1, other_rows, arrived_o)
    weight_out[:, :LANES] = others[:piece]
    weight_out[:, 2 * LANES :] = below(others[piece:])[:, : cols_w - 2 * LANES]
    all_sent(arrived_c, sum_sems.at[0, 0], near)
    all_sent(arrived_o, sum_sems.at[0, 1], near)
    gate_copy.wait()
    mixed_copy.wait()
    input_copy.wait()


def layer_grads(shard, x, mixed, gate, out_grad, s0, rate, bias, skip, docs, n_chip, n_dp):
    rows, width = x.shape
    pairs = width // LANES
    state = s0.shape[1]
    piece, cols = shard.shape
    proj = cols + -cols % LANES
    dma = pltpu.SemaphoreType.DMA
    line = jax.ShapeDtypeStruct((rows, width), BF16)
    whole_line = pltpu.VMEM((rows, width), BF16)
    square = pltpu.VMEM((rows, LANES), F32)
    packed_rows = 2 * piece + piece // 2
    full_w = pltpu.VMEM((n_chip, 2, n_dp, packed_rows, LANES), BF16)
    wide = pltpu.VMEM((pairs, rows, LANES), F32)
    tiles = pltpu.VMEM((proj // LANES, rows, LANES), BF16)
    plain = pltpu.VMEM((n_chip, state, LANES), BF16)
    anywhere = pl.BlockSpec(memory_space=pl.ANY)
    chips = dma((n_chip,))
    return pl.pallas_call(
        functools.partial(layer_kernel, n_chip, n_dp),
        out_shape=(line, line, line, jax.ShapeDtypeStruct((piece, cols), F32)),
        in_specs=[VMEM] + [anywhere] * 5 + [VMEM] * 3 + [SMEM],
        out_specs=(anywhere, anywhere, anywhere, VMEM),
        scratch_shapes=[
            whole_line, whole_line, whole_line, whole_line,
            pltpu.VMEM((width, state), F32),
            pltpu.VMEM((packed_rows, LANES), BF16),
            full_w,
            pltpu.VMEM((packed_rows, LANES), BF16),
            full_w,
            tiles,
            pltpu.VMEM((pairs, state, LANES), BF16),
            pltpu.VMEM((n_chip, 2, LANES, rows), BF16),
            pltpu.VMEM((n_chip, LANES, rows), BF16),
            pltpu.VMEM((n_dp, 2, n_chip, piece, rows), BF16),
            wide, wide,
            pltpu.VMEM((rows, proj + LANES), F32),
        ]
        + [square] * 11
        + [
            pltpu.VMEM((24, LANES), F32),
            pltpu.VMEM((pairs, state, LANES), BF16),
            pltpu.VMEM((2, n_chip, state, LANES), BF16),
            plain, plain, plain, plain, plain,
            pltpu.VMEM((pairs, state, LANES), BF16),
            wide,
            tiles,
            pltpu.VMEM((2, 8, LANES), F32),
            pltpu.VMEM((n_chip, 8, LANES), F32),
            whole_line, whole_line, whole_line,
        ]
        + [square] * 6
        + [
            pltpu.VMEM((8, LANES), F32),
            pltpu.VMEM((2, n_dp, proj // LANES, rows, LANES), BF16),
            pltpu.VMEM((n_chip, piece, LANES), BF16),
            pltpu.VMEM((n_chip, packed_rows - piece, LANES), BF16),
            pltpu.VMEM((proj // LANES, n_chip * piece, LANES), F32),
            pltpu.VMEM((n_chip - 1, piece, LANES), BF16),
            pltpu.VMEM((n_chip - 1, packed_rows - piece, LANES), BF16),
            pltpu.VMEM((piece, proj), F32),
            (
                dma((5,)), dma((3,)), gather_sems(n_chip, n_dp), dma((6,)), dma((2,)), dma((2, 3)), dma((4,)),
                dma((2,)), dma((n_chip // 2,)), dma((2,)), chips, chips, dma((n_chip // GROUP,)), dma((2,)),
                dma((2,)), dma((3, n_dp - 1)), dma((2, 3)), dma((3,)), dma((2, 2)),
            ),
        ],
        compiler_params=pltpu.CompilerParams(
            collective_id=1, has_side_effects=True, vmem_limit_bytes=VMEM_BYTES
        ),
    )(shard, x, mixed, gate, out_grad, s0, rate, bias, skip, docs)


def deliver_kernel(cuts, *refs):
    count = len(cuts)
    held, sems = refs[2 * count : 3 * count], refs[-1]
    steps = []
    for i, cut in enumerate(cuts):
        size = held[i].shape[0] // cut
        for k in range(cut):
            rows = pl.ds(k * size, size)
            at = len(steps)
            load = pltpu.make_async_copy(refs[i].at[rows], held[i].at[rows], sems.at[0, at])
            store = pltpu.make_async_copy(held[i].at[rows], refs[count + i].at[rows], sems.at[1, at])
            steps.append((load, store))
    for load, _ in steps:
        load.start()
    for load, store in steps:
        load.wait()
        store.start()
    for _, store in steps:
        store.wait()


def deliver(values):
    anywhere = pl.BlockSpec(memory_space=pl.ANY)
    cuts = [2 if value.dtype == BF16 else 1 for value in values]
    return pl.pallas_call(
        functools.partial(deliver_kernel, cuts),
        out_shape=tuple(jax.ShapeDtypeStruct(value.shape, value.dtype) for value in values),
        in_specs=[anywhere] * len(values),
        out_specs=(anywhere,) * len(values),
        scratch_shapes=[pltpu.VMEM(value.shape, value.dtype) for value in values]
        + [pltpu.SemaphoreType.DMA((2, sum(cuts)))],
    )(*values)


def local(
    inputs, mixed, gate_in, entry_states, out_grad, doc_lengths, proj_weight, decay_rate, dt_bias, skip_gain
):
    n_chip = lax.axis_size("seg") // 2
    n_dp = lax.axis_size("dp")
    width = inputs.shape[-1]
    s0 = entry_states.reshape(width, entry_states.shape[-1])
    outs = layer_grads(
        proj_weight[0], inputs[0, 0], mixed[0, 0], gate_in[0, 0], out_grad[0], s0,
        decay_rate, dt_bias, skip_gain, doc_lengths, n_chip, n_dp,
    )
    input_grad, mixed_grad, gate_grad, weight_grad = deliver(outs)
    return (
        input_grad[None, None],
        mixed_grad[None, None],
        gate_grad[None, None],
        weight_grad[None],
    )


def solution(mesh):
    in_specs = (
        P("pipe", "dp", "seg", None),
        P("pipe", "dp", "seg", None),
        P("pipe", "dp", "seg", None),
        P("pipe", "dp", "seg", None, None, None),
        P("dp", "seg", None),
        P("dp", None),
        P("pipe", ("seg", "dp"), None),
        P("pipe", None),
        P("pipe", None),
        P("pipe", None),
    )
    out_specs = (
        P("pipe", "dp", "seg", None),
        P("pipe", "dp", "seg", None),
        P("pipe", "dp", "seg", None),
        P("pipe", ("seg", "dp"), None),
    )
    return jax.shard_map(local, mesh=mesh, in_specs=in_specs, out_specs=out_specs, check_vma=False)
```
